32 devices in a mesh: dp: 16 (over z, y, x), seq: 2 (over core).
Axes of the slice: x: 2, y: 2, z: 4, core: 2. Of those that a mesh axis runs over, the one named last changes fastest.
Arguments:
- tokens: bfloat16 [11200, 768], P(('dp', 'seq')), may hold values from -6 to 6
- crop_len: int32 [16, 10], P('dp'), may hold values from 19 to 197, as said below
- qkv_weight: bfloat16 [2, 768, 2304], replicated, may hold values from -0.3125 to 0.3125
- query_bias: float32 [2, 768], replicated, may hold values from -3 to 3
- value_bias: float32 [2, 768], replicated, may hold values from -3 to 3
- out_weight: bfloat16 [2, 768, 768], replicated, may hold values from -0.625 to 0.625
- out_bias: float32 [2, 768], replicated, may hold values from -3 to 3
- first_gain: float32 [2, 768], replicated, may hold values from 0.5 to 1.5
- first_shift: float32 [2, 768], replicated, may hold values from -3 to 3
- second_gain: float32 [2, 768], replicated, may hold values from 0.5 to 1.5
- second_shift: float32 [2, 768], replicated, may hold values from -3 to 3
- up_weight: bfloat16 [2, 768, 3072], replicated, may hold values from -0.21875 to 0.21875
- up_bias: float32 [2, 3072], replicated, may hold values from -3 to 3
- down_weight: bfloat16 [2, 3072, 768], replicated, may hold values from -0.109375 to 0.109375
- down_bias: float32 [2, 768], replicated, may hold values from -3 to 3
- cotangent: bfloat16 [11200, 768], P(('dp', 'seq')), may hold values from -6 to 6
Outputs:
- result: bfloat16 [11200, 768], P(('dp', 'seq'))
- grad_tokens: bfloat16 [11200, 768], P(('dp', 'seq'))
- grad_qkv_weight: float32 [2, 768, 2304], P(None, 'dp', 'seq')
- grad_query_bias: float32 [2, 768], P(None, 'dp')
- grad_value_bias: float32 [2, 768], P(None, 'dp')
- grad_out_weight: float32 [2, 768, 768], P(None, 'dp', 'seq')
- grad_out_bias: float32 [2, 768], P(None, 'dp')
- grad_first_gain: float32 [2, 768], P(None, 'dp')
- grad_first_shift: float32 [2, 768], P(None, 'dp')
- grad_second_gain: float32 [2, 768], P(None, 'dp')
- grad_second_shift: float32 [2, 768], P(None, 'dp')
- grad_up_weight: float32 [2, 768, 3072], P(None, 'dp', 'seq')
- grad_up_bias: float32 [2, 3072], P(None, 'dp')
- grad_down_weight: float32 [2, 3072, 768], P(None, 'dp', 'seq')
- grad_down_bias: float32 [2, 768], P(None, 'dp')
The draws below stay inside these ranges and needn't reach their ends.
Inputs may be any that keep to these rules, and one draw needn't show every extreme that they name: `crop_len`: the first 2 entries of a row are global crops of 99 to 197 live tokens, the other 8 local crops of 19 to 37. The global crop that holds row 350 of its group has 197 live tokens.
All inputs are finite; a program needn't handle non-finite values.
Results may differ from the reference program's by a relative error of at most 0.019.
The reference program's roundings to bfloat16 on the way count: a program that leaves them out, or rounds other values in their place, can miss the bound.
Values may be sent and summed in bfloat16 or wider, within the bound.
No kernel may reach another device: no remote copies, remote signals or barrier semaphores. Data moves between devices by JAX's collectives and lax.ppermute only.
A program may use at most 256 MiB of HBM per device.

```python
import jax
import jax.numpy as jnp
from jax import lax

D = 768
HEADS = 12
HD = 64
FF = 3072
LAYERS = 2
LG = 197
LL = 37
GPAD = 198
LPAD = 38
IMG_DEV = 1
GROUPS = 16
GROUP_TOK = 700
TOKENS = 11200


def draw_crop_len(key, part):
    key = jax.random.fold_in(key, 7)
    wide_key, narrow_key = jax.random.split(key, 2)
    wide_count = 2 * IMG_DEV
    narrow_count = 8 * IMG_DEV
    wide_len = jax.random.randint(wide_key, (GROUPS, wide_count), (LG + 1) // 2, LG + 1)
    narrow_len = jax.random.randint(narrow_key, (GROUPS, narrow_count), (LL + 1) // 2, LL + 1)
    middle_crop = (GPAD + 4 * LPAD) * IMG_DEV // GPAD
    wide_len = jnp.where(jnp.arange(wide_count)[None, :] == middle_crop, LG, wide_len)
    narrow_full = jax.random.randint(jax.random.fold_in(key, 3), (GROUPS, 1), 0, narrow_count)
    narrow_len = jnp.where(jnp.arange(narrow_count)[None, :] == narrow_full, LL, narrow_len)
    return jnp.concatenate([wide_len, narrow_len], axis=1).astype(jnp.int32)


def raised(drawn, stream_key, source, target, blocks, factor):
    def block_of(dim):
        return (jnp.arange(drawn.shape[dim]) // (drawn.shape[dim] // blocks)).reshape((-1,) + (1,) * (drawn.ndim - 1 - dim))

    first = jax.random.permutation(stream_key, blocks)[block_of(target)]
    far = (block_of(target) + blocks // 2) % blocks
    return jnp.where((block_of(source) == first) | (block_of(source) == far), factor * drawn, drawn)


def block_scale(rng, extent, cuts, low, top_value):
    factor_of = 1.0
    for position, blocks in cuts:
        heights = jax.random.uniform(jax.random.fold_in(jax.random.fold_in(rng, 6), position), (blocks,), jnp.float32, low / len(cuts), top_value / len(cuts))
        factor_of = factor_of * jnp.repeat(jnp.exp(heights), extent[position] // blocks).reshape((-1,) + (1,) * (len(extent) - 1 - position))
    return factor_of


def noise(stream_key, dims, scale, limit, shards=(), dtype=jnp.bfloat16):
    loudness = block_scale(stream_key, dims, shards, -0.22, 0.18) if shards else 1.0
    entries = jax.random.normal(stream_key, dims, jnp.float32) * scale * loudness
    return jnp.minimum(jnp.maximum(entries, -limit), limit).astype(dtype)


def bell_draw_with(rng, dims, spread, limit, cuts, heavy, kind=jnp.bfloat16):
    entries = spread * jax.random.normal(rng, dims, jnp.float32)
    if cuts:
        entries = entries * block_scale(rng, dims, cuts, -0.22, 0.18)
    return jnp.clip(raised(entries, jax.random.fold_in(rng, 3), *heavy), -limit, limit).astype(kind)


def setup_inputs(seed: int = 0) -> dict:
    key_list = jax.random.split(jax.random.key(seed), 17)
    return {
        "tokens": bell_draw_with(key_list[0], (TOKENS, D), 1.0, 6.0, ((0, 32),), (0, 1, 32, 2.75)),
        "crop_len": draw_crop_len(jax.random.fold_in(key_list[16], 71), 0),
        "qkv_weight": noise(key_list[2], (LAYERS, D, 3 * D), (D // 2) ** -0.5, 0.3125),
        "query_bias": noise(key_list[3], (LAYERS, D), 0.5, 3.0, (), jnp.float32),
        "value_bias": noise(key_list[4], (LAYERS, D), 0.5, 3.0, (), jnp.float32),
        "out_weight": noise(key_list[5], (LAYERS, D, D), (D // 8) ** -0.5, 0.625),
        "out_bias": noise(key_list[6], (LAYERS, D), 0.5, 3.0, (), jnp.float32),
        "first_gain": jnp.clip(1.0 + 0.1 * jax.random.normal(key_list[7], (LAYERS, D), jnp.float32), 0.5, 1.5),
        "first_shift": noise(key_list[8], (LAYERS, D), 0.5, 3.0, (), jnp.float32),
        "second_gain": jnp.clip(1.0 + 0.1 * jax.random.normal(key_list[9], (LAYERS, D), jnp.float32), 0.5, 1.5),
        "second_shift": noise(key_list[10], (LAYERS, D), 0.5, 3.0, (), jnp.float32),
        "up_weight": noise(key_list[11], (LAYERS, D, FF), D ** -0.5, 0.21875),
        "up_bias": noise(key_list[12], (LAYERS, FF), 0.5, 3.0, (), jnp.float32),
        "down_weight": noise(key_list[13], (LAYERS, FF, D), FF ** -0.5, 0.109375),
        "down_bias": noise(key_list[14], (LAYERS, D), 0.5, 3.0, (), jnp.float32),
        "cotangent": bell_draw_with(key_list[15], (TOKENS, D), 1.0, 6.0, ((0, 32),), (0, 1, 32, 2.75)),
    }


EPS = 1e-06
MASKED = -1e+30
HIGHEST = lax.Precision.HIGHEST

@jax.custom_vjp
def low(v):
    return lax.optimization_barrier(v.astype(jnp.bfloat16)).astype(jnp.float32)

@jax.custom_vjp
def low_back(v):
    return v

def low_keep(v):
    return (low(v), None)

def low_pass(kept, grad):
    return (grad,)

def back_keep(v):
    return (v, None)

def back_low(kept, grad):
    return (low(grad),)
low.defvjp(low_keep, low_pass)
low_back.defvjp(back_keep, back_low)

def dense(left, right):
    return jnp.dot(left, right, precision=HIGHEST)

def layer_norm(hidden, norm_gain, norm_shift):
    row_mean = lax.optimization_barrier(jnp.mean(hidden, axis=-1, keepdims=True))
    centered = hidden - row_mean
    variance = lax.optimization_barrier(jnp.mean(centered * centered, axis=-1, keepdims=True))
    return centered * lax.rsqrt(variance + EPS) * norm_gain + norm_shift

def crop_attention(joint_crops, lengths):
    queries = joint_crops[:, :, :, 0]
    keys_in = joint_crops[:, :, :, 1]
    values = joint_crops[:, :, :, 2]
    scores = low_back(jnp.einsum('gcqhe,gckhe->gchqk', queries, keys_in, precision=HIGHEST) * HD ** (-0.5))
    positions = lax.broadcasted_iota(jnp.int32, scores.shape, 4)
    scores = jnp.where(positions < lengths[:, :, None, None, None], scores, MASKED)
    row_max = lax.optimization_barrier(jnp.max(scores, axis=-1, keepdims=True))
    exponent = jnp.exp(scores - row_max)
    weights = low(exponent / lax.optimization_barrier(jnp.sum(exponent, axis=-1, keepdims=True)))
    return jnp.einsum('gchqk,gckhe->gcqhe', weights, values, precision=HIGHEST)

def forward(hidden, lengths, params):
    groups = hidden.shape[0] // GROUP_TOK
    split_at = 2 * IMG_DEV * GPAD
    for layer_at in range(LAYERS):
        qkv_w, query_b, value_b, out_w, out_b, gain_one, shift_one, gain_two, shift_two, up_w, up_b, down_w, down_b = [member[layer_at] for member in params]
        normed_in = low(layer_norm(hidden, gain_one, shift_one))
        qkv_bias = jnp.concatenate([query_b, jnp.zeros_like(query_b), value_b])
        joint_rows = low(low_back(dense(normed_in, qkv_w) + qkv_bias))
        joint_rows = joint_rows.reshape(groups, GROUP_TOK, 3, HEADS, HD)
        wide_crops = joint_rows[:, :split_at].reshape(groups, 2 * IMG_DEV, GPAD, 3, HEADS, HD)
        narrow_crops = joint_rows[:, split_at:].reshape(groups, 8 * IMG_DEV, LPAD, 3, HEADS, HD)
        mixed_wide = crop_attention(wide_crops, lengths[:, :2 * IMG_DEV]).reshape(groups, split_at, D)
        mixed_narrow = crop_attention(narrow_crops, lengths[:, 2 * IMG_DEV:]).reshape(groups, GROUP_TOK - split_at, D)
        merged = low(low_back(jnp.concatenate([mixed_wide, mixed_narrow], axis=1).reshape(-1, D)))
        hidden = hidden + low_back(dense(merged, out_w) + out_b)
        normed_mid = low(layer_norm(hidden, gain_two, shift_two))
        up_values = low_back(dense(normed_mid, up_w) + up_b)
        active = low(jax.nn.gelu(up_values, approximate=False))
        hidden = hidden + low_back(dense(active, down_w) + down_b)
    return hidden

def reference(tokens, crop_len, qkv_weight, query_bias, value_bias, out_weight, out_bias, first_gain, first_shift, second_gain, second_shift, up_weight, up_bias, down_weight, down_bias, cotangent):
    params = tuple((member.astype(jnp.float32) for member in (qkv_weight, query_bias, value_bias, out_weight, out_bias, first_gain, first_shift, second_gain, second_shift, up_weight, up_bias, down_weight, down_bias)))

    def wrapped(hidden, weights):
        return forward(hidden, crop_len, weights)
    result, pullback = jax.vjp(wrapped, tokens.astype(jnp.float32), params)
    grad_tokens, gradients = pullback(cotangent.astype(jnp.float32))
    return (result.astype(jnp.bfloat16), grad_tokens.astype(jnp.bfloat16), gradients[0], gradients[1], gradients[2], gradients[3], gradients[4], gradients[5], gradients[6], gradients[7], gradients[8], gradients[9], gradients[10], gradients[11], gradients[12])
```

```python
from functools import partial

import jax
import jax.numpy as jnp
from jax import lax
from jax.sharding import PartitionSpec as P

HD = 64
GPAD = 198
LPAD = 38
IMG_DEV = 1


EPS = 1e-06
MASKED = -1e30
MATRIX_SLOTS = (0, 3, 9, 11)
VECTOR_SLOTS = (1, 2, 4, 5, 6, 7, 8, 10, 12)


def layer_norm(hidden, norm_gain, norm_shift):
    row_mean = jnp.mean(hidden, axis=-1, keepdims=True)
    centered = hidden - row_mean
    inverse = lax.rsqrt(jnp.mean(centered * centered, axis=-1, keepdims=True) + EPS)
    normed = centered * inverse
    return (normed * norm_gain + norm_shift, normed, inverse)


def norm_back(upstream, normed, inverse, norm_gain):
    scaled = upstream * norm_gain
    centered = scaled - jnp.mean(scaled, axis=-1, keepdims=True)
    centered = centered - normed * jnp.mean(scaled * normed, axis=-1, keepdims=True)
    return (centered * inverse, jnp.sum(upstream * normed, axis=0), jnp.sum(upstream, axis=0))


def crop_views(group_rows):
    split_at = 2 * IMG_DEV * GPAD
    wide_crops = group_rows[:split_at].reshape((2 * IMG_DEV, GPAD) + group_rows.shape[1:])
    narrow_crops = group_rows[split_at:].reshape((8 * IMG_DEV, LPAD) + group_rows.shape[1:])
    return (wide_crops, narrow_crops)


def join_views(wide_crops, narrow_crops):
    return jnp.concatenate(
        [
            wide_crops.reshape((-1,) + wide_crops.shape[2:]),
            narrow_crops.reshape((-1,) + narrow_crops.shape[2:]),
        ],
        axis=0,
    )


def crop_scores(queries, keys_in, lengths, scaling):
    scores = (
        jnp.einsum("cqhe,ckhe->chqk", queries, keys_in, preferred_element_type=jnp.float32)
        * scaling
    )
    positions = lax.broadcasted_iota(jnp.int32, scores.shape, 3)
    return jnp.where(positions < lengths[:, None, None, None], scores, MASKED)


def attend(queries, keys_in, values, lengths, scaling):
    scores = crop_scores(queries, keys_in, lengths, scaling)
    row_max = jnp.max(scores, axis=-1, keepdims=True)
    exponent = jnp.exp(scores - row_max)
    totals = jnp.sum(exponent, axis=-1, keepdims=True)
    weights = (exponent / totals).astype(jnp.bfloat16)
    mixed_rows = jnp.einsum("chqk,ckhe->cqhe", weights, values, preferred_element_type=jnp.float32)
    return (mixed_rows.astype(jnp.bfloat16), row_max + jnp.log(totals))


def attend_back(queries, keys_in, values, lengths, log_total, upstream, scaling):
    scores = crop_scores(queries, keys_in, lengths, scaling)
    weights = jnp.exp(scores - log_total)
    low_weights = weights.astype(jnp.bfloat16)
    grad_values = jnp.einsum(
        "chqk,cqhe->ckhe", low_weights, upstream, preferred_element_type=jnp.float32
    )
    grad_weights = jnp.einsum(
        "cqhe,ckhe->chqk", upstream, values, preferred_element_type=jnp.float32
    )
    row_dot = jnp.sum(weights * grad_weights, axis=-1, keepdims=True)
    grad_scores = (weights * (grad_weights - row_dot)).astype(jnp.bfloat16)
    grad_queries = (
        jnp.einsum("chqk,ckhe->cqhe", grad_scores, keys_in, preferred_element_type=jnp.float32)
        * scaling
    )
    grad_keys = (
        jnp.einsum("chqk,cqhe->ckhe", grad_scores, queries, preferred_element_type=jnp.float32)
        * scaling
    )
    return (grad_queries, grad_keys, grad_values)


def heads_attention(stacked, lengths):
    group_rows = stacked.shape[0]
    split_rows = stacked.reshape(group_rows, 3, -1, HD)
    wide_crops, narrow_crops = crop_views(split_rows)
    scaling = HD ** (-0.5)
    mixed_wide, log_wide = attend(
        wide_crops[:, :, 0],
        wide_crops[:, :, 1],
        wide_crops[:, :, 2],
        lengths[: 2 * IMG_DEV],
        scaling,
    )
    mixed_narrow, log_narrow = attend(
        narrow_crops[:, :, 0],
        narrow_crops[:, :, 1],
        narrow_crops[:, :, 2],
        lengths[2 * IMG_DEV :],
        scaling,
    )
    mixed_rows = join_views(mixed_wide, mixed_narrow)
    return (mixed_rows.reshape(group_rows, 1, -1), (log_wide, log_narrow))


def heads_attention_back(stacked, lengths, log_total, grad_heads):
    group_rows = stacked.shape[0]
    split_rows = stacked.reshape(group_rows, 3, -1, HD)
    upstream = grad_heads.reshape(group_rows, -1, HD)
    wide_crops, narrow_crops = crop_views(split_rows)
    up_wide, up_narrow = crop_views(upstream)
    scaling = HD ** (-0.5)
    wide_grads = attend_back(
        wide_crops[:, :, 0],
        wide_crops[:, :, 1],
        wide_crops[:, :, 2],
        lengths[: 2 * IMG_DEV],
        log_total[0],
        up_wide,
        scaling,
    )
    narrow_grads = attend_back(
        narrow_crops[:, :, 0],
        narrow_crops[:, :, 1],
        narrow_crops[:, :, 2],
        lengths[2 * IMG_DEV :],
        log_total[1],
        up_narrow,
        scaling,
    )
    wide_stack = jnp.stack(wide_grads, axis=2).astype(jnp.bfloat16)
    narrow_stack = jnp.stack(narrow_grads, axis=2).astype(jnp.bfloat16)
    return join_views(wide_stack, narrow_stack).reshape(group_rows, 3, 1, -1)


def layer_forward(hidden, weights, lengths):
    (
        qkv_w,
        query_b,
        value_b,
        out_w,
        out_b,
        gain_one,
        shift_one,
        gain_two,
        shift_two,
        up_w,
        up_b,
        down_w,
        down_b,
    ) = weights
    row_count, model_width = hidden.shape
    seq_parts = lax.axis_size("seq")
    normed_in, first_hat, first_inv = layer_norm(hidden, gain_one, shift_one)
    first_low = normed_in.astype(jnp.bfloat16)
    qkv_bias = jnp.concatenate([query_b, jnp.zeros_like(query_b), value_b])
    joint_rows = jnp.dot(first_low, qkv_w, preferred_element_type=jnp.float32) + qkv_bias
    joint_low = joint_rows.astype(jnp.bfloat16).reshape(
        row_count, 3, seq_parts, model_width // seq_parts
    )
    stacked = lax.all_to_all(joint_low, "seq", split_axis=2, concat_axis=0, tiled=True)
    mixed_rows, log_total = heads_attention(stacked, lengths)
    merged = lax.all_to_all(mixed_rows, "seq", split_axis=0, concat_axis=1, tiled=True).reshape(
        row_count, model_width
    )
    middle = hidden + jnp.dot(merged, out_w, preferred_element_type=jnp.float32) + out_b
    normed_mid, second_hat, second_inv = layer_norm(middle, gain_two, shift_two)
    second_low = normed_mid.astype(jnp.bfloat16)
    up_values = jnp.dot(second_low, up_w, preferred_element_type=jnp.float32) + up_b
    active = jax.nn.gelu(up_values, approximate=False).astype(jnp.bfloat16)
    output = middle + jnp.dot(active, down_w, preferred_element_type=jnp.float32) + down_b
    return (
        output,
        first_hat,
        first_inv,
        first_low,
        stacked,
        log_total,
        merged,
        second_hat,
        second_inv,
        second_low,
        up_values,
        active,
    )


def layer_backward(upstream, hidden, weights, lengths):
    (
        qkv_w,
        query_b,
        value_b,
        out_w,
        out_b,
        gain_one,
        shift_one,
        gain_two,
        shift_two,
        up_w,
        up_b,
        down_w,
        down_b,
    ) = weights
    saved_state = layer_forward(hidden, weights, lengths)
    (
        output,
        first_hat,
        first_inv,
        first_low,
        stacked,
        log_total,
        merged,
        second_hat,
        second_inv,
        second_low,
        up_values,
        active,
    ) = saved_state
    row_count, model_width = hidden.shape
    seq_parts = lax.axis_size("seq")
    grad_down = upstream.astype(jnp.bfloat16)
    down_w_grad = jnp.einsum("tf,td->fd", active, grad_down, preferred_element_type=jnp.float32)
    down_b_grad = jnp.sum(grad_down, axis=0, dtype=jnp.float32)
    grad_active = jnp.einsum("td,fd->tf", grad_down, down_w, preferred_element_type=jnp.float32)
    unused_value, gelu_pull = jax.vjp(partial(jax.nn.gelu, approximate=False), up_values)
    grad_up = gelu_pull(grad_active)[0].astype(jnp.bfloat16)
    up_w_grad = jnp.einsum("td,tf->df", second_low, grad_up, preferred_element_type=jnp.float32)
    up_b_grad = jnp.sum(grad_up, axis=0, dtype=jnp.float32)
    grad_normed = jnp.einsum("tf,df->td", grad_up, up_w, preferred_element_type=jnp.float32)
    grad_mid, gain_two_grad, shift_two_grad = norm_back(
        grad_normed, second_hat, second_inv, gain_two
    )
    grad_mid = grad_mid + upstream
    grad_branch = grad_mid.astype(jnp.bfloat16)
    out_w_grad = jnp.einsum("td,te->de", merged, grad_branch, preferred_element_type=jnp.float32)
    out_b_grad = jnp.sum(grad_branch, axis=0, dtype=jnp.float32)
    grad_merged = jnp.einsum(
        "te,de->td", grad_branch, out_w, preferred_element_type=jnp.float32
    ).astype(jnp.bfloat16)
    grad_heads = lax.all_to_all(
        grad_merged.reshape(row_count, seq_parts, model_width // seq_parts),
        "seq",
        split_axis=1,
        concat_axis=0,
        tiled=True,
    )
    grad_stacked = heads_attention_back(stacked, lengths, log_total, grad_heads)
    grad_joint = lax.all_to_all(
        grad_stacked, "seq", split_axis=0, concat_axis=2, tiled=True
    ).reshape(row_count, 3 * model_width)
    qkv_w_grad = jnp.einsum("td,tf->df", first_low, grad_joint, preferred_element_type=jnp.float32)
    joint_sums = jnp.sum(grad_joint, axis=0, dtype=jnp.float32)
    query_b_grad = joint_sums[:model_width]
    value_b_grad = joint_sums[2 * model_width :]
    grad_first = jnp.einsum("tf,df->td", grad_joint, qkv_w, preferred_element_type=jnp.float32)
    grad_in, gain_one_grad, shift_one_grad = norm_back(grad_first, first_hat, first_inv, gain_one)
    gradients = (
        qkv_w_grad,
        query_b_grad,
        value_b_grad,
        out_w_grad,
        out_b_grad,
        gain_one_grad,
        shift_one_grad,
        gain_two_grad,
        shift_two_grad,
        up_w_grad,
        up_b_grad,
        down_w_grad,
        down_b_grad,
    )
    return (grad_in + grad_mid, gradients)


def assemble(matrices, vectors):
    members = [None] * (len(MATRIX_SLOTS) + len(VECTOR_SLOTS))
    for place_at, slot_at in enumerate(MATRIX_SLOTS):
        members[slot_at] = matrices[place_at]
    for place_at, slot_at in enumerate(VECTOR_SLOTS):
        members[slot_at] = vectors[place_at]
    return tuple(members)


def reduce_matrix(partial_sum, bit_order):
    parts = lax.axis_size("dp")
    core = lax.axis_index("seq")
    place = lax.axis_index("dp")
    rows, columns = partial_sum.shape
    halves = partial_sum.reshape(rows, 2, columns // 2)
    kept = lax.dynamic_index_in_dim(halves, core, 1, keepdims=False)
    sent = lax.dynamic_index_in_dim(halves, 1 - core, 1, keepdims=False).astype(jnp.bfloat16)
    total = kept + lax.ppermute(sent, "seq", [(0, 1), (1, 0)]).astype(jnp.float32)
    bits = parts.bit_length() - 1
    total = total.astype(jnp.bfloat16).reshape((2,) * bits + (rows // parts, columns // 2))
    left = list(range(bits))
    for bit in bit_order:
        axis = left.index(bit)
        left.remove(bit)
        flip = 1 << (bits - 1 - bit)
        mine = (place // flip) % 2
        sent = lax.dynamic_index_in_dim(total, 1 - mine, axis, keepdims=False)
        kept = lax.dynamic_index_in_dim(total, mine, axis, keepdims=False)
        came = lax.ppermute(sent, "dp", [(i, i ^ flip) for i in range(parts)])
        total = (kept.astype(jnp.float32) + came.astype(jnp.float32)).astype(jnp.bfloat16)
    return total.reshape(rows // parts, columns // 2).astype(jnp.float32)


def reduce_vector(partial_sum):
    parts = lax.axis_size("dp")
    place = lax.axis_index("dp")
    total = partial_sum + lax.ppermute(partial_sum, "seq", [(0, 1), (1, 0)])
    bits = parts.bit_length() - 1
    total = total.reshape((2,) * bits + (-1,))
    for bit in range(bits):
        flip = 1 << (bits - 1 - bit)
        mine = (place // flip) % 2
        sent = lax.dynamic_index_in_dim(total, 1 - mine, 0, keepdims=False)
        kept = lax.dynamic_index_in_dim(total, mine, 0, keepdims=False)
        total = kept + lax.ppermute(sent, "dp", [(i, i ^ flip) for i in range(parts)])
    return total


def reduce_layer(gradients, layer_at):
    bits = lax.axis_size("dp").bit_length() - 1
    order = list(range(bits))[::-1]
    matrices = []
    for place_at, slot_at in enumerate(MATRIX_SLOTS):
        turn = (place_at + layer_at) % bits
        matrices.append(reduce_matrix(gradients[slot_at], order[turn:] + order[:turn]))
    parts = lax.axis_size("dp")
    sizes = [gradients[slot_at].shape[0] // parts for slot_at in VECTOR_SLOTS]
    packed = jnp.concatenate(
        [gradients[slot_at].reshape(parts, -1) for slot_at in VECTOR_SLOTS], axis=1
    )
    total = reduce_vector(packed)
    vectors = []
    begin = 0
    for size in sizes:
        vectors.append(total[begin : begin + size])
        begin += size
    return assemble(matrices, vectors)


def shards(
    tokens,
    crop_len,
    qkv_weight,
    query_bias,
    value_bias,
    out_weight,
    out_bias,
    first_gain,
    first_shift,
    second_gain,
    second_shift,
    up_weight,
    up_bias,
    down_weight,
    down_bias,
    cotangent,
):
    lengths = crop_len[0]
    stacks = (
        qkv_weight,
        query_bias,
        value_bias,
        out_weight,
        out_bias,
        first_gain,
        first_shift,
        second_gain,
        second_shift,
        up_weight,
        up_bias,
        down_weight,
        down_bias,
    )
    layer_count = qkv_weight.shape[0]
    member_count = len(stacks)
    inputs_kept = []
    attention_kept = []
    hidden = tokens.astype(jnp.float32)
    for layer_at in range(layer_count):
        weights = tuple((member[layer_at] for member in stacks))
        inputs_kept.append(hidden)
        saved_state = layer_forward(hidden, weights, lengths)
        attention_kept.append((saved_state[4], saved_state[5], saved_state[6]))
        hidden = saved_state[0]
    result = hidden.astype(jnp.bfloat16)
    upstream = cotangent.astype(jnp.float32)
    summed = [None] * layer_count
    for layer_at in reversed(range(layer_count)):
        weights = tuple((member[layer_at] for member in stacks))
        upstream, gradients = layer_backward(upstream, inputs_kept[layer_at], weights, lengths)
        summed[layer_at] = reduce_layer(gradients, layer_at)
    outputs = tuple(
        (
            jnp.stack([summed[layer_at][member_at] for layer_at in range(layer_count)])
            for member_at in range(member_count)
        )
    )
    grad_tokens = upstream.astype(jnp.bfloat16)
    return (
        result,
        grad_tokens,
        outputs[0],
        outputs[1],
        outputs[2],
        outputs[3],
        outputs[4],
        outputs[5],
        outputs[6],
        outputs[7],
        outputs[8],
        outputs[9],
        outputs[10],
        outputs[11],
        outputs[12],
    )


def solution(mesh):
    placed = (
        P(("dp", "seq"), None),
        P("dp", None),
        P(),
        P(),
        P(),
        P(),
        P(),
        P(),
        P(),
        P(),
        P(),
        P(),
        P(),
        P(),
        P(),
        P(("dp", "seq"), None),
    )
    return jax.shard_map(
        shards,
        mesh=mesh,
        in_specs=placed,
        out_specs=(
            P(("dp", "seq"), None),
            P(("dp", "seq"), None),
            P(None, "dp", "seq"),
            P(None, "dp"),
            P(None, "dp"),
            P(None, "dp", "seq"),
            P(None, "dp"),
            P(None, "dp"),
            P(None, "dp"),
            P(None, "dp"),
            P(None, "dp"),
            P(None, "dp", "seq"),
            P(None, "dp"),
            P(None, "dp", "seq"),
            P(None, "dp"),
        ),
        check_vma=False,
    )
```

```python
import jax
import jax.numpy as jnp
from jax import lax
from jax.experimental import pallas as pl
from jax.experimental.pallas import tpu as pltpu
from jax.sharding import PartitionSpec as P

HD = 64
GPAD = 198
LPAD = 38
HALF = 350
SPLIT = HALF - GPAD
REST = GPAD - SPLIT
WIDE = 208
SLOT = 40
LOCALS = 4
ROWS = WIDE + SLOT * LOCALS
MOVED = SLOT * LOCALS
HEADS = 12
D = 768
FF = 3072
BLOCK = 768
FFB = FF // BLOCK

EPS = 1e-06
MASKED = -1e30
SCALE = HD ** (-0.5)
BF16 = jnp.bfloat16
F32 = jnp.float32

SLOPE = 0.3
TAIL = (
    0.11962928975632706,
    0.12075411058235795,
    0.09991242677730684,
    0.12856547820765205,
    -0.05369154367102963,
    0.20636272321296675,
    -0.1572087678334877,
    0.03567620984946347,
)
VMEM_LIMIT = 56 * 1024 * 1024


def dot(left, right):
    return jnp.dot(left, right, preferred_element_type=F32)


def dot_nt(left, right):
    return lax.dot_general(left, right, (((1,), (1,)), ((), ())), preferred_element_type=F32)


def dot_tn(left, right):
    return lax.dot_general(left, right, (((0,), (0,)), ((), ())), preferred_element_type=F32)


def normal_parts(values):
    size = jnp.abs(values)
    t = 1.0 / (1.0 + SLOPE * size)
    bell = jnp.exp(-0.5 * values * values)
    tail = TAIL[-1]
    for factor in TAIL[-2::-1]:
        tail = tail * t + factor
    tail = tail * t * bell
    return jnp.where(values >= 0, 1.0 - tail, tail), bell * 0.3989422804014327


def norm_parts(hidden):
    row_mean = jnp.mean(hidden, axis=-1, keepdims=True)
    centered = hidden - row_mean
    inverse = lax.rsqrt(jnp.mean(centered * centered, axis=-1, keepdims=True) + EPS)
    return centered * inverse, inverse


def norm_back(upstream, normed, inverse, norm_gain):
    scaled = upstream * norm_gain
    centered = scaled - jnp.mean(scaled, axis=-1, keepdims=True)
    centered = centered - normed * jnp.mean(scaled * normed, axis=-1, keepdims=True)
    return centered * inverse


def column_sum(array):
    return jnp.sum(array.astype(F32), axis=0, keepdims=True)


def slot_row(position):
    crop = jnp.zeros_like(position)
    for at in range(1, LOCALS):
        crop = crop + (position >= SLOT * at).astype(jnp.int32)
    inner = position - SLOT * crop
    return jnp.where((position >= 0) & (inner < LPAD), LPAD * crop + inner, -4 * HALF)


def spread(own, came, core):
    position = lax.broadcasted_iota(jnp.int32, (ROWS, HALF), 0)
    column = lax.broadcasted_iota(jnp.int32, (ROWS, HALF), 1)
    local = slot_row(position - WIDE)
    own0 = jnp.where(position < GPAD, position, -1)
    came0 = local + REST
    own1 = jnp.where(
        (position >= SPLIT) & (position < GPAD), position - SPLIT, local + GPAD
    )
    came1 = jnp.where(position < SPLIT, position + GPAD, -1)
    own_from = own0 * (1 - core) + own1 * core
    came_from = came0 * (1 - core) + came1 * core
    return dot(jnp.where(own_from == column, 1.0, 0.0).astype(BF16), own) + dot(
        jnp.where(came_from == column, 1.0, 0.0).astype(BF16), came
    )


def gather_back(own, came, core):
    row = lax.broadcasted_iota(jnp.int32, (HALF, ROWS), 0)
    position = lax.broadcasted_iota(jnp.int32, (HALF, ROWS), 1)
    local = slot_row(position - WIDE)
    own0 = jnp.where(position < GPAD, position, -1)
    own1 = jnp.where(
        (position >= SPLIT) & (position < GPAD), position - SPLIT, local + GPAD
    )
    own_to = own0 * (1 - core) + own1 * core
    came_row = lax.broadcasted_iota(jnp.int32, (HALF, MOVED), 0)
    came_position = lax.broadcasted_iota(jnp.int32, (HALF, MOVED), 1)
    came0 = jnp.where(came_position < SPLIT, came_position + GPAD, -1)
    came1 = slot_row(came_position) + REST
    came_to = came0 * (1 - core) + came1 * core
    return (
        dot(jnp.where(own_to == row, 1.0, 0.0).astype(BF16), own)
        + dot(jnp.where(came_to == came_row, 1.0, 0.0).astype(BF16), came)
    ).astype(BF16)


def head_lanes():
    lane = lax.broadcasted_iota(jnp.int32, (1, 2 * HD), 1)
    left = jnp.where(lane < HD, 1.0, 0.0)
    return (left.astype(BF16), (1.0 - left).astype(BF16)), (
        (left * SCALE).astype(BF16),
        ((1.0 - left) * SCALE).astype(BF16),
    )


def pair(at, block):
    return slice(block * D + 2 * HD * at, block * D + 2 * HD * (at + 1))


def windows(lens_ref, core):
    column = lax.broadcasted_iota(jnp.int32, (WIDE, WIDE), 1)
    plan = [(slice(0, WIDE), column < lens_ref[core])]
    for at in range(LOCALS // 2):
        row = lax.broadcasted_iota(jnp.int32, (2 * SLOT, 2 * SLOT), 0)
        column = lax.broadcasted_iota(jnp.int32, (2 * SLOT, 2 * SLOT), 1)
        first = lens_ref[2 + LOCALS * core + 2 * at]
        second = lens_ref[3 + LOCALS * core + 2 * at]
        allowed = ((row < SLOT) & (column < first)) | (
            (row >= SLOT) & (column >= SLOT) & (column < SLOT + second)
        )
        begin = WIDE + 2 * SLOT * at
        plan.append((slice(begin, begin + 2 * SLOT), allowed))
    return plan


def attend(lens_ref, core, joint_ref, merged_ref, log_ref):
    plain, scaled = head_lanes()
    lane = lax.broadcasted_iota(jnp.int32, (1, 128), 1)
    for rows, allowed in windows(lens_ref, core):
        count = rows.stop - rows.start
        logs = jnp.zeros((count, 128), F32)
        for at in range(HEADS // 2):
            queries = joint_ref[rows, pair(at, 0)]
            keys = joint_ref[rows, pair(at, 1)]
            values = joint_ref[rows, pair(at, 2)]
            mixed = jnp.zeros((count, 2 * HD), F32)
            for side in range(2):
                scores = jnp.where(allowed, dot_nt(queries * scaled[side], keys), MASKED)
                row_max = jnp.max(scores, axis=-1, keepdims=True)
                exponent = jnp.exp(scores - row_max)
                totals = jnp.sum(exponent, axis=-1, keepdims=True)
                weights = (exponent * (1.0 / totals)).astype(BF16)
                mixed = mixed + dot(weights, values * plain[side])
                logs = jnp.where(lane == 2 * at + side, row_max + jnp.log(totals), logs)
            merged_ref[rows, pair(at, 0)] = mixed.astype(BF16)
        log_ref[rows, :] = logs


def attend_back(lens_ref, core, joint_ref, up_ref, log_ref, grad_ref):
    plain, scaled = head_lanes()
    lane = lax.broadcasted_iota(jnp.int32, (1, 128), 1)
    for rows, allowed in windows(lens_ref, core):
        logs = log_ref[rows, :]
        for at in range(HEADS // 2):
            queries = joint_ref[rows, pair(at, 0)]
            keys = joint_ref[rows, pair(at, 1)]
            values = joint_ref[rows, pair(at, 2)]
            upstream = up_ref[rows, pair(at, 0)]
            grad_q = grad_k = grad_v = 0.0
            for side in range(2):
                scaled_queries = queries * scaled[side]
                own_up = upstream * plain[side]
                scores = jnp.where(allowed, dot_nt(scaled_queries, keys), MASKED)
                log_total = jnp.sum(
                    jnp.where(lane == 2 * at + side, logs, 0.0), axis=-1, keepdims=True
                )
                weights = jnp.exp(scores - log_total)
                grad_weights = dot_nt(own_up, values)
                weighted = weights * grad_weights
                row_dot = jnp.sum(weighted, axis=-1, keepdims=True)
                grad_scores = (weighted - weights * row_dot).astype(BF16)
                grad_v = grad_v + dot_tn(weights.astype(BF16), own_up)
                grad_k = grad_k + dot_tn(grad_scores, scaled_queries)
                grad_q = grad_q + dot(grad_scores, keys * scaled[side])
            grad_ref[rows, pair(at, 0)] = grad_q.astype(BF16)
            grad_ref[rows, pair(at, 1)] = grad_k.astype(BF16)
            grad_ref[rows, pair(at, 2)] = grad_v.astype(BF16)


class Copies:
    def __init__(self, sems):
        self.sems = sems
        self.started = 0

    def start(self, source, target):
        copy = pltpu.make_async_copy(source, target, self.sems.at[self.started])
        self.started += 1
        copy.start()
        return copy


def wait_all(copies):
    for copy in copies:
        copy.wait()


def columns_of(ref, at):
    return ref.at[:, BLOCK * at : BLOCK * (at + 1)]


def core_half(ref, core):
    width = ref.shape[1] // 2
    return ref.at[:, pl.ds(pl.multiple_of(core * width, 128), width)]


def vector(ref, layer):
    return ref[layer : layer + 1, :]


def ahead_kernel(
    lens, tokens, came, gain1, shift1, query_b, value_b, out_b, gain2, shift2, up_b, down_b,
    qkv_w, out_w, up_w, down_w, *refs,
):
    outs, held = refs[:18], refs[18:36]
    weights, weight_sems, out_sems = refs[36:]
    core = lax.axis_index("seq")
    loads = Copies(weight_sems)
    stores = Copies(out_sems)
    fetched = []
    for layer in range(2):
        slot = 12 * layer
        qkv = [loads.start(columns_of(qkv_w.at[layer], at), weights.at[slot + at]) for at in range(3)]
        out = [loads.start(out_w.at[layer], weights.at[slot + 3])]
        ups = [loads.start(columns_of(up_w.at[layer], at), weights.at[slot + 4 + at]) for at in range(FFB)]
        downs = []
        if layer == 0:
            downs = [
                loads.start(down_w.at[layer, BLOCK * at : BLOCK * (at + 1), :], weights.at[slot + 8 + at])
                for at in range(FFB)
            ]
        fetched.append((slot, qkv, out, ups, downs))
    leaving = []

    def leave(at):
        leaving.append(stores.start(held[at], outs[at]))

    hidden = spread(tokens[...], came[...], core)
    for layer in range(2):
        slot, qkv, out, ups, downs = fetched[layer]
        at = 9 * layer
        hidden_ref, low1_ref, joint_ref, merged_ref, log_ref, middle_ref, low2_ref, active_ref, slope_ref = (
            held[at : at + 9]
        )
        hidden_ref[...] = hidden
        leave(at)
        normed, _ = norm_parts(hidden)
        low1_ref[...] = (normed * vector(gain1, layer) + vector(shift1, layer)).astype(BF16)
        leave(at + 1)
        wait_all(qkv)
        for block, bias in enumerate((vector(query_b, layer), None, vector(value_b, layer))):
            joint = dot(low1_ref[...], weights[slot + block])
            if bias is not None:
                joint = joint + bias
            joint_ref[:, BLOCK * block : BLOCK * (block + 1)] = joint.astype(BF16)
        leave(at + 2)
        attend(lens, core, joint_ref, merged_ref, log_ref)
        leave(at + 3)
        leave(at + 4)
        wait_all(out)
        middle = hidden_ref[...] + dot(merged_ref[...], weights[slot + 3]) + vector(out_b, layer)
        middle_ref[...] = middle
        leave(at + 5)
        normed, _ = norm_parts(middle)
        low2_ref[...] = (normed * vector(gain2, layer) + vector(shift2, layer)).astype(BF16)
        leave(at + 6)
        wait_all(ups)
        for block in range(FFB):
            columns = slice(BLOCK * block, BLOCK * (block + 1))
            up_values = dot(low2_ref[...], weights[slot + 4 + block]) + up_b[layer : layer + 1, columns]
            mass, bell = normal_parts(up_values)
            active_ref[:, columns] = (up_values * mass).astype(BF16)
            slope_ref[:, columns] = (mass + up_values * bell).astype(BF16)
        leave(at + 7)
        leave(at + 8)
        if layer == 0:
            wait_all(downs)
            down = weights[slot + 8 : slot + 12].reshape(FF, D)
            hidden = middle_ref[...] + dot(active_ref[...], down) + vector(down_b, layer)
    wait_all(leaving)


def mlp_back_kernel(layer, *refs):
    top = layer == 1
    if top:
        own_cot, came_cot, down_b, *refs = refs
    gain2, out_w, up_w, down_w, *refs = refs
    sources, refs = refs[:3], refs[3:]
    outs, refs = refs[: 7 + 3 * top], refs[7 + 3 * top :]
    held, refs = refs[:3], refs[3:]
    grad_up_ref, mid_ref, branch_ref, grad_merged_ref, sums_ref, *refs = refs
    if top:
        grad_ref, other_ref, result_ref, *refs = refs
    weights, load_sems, out_sems = refs
    core = lax.axis_index("seq")
    loads = Copies(load_sems)
    stores = Copies(out_sems)
    coming = [loads.start(source, target) for source, target in zip(sources, held)]
    downs = [
        loads.start(down_w.at[layer, BLOCK * at : BLOCK * (at + 1), :], weights.at[at])
        for at in range(FFB)
    ]
    ups = [loads.start(columns_of(up_w.at[layer], at), weights.at[FFB + at]) for at in range(FFB)]
    out = loads.start(out_w.at[layer], weights.at[2 * FFB])
    slope_ref, middle_ref = held[0], held[1]
    leaving = []
    if top:
        active_ref, upstream_ref = held[2], None
        grad_ref[...] = spread(own_cot[...], came_cot[...], core).astype(BF16)
        other_ref[...] = spread(came_cot[...], own_cot[...], 1 - core).astype(BF16)
        leaving.append(stores.start(core_half(grad_ref, core), outs[8]))
        leaving.append(stores.start(core_half(other_ref, core), outs[9]))
        grad = grad_ref[...]
    else:
        wait_all(coming)
        upstream_ref = held[2]
        grad = upstream_ref[...].astype(BF16)
    sums_ref[3:4, :] = column_sum(grad)
    wait_all(downs)
    if top:
        wait_all(coming)
        result = middle_ref[...] + dot(active_ref[...], weights[0:FFB].reshape(FF, D)) + vector(down_b, layer)
        result_ref[...] = result.astype(BF16)
        leaving.append(stores.start(result_ref, outs[7]))
    wait_all(ups)
    back = 0.0
    for block in range(FFB):
        columns = slice(BLOCK * block, BLOCK * (block + 1))
        grad_up = (dot_nt(grad, weights[block]) * slope_ref[:, columns].astype(F32)).astype(BF16)
        grad_up_ref[:, columns] = grad_up
        sums_ref[4 + block : 5 + block, :] = column_sum(grad_up)
        back = back + dot_nt(grad_up, weights[FFB + block])
    leaving.append(stores.start(core_half(grad_up_ref, 1 - core), outs[1]))
    leaving.append(stores.start(core_half(grad_up_ref, core), outs[0]))
    normed, inverse = norm_parts(middle_ref[...])
    sums_ref[1:2, :] = column_sum(back * normed)
    sums_ref[2:3, :] = column_sum(back)
    upstream = grad.astype(F32) if top else upstream_ref[...]
    grad_mid = norm_back(back, normed, inverse, vector(gain2, layer)) + upstream
    mid_ref[...] = grad_mid
    leaving.append(stores.start(mid_ref, outs[4]))
    branch = grad_mid.astype(BF16)
    branch_ref[...] = branch
    leaving.append(stores.start(core_half(branch_ref, core), outs[2]))
    leaving.append(stores.start(core_half(branch_ref, 1 - core), outs[3]))
    sums_ref[0:1, :] = column_sum(branch)
    leaving.append(stores.start(sums_ref, outs[6]))
    out.wait()
    grad_merged_ref[...] = dot_nt(branch, weights[2 * FFB]).astype(BF16)
    leaving.append(stores.start(grad_merged_ref, outs[5]))
    wait_all(leaving)


def attention_back_kernel(layer, lens, gain1, qkv_w, *refs):
    top = layer == 1
    sources, refs = refs[:5], refs[5:]
    outs, refs = refs[: 4 + 2 * top], refs[4 + 2 * top :]
    held, refs = refs[:5], refs[5:]
    grad_joint_ref, sums_ref, out_ref, *refs = refs
    if top:
        upstream_ref, *refs = refs
    weights, load_sems, out_sems = refs
    core = lax.axis_index("seq")
    loads = Copies(load_sems)
    stores = Copies(out_sems)
    coming = [loads.start(source, target) for source, target in zip(sources, held)]
    qkv = [loads.start(columns_of(qkv_w.at[layer], at), weights.at[at]) for at in range(3)]
    joint_ref, up_ref, log_ref, hidden_ref, mid_ref = held
    wait_all(coming[:3])
    leaving = []
    attend_back(lens, core, joint_ref, up_ref, log_ref, grad_joint_ref)
    leaving.append(stores.start(core_half(grad_joint_ref, 1 - core), outs[1]))
    leaving.append(stores.start(core_half(grad_joint_ref, core), outs[0]))
    sums_ref[...] = jnp.zeros_like(sums_ref)
    sums_ref[0:1, :] = column_sum(grad_joint_ref[:, 0:D])
    sums_ref[1:2, :] = column_sum(grad_joint_ref[:, 2 * D : 3 * D])
    wait_all(qkv)
    grad_first = 0.0
    for block in range(3):
        grad_first = grad_first + dot_nt(
            grad_joint_ref[:, BLOCK * block : BLOCK * (block + 1)], weights[block]
        )
    wait_all(coming[3:])
    normed, inverse = norm_parts(hidden_ref[...])
    sums_ref[2:3, :] = column_sum(grad_first * normed)
    sums_ref[3:4, :] = column_sum(grad_first)
    leaving.append(stores.start(sums_ref, outs[2]))
    grad_in = norm_back(grad_first, normed, inverse, vector(gain1, layer)) + mid_ref[...]
    out_ref[...] = grad_in.astype(BF16)
    if top:
        upstream_ref[...] = grad_in
        leaving.append(stores.start(upstream_ref, outs[3]))
        leaving.append(stores.start(core_half(out_ref, core), outs[4]))
        leaving.append(stores.start(core_half(out_ref, 1 - core), outs[5]))
    else:
        leaving.append(stores.start(out_ref, outs[3]))
    wait_all(leaving)


def part_order(parts, core_orders):
    bits = parts.bit_length() - 1

    def part_at(position, place, core):
        moved = [0, 0]
        for side in range(2):
            for hop, bit in enumerate(core_orders[side]):
                moved[side] |= ((position >> (bits - 1 - hop)) & 1) << bit
        return place ^ (moved[0] * (1 - core) + moved[1] * core)

    return part_at


def weight_kernel(parts, core_orders, own_x, other_x, own_g, other_g, *refs):
    kept, sent, x_ref, g_ref, stage, load_sems, out_sems = refs
    core = lax.axis_index("seq")
    place = lax.axis_index("dp")
    loads = Copies(load_sems)
    stores = Copies(out_sems)
    first, second = slice(0, ROWS), slice(ROWS, 2 * ROWS)
    coming = [loads.start(own_g, g_ref.at[first, :]), loads.start(other_g, g_ref.at[second, :])]
    blocks = own_x.shape[1] // BLOCK
    share = stage.shape[1]
    for at in range(blocks):
        columns = slice(BLOCK * at, BLOCK * (at + 1))
        coming.append(loads.start(own_x.at[:, columns], x_ref.at[first, columns]))
        coming.append(loads.start(other_x.at[:, columns], x_ref.at[second, columns]))
    wait_all(coming[:2])
    count = BLOCK // share
    for at in range(blocks):
        wait_all(coming[2 + 2 * at : 4 + 2 * at])
        total = dot_tn(x_ref[:, BLOCK * at : BLOCK * (at + 1)], g_ref[...])
        stage[count * at : count * (at + 1)] = total.astype(BF16).reshape(count, share, -1)
    part_at = part_order(parts, core_orders)
    leaving = []
    half = parts // 2
    for position in list(range(half, parts)) + list(range(half)):
        target = sent if position >= half else kept
        leaving.append(
            stores.start(stage.at[part_at(position, place, core)], target.at[position % half])
        )
    wait_all(leaving)


def plain_weight_kernel(own_x, other_x, own_g, other_g, out):
    total = dot_tn(own_x[...], own_g[...]) + dot_tn(other_x[...], other_g[...])
    out[...] = total.astype(BF16)


def add_kernel(*refs):
    total = 0.0
    for ref in refs[:-1]:
        total = total + ref[...].astype(F32)
    refs[-1][...] = total.astype(refs[-1].dtype)


def assemble_kernel(result, came_result, tokens, came_tokens, result_out, tokens_out):
    core = lax.axis_index("seq")
    result_out[...] = gather_back(result[...], came_result[...], core)
    tokens_out[...] = gather_back(tokens[...], came_tokens[...], core)


ANY = pl.BlockSpec(memory_space=pl.ANY)


def shaped(*dims, dtype=BF16):
    return jax.ShapeDtypeStruct(dims, dtype)


def held(*dims, dtype=BF16):
    return pltpu.VMEM(dims, dtype)


def sems(count):
    return pltpu.SemaphoreType.DMA((count,))


def whole(shape):
    return pl.BlockSpec(shape, lambda: (0,) * len(shape))


def call(kernel, name, operands, outs, scratch, lens=None, after=(), out_specs=None):
    first = [] if lens is None else [lens]
    first_specs = [] if lens is None else [pl.BlockSpec(memory_space=pltpu.SMEM)]
    skip = len(first) + len(after)

    def body(*refs):
        kernel(*refs[: len(first)], *refs[skip:])

    return pl.pallas_call(
        body,
        in_specs=first_specs
        + [ANY] * len(after)
        + [whole(array.shape) if near else ANY for array, near in operands],
        out_specs=out_specs or [ANY] * len(outs),
        out_shape=list(outs),
        scratch_shapes=list(scratch),
        compiler_params=pltpu.CompilerParams(vmem_limit_bytes=VMEM_LIMIT),
        cost_estimate=pl.CostEstimate(flops=1, bytes_accessed=1, transcendentals=0),
        name=name,
    )(*first, *after, *(array for array, _ in operands))


def near(*arrays):
    return [(array, True) for array in arrays]


def far(*arrays):
    return [(array, False) for array in arrays]


def ahead(lens, tokens, came, vectors, matrices):
    kept = []
    for _ in range(2):
        kept += [
            (ROWS, D, F32), (ROWS, D, BF16), (ROWS, 3 * D, BF16), (ROWS, D, BF16), (ROWS, 128, F32), (ROWS, D, F32),
            (ROWS, D, BF16), (ROWS, FF, BF16), (ROWS, FF, BF16),
        ]
    return call(
        ahead_kernel, "ahead", near(tokens, came, *vectors) + far(*matrices),
        [shaped(r, c, dtype=t) for r, c, t in kept],
        [held(r, c, dtype=t) for r, c, t in kept] + [held(20, D, BLOCK), sems(20), sems(len(kept))],
        lens=lens,
    )


def mlp_back(layer, slope, middle, third, gain2, matrices, cots=None, down_b=None, after=()):
    top = layer == 1
    operands = near(*cots, down_b) if top else []
    operands += near(gain2) + far(*matrices) + far(slope, middle, third)
    outs = [
        shaped(ROWS, FF // 2), shaped(ROWS, FF // 2), shaped(ROWS, D // 2), shaped(ROWS, D // 2),
        shaped(ROWS, D, dtype=F32), shaped(ROWS, D), shaped(8, D, dtype=F32),
    ]
    if top:
        outs += [shaped(ROWS, D), shaped(ROWS, D // 2), shaped(ROWS, D // 2)]
    scratch = [held(ROWS, FF), held(ROWS, D, dtype=F32)]
    scratch += [held(ROWS, FF) if top else held(ROWS, D, dtype=F32)]
    scratch += [held(ROWS, FF), held(ROWS, D, dtype=F32), held(ROWS, D), held(ROWS, D), held(8, D, dtype=F32)]
    if top:
        scratch += [held(ROWS, D), held(ROWS, D), held(ROWS, D)]
    scratch += [held(2 * FFB + 1, D, BLOCK), sems(2 * FFB + 4), sems(10)]
    return call(
        lambda *refs: mlp_back_kernel(layer, *refs), f"mlp_back{layer}", operands, outs, scratch, after=after
    )


def attention_back(layer, lens, joint, grad_merged, log, hidden, mid, gain1, qkv_w, after=()):
    top = layer == 1
    outs = [shaped(ROWS, 3 * D // 2), shaped(ROWS, 3 * D // 2), shaped(8, D, dtype=F32)]
    if top:
        outs += [shaped(ROWS, D, dtype=F32), shaped(ROWS, D // 2), shaped(ROWS, D // 2)]
    else:
        outs += [shaped(ROWS, D)]
    scratch = [
        held(ROWS, 3 * D), held(ROWS, D), held(ROWS, 128, dtype=F32), held(ROWS, D, dtype=F32),
        held(ROWS, D, dtype=F32), held(ROWS, 3 * D), held(8, D, dtype=F32), held(ROWS, D),
    ]
    if top:
        scratch += [held(ROWS, D, dtype=F32)]
    scratch += [held(3, D, BLOCK), sems(8), sems(6)]
    return call(
        lambda lens, *refs: attention_back_kernel(layer, lens, *refs), f"attention_back{layer}",
        near(gain1) + far(qkv_w, joint, grad_merged, log, hidden, mid), outs, scratch, lens=lens, after=after,
    )


def add(terms, begin, count, name, after=()):
    share, columns = terms[0].shape[1:]
    skip = len(after)
    return pl.pallas_call(
        lambda *refs: add_kernel(*refs[skip:]),
        grid=(count,),
        in_specs=[ANY] * skip
        + [pl.BlockSpec((1, share, columns), lambda step: (begin + step, 0, 0)) for _ in terms],
        out_specs=pl.BlockSpec((1, share, columns), lambda step: (step, 0, 0)),
        out_shape=shaped(count, share, columns),
        cost_estimate=pl.CostEstimate(flops=1, bytes_accessed=1, transcendentals=0),
        name=name,
    )(*after, *terms)


def swap(array):
    return lax.ppermute(array, "seq", [(0, 1), (1, 0)])


ORDERS = ((0, 2, 1, 3), (1, 2, 0, 3))


class Halving:
    def __init__(self, name, kept, sent, orders):
        self.name, self.orders = name, orders
        self.parts = 2 * kept.shape[0]
        self.hop = 0
        self.terms = [kept]
        self.sent = sent
        self.send()

    def send(self):
        pairs = []
        for place in range(self.parts):
            for core in range(2):
                other = place ^ (1 << self.orders[core][self.hop])
                pairs.append((2 * place + core, 2 * other + core))
        self.terms.append(lax.ppermute(self.sent, ("dp", "seq"), pairs))
        self.hop += 1

    def step(self, after=()):
        count = self.parts >> (self.hop + 1)
        self.sent = add(self.terms, count, count, f"{self.name}_hop{self.hop}", after)
        self.send()
        return self.sent

    def total(self):
        while self.hop < self.parts.bit_length() - 1:
            self.step()
        return sum(term[0].astype(F32) for term in self.terms)


def weight_gradient(name, own_x, other_x, own_g, other_g, orders, after=()):
    parts = lax.axis_size("dp")
    rows, columns = own_x.shape[1], own_g.shape[1]
    share = rows // parts
    return call(
        lambda *refs: weight_kernel(parts, orders, *refs), name, far(own_x, other_x, own_g, other_g),
        [shaped(parts // 2, share, columns)] * 2,
        [held(2 * ROWS, rows), held(2 * ROWS, columns), held(parts, share, columns),
         sems(2 + 2 * (rows // BLOCK)), sems(parts)],
        after=after,
    )


def plain_weight_gradient(name, own_x, other_x, own_g, other_g):
    rows, columns = own_x.shape[1], own_g.shape[1]
    x_spec = pl.BlockSpec((ROWS, BLOCK), lambda step: (0, step))
    g_spec = pl.BlockSpec((ROWS, columns), lambda step: (0, 0))
    return pl.pallas_call(
        plain_weight_kernel,
        grid=(rows // BLOCK,),
        in_specs=[x_spec, x_spec, g_spec, g_spec],
        out_specs=pl.BlockSpec((BLOCK, columns), lambda step: (step, 0)),
        out_shape=shaped(rows, columns),
        compiler_params=pltpu.CompilerParams(vmem_limit_bytes=VMEM_LIMIT),
        name=name,
    )(own_x, other_x, own_g, other_g)


def plain_halving(total, bit_order):
    parts = lax.axis_size("dp")
    place = lax.axis_index("dp")
    bits = parts.bit_length() - 1
    total = total.reshape((2,) * bits + (total.shape[0] // parts, total.shape[1]))
    left = list(range(bits))[::-1]
    terms = [total]
    for bit in bit_order:
        axis = left.index(bit)
        left.remove(bit)
        mine = (place >> bit) & 1
        sent = sum(lax.dynamic_index_in_dim(t, 1 - mine, axis, keepdims=False).astype(F32) for t in terms)
        terms = [lax.dynamic_index_in_dim(t, mine, axis, keepdims=False) for t in terms]
        terms.append(
            lax.ppermute(sent.astype(BF16), "dp", [(i, i ^ (1 << bit)) for i in range(parts)])
        )
    return sum(t.astype(F32) for t in terms)


def sum_everywhere(array):
    total = array + swap(array)
    parts = lax.axis_size("dp")
    for bit in range(parts.bit_length() - 1):
        total = total + lax.ppermute(total, "dp", [(i, i ^ (1 << bit)) for i in range(parts)])
    return total


def split_kernel(parts, total, *outs):
    place = lax.axis_index("dp")
    width = D // parts
    turned = pltpu.roll(total[...], lax.rem(D - place * width, D), 1)
    rows = (0, 1, 8, 2, 3, 9, 10, 11)
    for out, row in zip(outs[:8], rows):
        for layer in range(2):
            out[layer : layer + 1, :] = turned[16 * layer + row : 16 * layer + row + 1, 0:width]
    begin = place * (FF // parts)
    offset = lax.rem(begin, D)
    for layer in range(2):
        row = total[pl.ds(16 * layer + 12 + lax.div(begin, D), 1), :]
        moved = pltpu.roll(jnp.broadcast_to(row, (8, D)), lax.rem(D - offset, D), 1)
        outs[8][layer : layer + 1, :] = moved[0:1, 0 : FF // parts]


def shards(
    tokens, crop_len, qkv_weight, query_bias, value_bias, out_weight, out_bias, first_gain, first_shift,
    second_gain, second_shift, up_weight, up_bias, down_weight, down_bias, cotangent,
):
    parts = lax.axis_size("dp")
    lens = crop_len.reshape(-1)
    core = lax.axis_index("seq")
    came_tokens = swap(tokens)
    came_cot = swap(cotangent)
    kept = ahead(
        lens, tokens, came_tokens,
        (first_gain, first_shift, query_bias, value_bias, out_bias, second_gain, second_shift, up_bias, down_bias),
        (qkv_weight, out_weight, up_weight, down_weight),
    )
    hidden0, low1_0, joint0, merged0, log0, middle0, low2_0, active0, slope0 = kept[:9]
    hidden1, low1_1, joint1, merged1, log1, middle1, low2_1, active1, slope1 = kept[9:]
    tiled = (D // parts) % 16 == 0 and parts == 16
    reductions = {}

    def product(name, own_x, own_g, sent_g, after=(), other_g=None):
        other_g = swap(sent_g) if other_g is None else other_g
        if not tiled:
            total = plain_weight_gradient(name, own_x, swap(own_x), own_g, other_g)
            reductions[name] = plain_halving(total, range(parts.bit_length() - 1))
            return (total,)
        here, gone = weight_gradient(name, own_x, swap(own_x), own_g, other_g, ORDERS, after)
        reductions[name] = Halving(name, here, gone, ORDERS)
        return (gone,)

    def step(name, after=()):
        return (reductions[name].step(after),) if tiled else after

    matrices = (out_weight, up_weight, down_weight)
    up_own1, up_sent1, branch_own1, branch_sent1, mid1, grad_merged1, sums_b1, result, grad_own1, grad_other1 = mlp_back(
        1, slope1, middle1, active1, second_gain, matrices, (cotangent, came_cot), down_bias
    )
    last = product("down1", active1, grad_own1, None, (grad_merged1,), grad_other1)
    last = product("up1", low2_1, up_own1, up_sent1, last)
    joint_own1, joint_sent1, sums_a1, upstream, grad_own0, grad_sent0 = attention_back(
        1, lens, joint1, grad_merged1, log1, hidden1, mid1, first_gain, qkv_weight, after=last
    )
    last = step("down1", (joint_own1,))
    last = product("out1", merged1, branch_own1, branch_sent1, last)
    last = step("up1", last)
    up_own0, up_sent0, branch_own0, branch_sent0, mid0, grad_merged0, sums_b0 = mlp_back(
        0, slope0, middle0, upstream, second_gain, matrices, after=last
    )
    last = step("down1", (up_own0,))
    last = product("qkv1", low1_1, joint_own1, joint_sent1, last)
    last = step("up1", last)
    last = step("out1", last)
    last = product("down0", active0, grad_own0, grad_sent0, last)
    last = step("down1", last)
    last = step("qkv1", last)
    joint_own0, joint_sent0, sums_a0, grad_tokens = attention_back(
        0, lens, joint0, grad_merged0, log0, hidden0, mid0, first_gain, qkv_weight, after=last
    )
    last = step("out1", (joint_own0,))
    last = product("up0", low2_0, up_own0, up_sent0, last)
    last = step("up1", last)
    last = step("qkv1", last)
    last = step("down0", last)
    last = product("out0", merged0, branch_own0, branch_sent0, last)
    last = product("qkv0", low1_0, joint_own0, joint_sent0, last)

    def moved(array):
        begin = WIDE * (1 - core)
        return swap(lax.dynamic_slice(array, (begin, 0), (MOVED, D)))

    result, grad_tokens = call(
        assemble_kernel, "assemble",
        near(result, moved(result), grad_tokens, moved(grad_tokens)),
        [shaped(HALF, D)] * 2, [], out_specs=[whole((HALF, D))] * 2, after=last,
    )
    sums = sum_everywhere(jnp.concatenate([sums_a0, sums_b0, sums_a1, sums_b1]))
    narrow = shaped(2, D // parts, dtype=F32)
    query_g, value_g, out_g, gain1_g, shift1_g, gain2_g, shift2_g, down_g, up_g = call(
        lambda *refs: split_kernel(parts, *refs), "split", near(sums),
        [narrow] * 8 + [shaped(2, FF // parts, dtype=F32)], [],
        out_specs=[whole((2, D // parts))] * 8 + [whole((2, FF // parts))],
    )

    def both(name):
        pair_of = [reductions[name + "0"], reductions[name + "1"]]
        return jnp.stack([r.total() if tiled else r for r in pair_of])

    qkv_g, out_wg, up_wg, down_wg = both("qkv"), both("out"), both("up"), both("down")
    return (
        result, grad_tokens, qkv_g, query_g, value_g, out_wg, out_g, gain1_g, shift1_g, gain2_g, shift2_g, up_wg,
        up_g, down_wg, down_g,
    )


def solution(mesh):
    rows = P(("dp", "seq"), None)
    matrix = P(None, "dp", "seq")
    narrow = P(None, "dp")
    return jax.shard_map(
        shards,
        mesh=mesh,
        in_specs=(rows, P("dp", None)) + (P(),) * 13 + (rows,),
        out_specs=(
            rows, rows, matrix, narrow, narrow, matrix, narrow, narrow, narrow, narrow, narrow, matrix, narrow,
            matrix, narrow,
        ),
        check_vma=False,
    )
```

```python
import jax
import jax.numpy as jnp
from jax import lax
from jax.experimental import pallas as pl
from jax.experimental.pallas import tpu as pltpu
from jax.sharding import PartitionSpec as P

HD = 64
GPAD = 198
LPAD = 38
HALF = 350
SPLIT = HALF - GPAD
REST = GPAD - SPLIT
WIDE = 208
SLOT = 40
LOCALS = 4
ROWS = WIDE + SLOT * LOCALS
MOVED = SLOT * LOCALS
HEADS = 12
D = 768
FF = 3072
BLOCK = 768
FFB = FF // BLOCK

EPS = 1e-06
MASKED = -1e30
SCALE = HD ** (-0.5)
BF16 = jnp.bfloat16
F32 = jnp.float32

VMEM_LIMIT = 63 * 1024 * 1024


def dot(left, right):
    return jnp.dot(left, right, preferred_element_type=F32)


def dot_nt(left, right):
    return lax.dot_general(left, right, (((1,), (1,)), ((), ())), preferred_element_type=F32)


def dot_tn(left, right):
    return lax.dot_general(left, right, (((0,), (0,)), ((), ())), preferred_element_type=F32)


def normal_parts(values):
    mass = 0.5 + 0.5 * lax.erf(values * 0.7071067811865476)
    return mass, jnp.exp(-0.5 * values * values) * 0.3989422804014327


def norm_parts(hidden):
    row_mean = jnp.mean(hidden, axis=-1, keepdims=True)
    centered = hidden - row_mean
    inverse = lax.rsqrt(jnp.mean(centered * centered, axis=-1, keepdims=True) + EPS)
    return centered * inverse, inverse


def norm_back(upstream, normed, inverse, norm_gain):
    scaled = upstream * norm_gain
    centered = scaled - jnp.mean(scaled, axis=-1, keepdims=True)
    centered = centered - normed * jnp.mean(scaled * normed, axis=-1, keepdims=True)
    return centered * inverse


def column_sum(array):
    return jnp.sum(array.astype(F32), axis=0, keepdims=True)


def slot_row(position):
    crop = jnp.zeros_like(position)
    for at in range(1, LOCALS):
        crop = crop + (position >= SLOT * at).astype(jnp.int32)
    inner = position - SLOT * crop
    return jnp.where((position >= 0) & (inner < LPAD), LPAD * crop + inner, -4 * HALF)


def spread(own, came, core):
    position = lax.broadcasted_iota(jnp.int32, (ROWS, HALF), 0)
    column = lax.broadcasted_iota(jnp.int32, (ROWS, HALF), 1)
    local = slot_row(position - WIDE)
    own0 = jnp.where(position < GPAD, position, -1)
    came0 = local + REST
    own1 = jnp.where(
        (position >= SPLIT) & (position < GPAD), position - SPLIT, local + GPAD
    )
    came1 = jnp.where(position < SPLIT, position + GPAD, -1)
    own_from = own0 * (1 - core) + own1 * core
    came_from = came0 * (1 - core) + came1 * core
    return dot(jnp.where(own_from == column, 1.0, 0.0).astype(BF16), own) + dot(
        jnp.where(came_from == column, 1.0, 0.0).astype(BF16), came
    )


def gather_back(own, came, core):
    row = lax.broadcasted_iota(jnp.int32, (HALF, ROWS), 0)
    position = lax.broadcasted_iota(jnp.int32, (HALF, ROWS), 1)
    local = slot_row(position - WIDE)
    own0 = jnp.where(position < GPAD, position, -1)
    own1 = jnp.where(
        (position >= SPLIT) & (position < GPAD), position - SPLIT, local + GPAD
    )
    own_to = own0 * (1 - core) + own1 * core
    came_row = lax.broadcasted_iota(jnp.int32, (HALF, MOVED), 0)
    came_position = lax.broadcasted_iota(jnp.int32, (HALF, MOVED), 1)
    came0 = jnp.where(came_position < SPLIT, came_position + GPAD, -1)
    came1 = slot_row(came_position) + REST
    came_to = came0 * (1 - core) + came1 * core
    return (
        dot(jnp.where(own_to == row, 1.0, 0.0).astype(BF16), own)
        + dot(jnp.where(came_to == came_row, 1.0, 0.0).astype(BF16), came)
    ).astype(BF16)


def head_lanes():
    lane = lax.broadcasted_iota(jnp.int32, (1, 2 * HD), 1)
    left = jnp.where(lane < HD, 1.0, 0.0)
    return (left.astype(BF16), (1.0 - left).astype(BF16)), (
        (left * SCALE).astype(BF16),
        ((1.0 - left) * SCALE).astype(BF16),
    )


def pair(at, block):
    return slice(block * D + 2 * HD * at, block * D + 2 * HD * (at + 1))


def windows(lens_ref, core):
    column = lax.broadcasted_iota(jnp.int32, (WIDE, WIDE), 1)
    plan = [(slice(0, WIDE), column < lens_ref[core])]
    for at in range(LOCALS // 2):
        row = lax.broadcasted_iota(jnp.int32, (2 * SLOT, 2 * SLOT), 0)
        column = lax.broadcasted_iota(jnp.int32, (2 * SLOT, 2 * SLOT), 1)
        first = lens_ref[2 + LOCALS * core + 2 * at]
        second = lens_ref[3 + LOCALS * core + 2 * at]
        allowed = ((row < SLOT) & (column < first)) | (
            (row >= SLOT) & (column >= SLOT) & (column < SLOT + second)
        )
        begin = WIDE + 2 * SLOT * at
        plan.append((slice(begin, begin + 2 * SLOT), allowed))
    return plan


def attend(lens_ref, core, joint_ref, merged_ref, log_ref):
    plain, scaled = head_lanes()
    lane = lax.broadcasted_iota(jnp.int32, (1, 128), 1)
    for rows, allowed in windows(lens_ref, core):
        count = rows.stop - rows.start
        logs = jnp.zeros((count, 128), F32)
        for at in range(HEADS // 2):
            queries = joint_ref[rows, pair(at, 0)]
            keys = joint_ref[rows, pair(at, 1)]
            values = joint_ref[rows, pair(at, 2)]
            mixed = jnp.zeros((count, 2 * HD), F32)
            for side in range(2):
                scores = jnp.where(allowed, dot_nt(queries * scaled[side], keys), MASKED)
                row_max = jnp.max(scores, axis=-1, keepdims=True)
                exponent = jnp.exp(scores - row_max)
                totals = jnp.sum(exponent, axis=-1, keepdims=True)
                weights = (exponent * (1.0 / totals)).astype(BF16)
                mixed = mixed + dot(weights, values * plain[side])
                logs = jnp.where(lane == 2 * at + side, row_max + jnp.log(totals), logs)
            merged_ref[rows, pair(at, 0)] = mixed.astype(BF16)
        log_ref[rows, :] = logs


def attend_back(lens_ref, core, joint_ref, up_ref, log_ref, grad_ref):
    plain, scaled = head_lanes()
    for rows, allowed in windows(lens_ref, core):
        logs = log_ref[rows, :]
        for at in range(HEADS // 2):
            queries = joint_ref[rows, pair(at, 0)]
            keys = joint_ref[rows, pair(at, 1)]
            values = joint_ref[rows, pair(at, 2)]
            upstream = up_ref[rows, pair(at, 0)]
            grad_q = grad_k = grad_v = 0.0
            for side in range(2):
                scaled_queries = queries * scaled[side]
                own_up = upstream * plain[side]
                scores = jnp.where(allowed, dot_nt(scaled_queries, keys), MASKED)
                log_total = logs[:, 2 * at + side : 2 * at + side + 1]
                weights = jnp.exp(scores - log_total)
                grad_weights = dot_nt(own_up, values)
                weighted = weights * grad_weights
                row_dot = jnp.sum(weighted, axis=-1, keepdims=True)
                grad_scores = (weighted - weights * row_dot).astype(BF16)
                grad_v = grad_v + dot_tn(weights.astype(BF16), own_up)
                grad_k = grad_k + dot_tn(grad_scores, scaled_queries)
                grad_q = grad_q + dot(grad_scores, keys * scaled[side])
            grad_ref[rows, pair(at, 0)] = grad_q.astype(BF16)
            grad_ref[rows, pair(at, 1)] = grad_k.astype(BF16)
            grad_ref[rows, pair(at, 2)] = grad_v.astype(BF16)


class Copies:
    def __init__(self, sems):
        self.sems = sems
        self.started = 0

    def start(self, source, target):
        copy = pltpu.make_async_copy(source, target, self.sems.at[self.started])
        self.started += 1
        copy.start()
        return copy


def wait_all(copies):
    for copy in copies:
        copy.wait()


def columns_of(ref, at):
    return ref.at[:, BLOCK * at : BLOCK * (at + 1)]


def core_half(ref, core):
    width = ref.shape[1] // 2
    return ref.at[:, pl.ds(pl.multiple_of(core * width, 128), width)]


def moved_rows(ref, core):
    return ref.at[pl.ds(pl.multiple_of(WIDE * (1 - core), 16), MOVED), :]


def vector(ref, layer):
    return ref[layer : layer + 1, :]


XS = FF + 3 * D
LOW2, MERGED, LOW1 = 0, D, 2 * D
GS = FF // 2 + D // 2
JS = 3 * D // 2
SUMS = 32


def ahead_kernel(
    lens, tokens, came, cot, came_cot, gain1, shift1, query_b, value_b, out_b, gain2, shift2, up_b, down_b,
    qkv_w, out_w, up_w, down_w, *refs,
):
    count = len(AHEAD)
    outs, held = refs[:count], refs[count : 2 * count]
    out_of = dict(zip((name for name, *_ in AHEAD), outs))
    ref_of = dict(zip((name for name, *_ in AHEAD), held))
    slope_ref, middle_ref, grad_ref, other_ref, grad_up_ref, branch_ref, weights, weight_sems, out_sems = refs[
        2 * count :
    ]
    core = lax.axis_index("seq")
    loads = Copies(weight_sems)
    stores = Copies(out_sems)
    leaving = []

    def leave(name):
        leaving.append(stores.start(ref_of[name], out_of[name]))

    def load_columns(ref, layer, blocks, slot):
        return [loads.start(columns_of(ref.at[layer], at), weights.at[slot + at]) for at in range(blocks)]

    def load_rows(ref, layer, blocks, slot):
        return [
            loads.start(ref.at[layer, BLOCK * at : BLOCK * (at + 1), :], weights.at[slot + at])
            for at in range(blocks)
        ]

    qkv = load_columns(qkv_w, 0, 3, 0)
    out = load_rows(out_w, 0, 1, 3)
    ups = load_columns(up_w, 0, FFB, 4)
    downs = load_rows(down_w, 0, FFB, 8)
    next_qkv = load_columns(qkv_w, 1, 3, 12)
    next_out = load_rows(out_w, 1, 1, 15)

    hidden = spread(tokens[...], came[...], core)
    for layer in range(2):
        if layer == 0:
            low1_ref = ref_of["xs0"].at[:, FF + LOW1 : FF + LOW1 + D]
            low2_ref = ref_of["xs0"].at[:, FF + LOW2 : FF + LOW2 + D]
            merged_ref = ref_of["xs0"].at[:, FF + MERGED : FF + MERGED + D]
            active_ref = ref_of["xs0"].at[:, 0:FF]
            joint_ref, log_ref, mid_ref, gelu_slope_ref = (
                ref_of["joint0"], ref_of["log0"], ref_of["middle0"], ref_of["slope0"],
            )
            ref_of["hidden0"][...] = hidden.astype(BF16)
            leave("hidden0")
            slot = 0
        else:
            low1_ref = ref_of["xs1"].at[:, LOW1 : LOW1 + D]
            low2_ref = ref_of["xs1"].at[:, LOW2 : LOW2 + D]
            merged_ref = ref_of["xs1"].at[:, MERGED : MERGED + D]
            active_ref = ref_of["active1"]
            joint_ref, log_ref, mid_ref, gelu_slope_ref = ref_of["joint1"], ref_of["log1"], middle_ref, slope_ref
            ref_of["hidden1"][...] = hidden
            leave("hidden1")
            slot = 12
            qkv, out = next_qkv, next_out
            ups = load_columns(up_w, 1, FFB, 4)
            downs = load_rows(down_w, 1, FFB, 8)
        normed, _ = norm_parts(hidden)
        low1_ref[...] = (normed * vector(gain1, layer) + vector(shift1, layer)).astype(BF16)
        wait_all(qkv)
        for block, bias in enumerate((vector(query_b, layer), None, vector(value_b, layer))):
            joint = dot(low1_ref[...], weights[slot + block])
            if bias is not None:
                joint = joint + bias
            joint_ref[:, BLOCK * block : BLOCK * (block + 1)] = joint.astype(BF16)
        leave(f"joint{layer}")
        attend(lens, core, joint_ref, merged_ref, log_ref)
        leave(f"log{layer}")
        wait_all(out)
        middle = hidden + dot(merged_ref[...], weights[slot + 3]) + vector(out_b, layer)
        mid_ref[...] = middle
        if layer == 0:
            leave("middle0")
        normed, _ = norm_parts(middle)
        low2_ref[...] = (normed * vector(gain2, layer) + vector(shift2, layer)).astype(BF16)
        if layer == 1:
            leave("xs1")
        wait_all(ups)
        for block in range(FFB):
            columns = slice(BLOCK * block, BLOCK * (block + 1))
            up_values = dot(low2_ref[...], weights[4 + block]) + up_b[layer : layer + 1, columns]
            mass, bell = normal_parts(up_values)
            active_ref[:, columns] = (up_values * mass).astype(BF16)
            gelu_slope_ref[:, columns] = (mass + up_values * bell).astype(BF16)
        leave("active1" if layer == 1 else "xs0")
        if layer == 0:
            leave("slope0")
        wait_all(downs)
        hidden = mid_ref[...] + dot(active_ref[...], weights[8:12].reshape(FF, D)) + vector(down_b, layer)
    ref_of["result"][...] = hidden.astype(BF16)
    leave("result")
    leaving.append(stores.start(moved_rows(ref_of["result"], core), out_of["moved_result"]))
    grad_ref[...] = spread(cot[...], came_cot[...], core).astype(BF16)
    other_ref[...] = spread(came_cot[...], cot[...], 1 - core).astype(BF16)
    leaving.append(stores.start(core_half(grad_ref, core), out_of["grad_own1"]))
    leaving.append(stores.start(core_half(other_ref, core), out_of["grad_other1"]))
    mlp_back_part(
        core, grad_ref[...], grad_ref[...].astype(F32), slope_ref, middle_ref, vector(gain2, 1),
        [weights[8 + at] for at in range(FFB)], [weights[4 + at] for at in range(FFB)], weights[15],
        grad_up_ref, branch_ref, ref_of["mid1"], ref_of["grad_merged1"], ref_of["sums_b1"], out_of["own1"],
        out_of["sent1"], stores, leaving,
    )
    for name in ("mid1", "grad_merged1", "sums_b1"):
        leave(name)
    wait_all(leaving)


def mlp_back_part(
    core, grad, upstream, slope_ref, middle_ref, gain, downs, ups, out_weight, grad_up_ref, branch_ref, mid_ref,
    grad_merged_ref, sums_ref, own, sent, stores, leaving,
):
    sums_ref[3:4, :] = column_sum(grad)
    back = 0.0
    for block in range(FFB):
        columns = slice(BLOCK * block, BLOCK * (block + 1))
        grad_up = (dot_nt(grad, downs[block]) * slope_ref[:, columns].astype(F32)).astype(BF16)
        grad_up_ref[:, columns] = grad_up
        sums_ref[4 + block : 5 + block, :] = column_sum(grad_up)
        back = back + dot_nt(grad_up, ups[block])
    leaving.append(stores.start(core_half(grad_up_ref, 1 - core), sent.at[:, 0 : FF // 2]))
    leaving.append(stores.start(core_half(grad_up_ref, core), own.at[:, 0 : FF // 2]))
    normed, inverse = norm_parts(middle_ref[...])
    sums_ref[1:2, :] = column_sum(back * normed)
    sums_ref[2:3, :] = column_sum(back)
    grad_mid = norm_back(back, normed, inverse, gain) + upstream
    mid_ref[...] = grad_mid
    branch = grad_mid.astype(BF16)
    branch_ref[...] = branch
    leaving.append(stores.start(core_half(branch_ref, 1 - core), sent.at[:, FF // 2 : GS]))
    leaving.append(stores.start(core_half(branch_ref, core), own.at[:, FF // 2 : GS]))
    sums_ref[0:1, :] = column_sum(branch)
    grad_merged_ref[...] = dot_nt(branch, out_weight).astype(BF16)


def attention_back_part(
    layer, lens, core, coming, qkv, held, gain1, weights, grad_joint_ref, sums_ref, sums_at, own, sent, stores, leaving
):
    joint_ref, up_ref, log_ref, hidden_ref, mid_ref = held
    wait_all(coming[:3])
    attend_back(lens, core, joint_ref, up_ref, log_ref, grad_joint_ref)
    leaving.append(stores.start(core_half(grad_joint_ref, 1 - core), sent.at[0:ROWS, 0:JS]))
    leaving.append(stores.start(core_half(grad_joint_ref, core), own.at[0:ROWS, 0:JS]))
    sums_ref[sums_at : sums_at + 1, :] = column_sum(grad_joint_ref[:, 0:D])
    sums_ref[sums_at + 1 : sums_at + 2, :] = column_sum(grad_joint_ref[:, 2 * D : 3 * D])
    wait_all(qkv)
    grad_first = 0.0
    for block in range(3):
        grad_first = grad_first + dot_nt(
            grad_joint_ref[:, BLOCK * block : BLOCK * (block + 1)], weights[block]
        )
    wait_all(coming[3:])
    normed, inverse = norm_parts(hidden_ref[...].astype(F32))
    sums_ref[sums_at + 2 : sums_at + 3, :] = column_sum(grad_first * normed)
    sums_ref[sums_at + 3 : sums_at + 4, :] = column_sum(grad_first)
    return norm_back(grad_first, normed, inverse, vector(gain1, layer)) + mid_ref[...]


def back1_kernel(
    lens, gain1, gain2, qkv_w, out_w, up_w, down_w, joint, grad_merged, log, hidden, mid, slope, middle,
    own_j, sent_j, own_g, sent_g, mid_out, grad_merged_out, sums_a_out, sums_b_out,
    joint_ref, up_ref, log_ref, hidden_ref, mid_ref, slope_ref, middle_ref, grad_joint_ref, sums_a_ref, grad_ref,
    upstream_ref, grad_up_ref, mid0_ref, branch_ref, grad_merged_ref, sums_b_ref, weights, load_sems, out_sems,
):
    core = lax.axis_index("seq")
    loads = Copies(load_sems)
    stores = Copies(out_sems)
    held = (joint_ref, up_ref, log_ref, hidden_ref, mid_ref)
    coming = [
        loads.start(source, target) for source, target in ((joint, joint_ref), (grad_merged, up_ref), (log, log_ref))
    ]
    qkv = [loads.start(columns_of(qkv_w.at[1], at), weights.at[at]) for at in range(3)]
    coming += [loads.start(hidden, hidden_ref), loads.start(mid, mid_ref)]
    later = [
        loads.start(down_w.at[0, BLOCK * at : BLOCK * (at + 1), :], weights.at[3 + at]) for at in range(FFB)
    ]
    later += [loads.start(slope, slope_ref)]
    later += [loads.start(columns_of(up_w.at[0], at), weights.at[3 + FFB + at]) for at in range(FFB)]
    later += [loads.start(middle, middle_ref), loads.start(out_w.at[0], weights.at[3 + 2 * FFB])]
    leaving = []
    sums_a_ref[...] = jnp.zeros_like(sums_a_ref)
    upstream = attention_back_part(
        1, lens, core, coming, qkv, held, gain1, weights, grad_joint_ref, sums_a_ref, 0, own_j, sent_j, stores, leaving
    )
    upstream_ref[...] = upstream
    grad = upstream.astype(BF16)
    grad_ref[...] = grad
    leaving.append(stores.start(core_half(grad_ref, 1 - core), sent_j.at[:, JS : JS + D // 2]))
    leaving.append(stores.start(core_half(grad_ref, core), own_j.at[:, JS : JS + D // 2]))
    leaving.append(stores.start(sums_a_ref, sums_a_out))
    wait_all(later)
    mlp_back_part(
        core, grad_ref[...], upstream_ref[...], slope_ref, middle_ref, vector(gain2, 0),
        [weights[3 + at] for at in range(FFB)], [weights[3 + FFB + at] for at in range(FFB)], weights[3 + 2 * FFB],
        grad_up_ref, branch_ref, mid0_ref, grad_merged_ref, sums_b_ref, own_g, sent_g, stores, leaving,
    )
    for source, target in ((mid0_ref, mid_out), (grad_merged_ref, grad_merged_out), (sums_b_ref, sums_b_out)):
        leaving.append(stores.start(source, target))
    wait_all(leaving)


def back0_kernel(
    lens, gain1, sums_b0, sums_a1, sums_b1, qkv_w, joint, grad_merged, log, hidden, mid,
    own_j, sent_j, tokens_out, moved_out,
    joint_ref, up_ref, log_ref, hidden_ref, mid_ref, grad_joint_ref, sums_ref, low_sums_ref, out_ref, weights,
    load_sems, out_sems,
):
    core = lax.axis_index("seq")
    loads = Copies(load_sems)
    stores = Copies(out_sems)
    held = (joint_ref, up_ref, log_ref, hidden_ref, mid_ref)
    sources = (joint, grad_merged, log, hidden, mid)
    coming = [loads.start(source, target) for source, target in zip(sources[:3], held[:3])]
    qkv = [loads.start(columns_of(qkv_w.at[0], at), weights.at[at]) for at in range(3)]
    coming += [loads.start(source, target) for source, target in zip(sources[3:], held[3:])]
    leaving = []
    sums_ref[...] = jnp.zeros_like(sums_ref)
    grad_in = attention_back_part(
        0, lens, core, coming, qkv, held, gain1, weights, grad_joint_ref, sums_ref, 0, own_j, sent_j, stores, leaving
    )
    sums_ref[4:8, :] = sums_b0[0:4, :]
    sums_ref[8:12, :] = sums_a1[0:4, :]
    sums_ref[12:16, :] = sums_b1[0:4, :]
    sums_ref[16:20, :] = sums_b0[4:8, :]
    sums_ref[20:24, :] = sums_b1[4:8, :]
    low_sums_ref[...] = sums_ref[...].astype(BF16)
    for target in (own_j, sent_j):
        leaving.append(stores.start(low_sums_ref, target.at[ROWS : ROWS + SUMS, 0:D]))
    out_ref[...] = grad_in.astype(BF16)
    leaving.append(stores.start(out_ref, tokens_out))
    leaving.append(stores.start(moved_rows(out_ref, core), moved_out))
    wait_all(leaving)


def part_order(parts, core_orders):
    bits = parts.bit_length() - 1

    def part_at(position, place, core):
        moved = [0, 0]
        for side in range(2):
            for hop, bit in enumerate(core_orders[side]):
                moved[side] |= ((position >> (bits - 1 - hop)) & 1) << bit
        return place ^ (moved[0] * (1 - core) + moved[1] * core)

    return part_at


def weight_kernel(parts, core_orders, products, with_sums, *refs):
    sources, refs = refs[: 4 * len(products)], refs[4 * len(products) :]
    kept, sent, *refs = refs
    inputs, refs = refs[: 2 * len(products)], refs[2 * len(products) :]
    if with_sums:
        own_sums, other_sums, *refs = refs
    stage, load_sems, out_sems = refs
    core = lax.axis_index("seq")
    place = lax.axis_index("dp")
    loads = Copies(load_sems)
    stores = Copies(out_sems)
    first, second = slice(0, ROWS), slice(ROWS, 2 * ROWS)
    rows = stage.shape[1]
    coming = []
    for at, (x_from, x_count, g_from, g_count) in enumerate(products):
        own_x, other_x, own_g, other_g = sources[4 * at : 4 * at + 4]
        x_ref, g_ref = inputs[2 * at : 2 * at + 2]
        columns = slice(g_from, g_from + g_count)
        group = [
            loads.start(own_g.at[0:ROWS, columns], g_ref.at[first, :]),
            loads.start(other_g.at[0:ROWS, columns], g_ref.at[second, :]),
        ]
        for block in range(x_count // BLOCK):
            columns = slice(x_from + BLOCK * block, x_from + BLOCK * (block + 1))
            place_at = slice(BLOCK * block, BLOCK * (block + 1))
            group.append(loads.start(own_x.at[:, columns], x_ref.at[first, place_at]))
            group.append(loads.start(other_x.at[:, columns], x_ref.at[second, place_at]))
        coming.append(group)
    done = 0
    if with_sums:
        below = slice(ROWS, ROWS + SUMS)
        wait_all(
            [
                loads.start(sources[2].at[below, 0:D], own_sums),
                loads.start(sources[3].at[below, 0:D], other_sums),
            ]
        )
        width = D // parts
        sums = (own_sums[...].astype(F32) + other_sums[...].astype(F32)).astype(BF16)
        begin = sum(g_count for _, _, _, g_count in products)
        for part in range(parts):
            stage[part, 0:16, begin : begin + width] = sums[0:16, width * part : width * (part + 1)]
            wide = FF // parts
            for layer in range(2):
                row = 16 + 4 * layer + part * wide // D
                for side in range(2):
                    lanes = part * wide % D + side * wide // 2
                    stage[part, 16 + 2 * layer + side : 17 + 2 * layer + side, begin : begin + wide // 2] = sums[
                        row : row + 1, lanes : lanes + wide // 2
                    ]
    for at, (x_from, x_count, g_from, g_count) in enumerate(products):
        x_ref, g_ref = inputs[2 * at : 2 * at + 2]
        wait_all(coming[at][:2])
        for block in range(x_count // BLOCK):
            wait_all(coming[at][2 + 2 * block : 4 + 2 * block])
            total = dot_tn(x_ref[:, BLOCK * block : BLOCK * (block + 1)], g_ref[...]).astype(BF16)
            share = x_count // parts
            count = BLOCK // share
            total = total.reshape(count, share // rows, rows, g_count)
            for piece in range(share // rows):
                begin = done + g_count * piece
                stage[count * block : count * (block + 1), :, begin : begin + g_count] = total[:, piece]
        done += g_count * (x_count // parts // rows)
    part_at = part_order(parts, core_orders)
    leaving = []
    half = parts // 2
    for position in list(range(half, parts)) + list(range(half)):
        target = sent if position >= half else kept
        leaving.append(
            stores.start(stage.at[part_at(position, place, core)], target.at[position % half])
        )
    wait_all(leaving)


def plain_weight_kernel(own_x, other_x, own_g, other_g, out):
    total = dot_tn(own_x[...], own_g[...]) + dot_tn(other_x[...], other_g[...])
    out[...] = total.astype(BF16)


def add_kernel(*refs):
    total = 0.0
    for ref in refs[:-1]:
        total = total + ref[...].astype(F32)
    refs[-1][...] = total.astype(refs[-1].dtype)


def finish_kernel(layers, splits, parts, terms, outs):
    for layer, columns in enumerate(layers):
        total = 0.0
        for ref, first in terms[layer]:
            total = total + ref[0, :, first : first + columns].astype(F32)
        rows = total.shape[0]
        for out, (begin, count) in zip(outs, splits):
            for piece in range(out.shape[1] // rows):
                at = begin + count * piece
                out[layer, rows * piece : rows * (piece + 1), :] = total[:, at : at + count]
        if parts is not None and layer == 0:
            sums = total[0:SUMS, columns - 128 : columns]
            width = D // parts
            for to in range(2):
                for out, row in zip(outs[len(splits) :], (0, 1, 4, 2, 3, 5, 6, 7)):
                    row += 8 * to
                    out[to : to + 1, :] = sums[row : row + 1, 0:width]
                half_wide = FF // parts // 2
                for side in range(2):
                    row = 16 + 2 * to + side
                    outs[-1][to : to + 1, half_wide * side : half_wide * (side + 1)] = sums[
                        row : row + 1, 0:half_wide
                    ]


def assemble_kernel(result, came_result, tokens, came_tokens, result_out, tokens_out):
    core = lax.axis_index("seq")
    result_out[...] = gather_back(result[...], came_result[...], core)
    tokens_out[...] = gather_back(tokens[...], came_tokens[...], core)


ANY = pl.BlockSpec(memory_space=pl.ANY)
def shaped(*dims, dtype=BF16):
    return jax.ShapeDtypeStruct(dims, dtype)


def held(*dims, dtype=BF16):
    return pltpu.VMEM(dims, dtype)


def sems(count):
    return pltpu.SemaphoreType.DMA((count,))


def whole(shape):
    return pl.BlockSpec(shape, lambda: (0,) * len(shape))


EXPECTED_US = {
    "ahead": 33.0, "down1": 6.4, "up1": 6.6, "qkv1": 5.0, "down0": 6.4, "up0": 6.6, "qkv0": 5.0, "back1": 20.0,
    "back0": 13.6, "assemble": 3.3,
}


def expected(name):
    time = EXPECTED_US.get(name, 2.0)
    return pl.CostEstimate(flops=int(time * 1.15e9), bytes_accessed=int(time * 3.69e6), transcendentals=0)


def call(kernel, name, operands, outs, scratch, lens=None, after=(), carry=(), out_specs=None):
    first = [] if lens is None else [lens]
    first_specs = [] if lens is None else [pl.BlockSpec(memory_space=pltpu.SMEM)]
    skip = len(first) + len(after) + len(carry)
    inputs = skip + len(operands)

    def body(*refs):
        kernel(
            *refs[: len(first)], *refs[skip:inputs], *refs[inputs : inputs + len(outs)],
            *refs[inputs + len(outs) + len(carry) :],
        )

    return pl.pallas_call(
        body,
        in_specs=first_specs
        + [ANY] * (len(after) + len(carry))
        + [whole(array.shape) if near else ANY for array, near in operands],
        out_specs=(out_specs or [ANY] * len(outs)) + [ANY] * len(carry),
        out_shape=list(outs) + [shaped(*array.shape, dtype=array.dtype) for array in carry],
        input_output_aliases={len(first) + len(after) + at: len(outs) + at for at in range(len(carry))},
        scratch_shapes=list(scratch),
        compiler_params=pltpu.CompilerParams(vmem_limit_bytes=VMEM_LIMIT),
        cost_estimate=expected(name),
        name=name,
    )(*first, *after, *carry, *(array for array, _ in operands))


def near(*arrays):
    return [(array, True) for array in arrays]


def far(*arrays):
    return [(array, False) for array in arrays]


AHEAD = (
    ("hidden0", ROWS, D, BF16), ("xs0", ROWS, XS, BF16), ("joint0", ROWS, 3 * D, BF16), ("log0", ROWS, 128, F32),
    ("middle0", ROWS, D, F32), ("slope0", ROWS, FF, BF16), ("hidden1", ROWS, D, F32), ("xs1", ROWS, 3 * D, BF16),
    ("joint1", ROWS, 3 * D, BF16), ("log1", ROWS, 128, F32), ("active1", ROWS, FF, BF16), ("result", ROWS, D, BF16),
    ("moved_result", MOVED, D, BF16),
    ("grad_own1", ROWS, D // 2, BF16), ("grad_other1", ROWS, D // 2, BF16), ("own1", ROWS, GS, BF16),
    ("sent1", ROWS, GS, BF16), ("mid1", ROWS, D, F32), ("grad_merged1", ROWS, D, BF16), ("sums_b1", 8, D, F32),
)


def ahead(lens, tokens, came, cot, came_cot, vectors, matrices):
    direct = ("moved_result", "grad_own1", "grad_other1", "own1", "sent1")
    outs = call(
        ahead_kernel, "ahead", near(tokens, came, cot, came_cot, *vectors) + far(*matrices),
        [shaped(r, c, dtype=t) for _, r, c, t in AHEAD],
        [held(8, 128) if name in direct else held(r, c, dtype=t) for name, r, c, t in AHEAD]
        + [held(ROWS, FF), held(ROWS, D, dtype=F32), held(ROWS, D), held(ROWS, D), held(ROWS, FF), held(ROWS, D),
           held(16, D, BLOCK), sems(24), sems(24)],
        lens=lens,
    )
    return {name: out for (name, *_), out in zip(AHEAD, outs)}


def back1(lens, operands, gain1, gain2, matrices, after=()):
    sums = shaped(8, D, dtype=F32)
    return call(
        back1_kernel, "back1", near(gain1, gain2) + far(*matrices, *operands),
        [shaped(ROWS, JS + D // 2), shaped(ROWS, JS + D // 2), shaped(ROWS, GS), shaped(ROWS, GS),
         shaped(ROWS, D, dtype=F32), shaped(ROWS, D), sums, sums],
        [held(ROWS, 3 * D), held(ROWS, D), held(ROWS, 128, dtype=F32), held(ROWS, D, dtype=F32),
         held(ROWS, D, dtype=F32), held(ROWS, FF), held(ROWS, D, dtype=F32), held(ROWS, 3 * D),
         held(8, D, dtype=F32), held(ROWS, D), held(ROWS, D, dtype=F32), held(ROWS, FF), held(ROWS, D, dtype=F32),
         held(ROWS, D), held(ROWS, D), held(8, D, dtype=F32),
         held(4 + 2 * FFB, D, BLOCK), sems(11 + 2 * FFB), sems(12)],
        lens=lens, after=after,
    )


def back0(lens, operands, gain1, sums, qkv_w, after=()):
    return call(
        back0_kernel, "back0", near(gain1, *sums) + far(qkv_w, *operands),
        [shaped(ROWS + SUMS, JS), shaped(ROWS + SUMS, JS), shaped(ROWS, D), shaped(MOVED, D)],
        [held(ROWS, 3 * D), held(ROWS, D), held(ROWS, 128, dtype=F32), held(ROWS, D), held(ROWS, D, dtype=F32),
         held(ROWS, 3 * D), held(SUMS, D, dtype=F32), held(SUMS, D), held(ROWS, D), held(3, D, BLOCK), sems(8),
         sems(6)],
        lens=lens, after=after,
    )


def add(sums, begin, count, name, after=(), carry=()):
    arrays = []
    for _, terms in sums:
        for array, _ in terms:
            if not any(array is seen for seen in arrays):
                arrays.append(array)
    index = {id(array): at for at, array in enumerate(arrays)}
    share = arrays[0].shape[1]
    total = sum(columns for columns, _ in sums)
    skip = len(after) + len(carry)
    pieces = min(count, 2)
    size = count // pieces

    def body(*refs):
        out = refs[skip + len(arrays)]
        done = 0
        for columns, terms in sums:
            value = 0.0
            for array, first in terms:
                value = value + refs[skip + index[id(array)]][:, :, first : first + columns].astype(F32)
            out[:, :, done : done + columns] = value.astype(BF16)
            done += columns

    return pl.pallas_call(
        body,
        grid=(pieces,),
        in_specs=[ANY] * skip
        + [
            pl.BlockSpec((size, share, array.shape[2]), lambda step: (begin // size + step, 0, 0))
            for array in arrays
        ],
        out_specs=[pl.BlockSpec((size, share, total), lambda step: (step, 0, 0))] + [ANY] * len(carry),
        out_shape=[shaped(count, share, total)]
        + [shaped(*array.shape, dtype=array.dtype) for array in carry],
        input_output_aliases={len(after) + at: 1 + at for at in range(len(carry))},
        compiler_params=pltpu.CompilerParams(vmem_limit_bytes=VMEM_LIMIT),
        cost_estimate=expected(name),
        name=name,
    )(*after, *carry, *arrays)


def swap(array):
    return lax.ppermute(array, "seq", [(0, 1), (1, 0)])


EVEN = ((0, 2, 1, 3), (1, 2, 0, 3))
LATE = ((0, 1, 2, 3), (1, 0, 2, 3))


class Halving:
    def __init__(self, name, kept, orders):
        self.name, self.orders = name, orders
        self.hop = 0
        self.columns = kept.shape[2]
        self.terms = [(kept, 0)]


def send(halvings, sent):
    hop, orders = halvings[0].hop, halvings[0].orders
    pairs = []
    for place in range(lax.axis_size("dp")):
        for core in range(2):
            other = place ^ (1 << orders[core][hop])
            pairs.append((2 * place + core, 2 * other + core))
    came = lax.ppermute(sent, ("dp", "seq"), pairs)
    first = 0
    for halving in halvings:
        halving.terms.append((came, first))
        halving.hop += 1
        first += halving.columns
    return came


def weight_gradient(name, operands, products, orders, with_sums, after=(), carry=()):
    parts = lax.axis_size("dp")
    columns = sum(g_count * (x_count // D) for _, x_count, _, g_count in products) + (128 if with_sums else 0)
    share = D // parts
    scratch = []
    copies = 2
    for _, x_count, _, g_count in products:
        scratch += [held(2 * ROWS, x_count), held(2 * ROWS, g_count)]
        copies += 2 + 2 * (x_count // BLOCK)
    if with_sums:
        scratch += [held(SUMS, D), held(SUMS, D)]
    return call(
        lambda *refs: weight_kernel(parts, orders, products, with_sums, *refs), name, far(*operands),
        [shaped(parts // 2, share, columns)] * 2,
        scratch + [held(parts, share, columns), sems(copies), sems(parts)],
        after=after, carry=carry,
    )


def finish(name, halvings, splits, parts=None, after=()):
    arrays = []
    for halving in halvings:
        for array, _ in halving.terms:
            if not any(array is seen for seen in arrays):
                arrays.append(array)
    index = {id(array): at for at, array in enumerate(arrays)}
    outs = [shaped(2, rows, count, dtype=F32) for _, count, rows in splits]
    if parts is not None:
        outs += [shaped(2, D // parts, dtype=F32)] * 8 + [shaped(2, FF // parts, dtype=F32)]

    def body(*refs):
        refs = refs[len(after) :]
        terms = [
            [(refs[index[id(array)]], first) for array, first in halving.terms] for halving in halvings
        ]
        finish_kernel(
            [halving.columns for halving in halvings], [split[:2] for split in splits], parts, terms,
            refs[len(arrays) :],
        )

    return pl.pallas_call(
        body,
        grid=(1,),
        in_specs=[ANY] * len(after)
        + [pl.BlockSpec((1,) + array.shape[1:], lambda step: (0, 0, 0)) for array in arrays],
        out_specs=[
            pl.BlockSpec(out.shape, lambda step, rank=len(out.shape): (0,) * rank) for out in outs
        ],
        out_shape=outs,
        compiler_params=pltpu.CompilerParams(vmem_limit_bytes=VMEM_LIMIT),
        cost_estimate=expected(name),
        name=name,
    )(*after, *arrays)


def plain_weight_gradient(name, own_x, other_x, own_g, other_g):
    rows, columns = own_x.shape[1], own_g.shape[1]
    x_spec = pl.BlockSpec((ROWS, BLOCK), lambda step: (0, step))
    g_spec = pl.BlockSpec((ROWS, columns), lambda step: (0, 0))
    return pl.pallas_call(
        plain_weight_kernel,
        grid=(rows // BLOCK,),
        in_specs=[x_spec, x_spec, g_spec, g_spec],
        out_specs=pl.BlockSpec((BLOCK, columns), lambda step: (step, 0)),
        out_shape=shaped(rows, columns),
        compiler_params=pltpu.CompilerParams(vmem_limit_bytes=VMEM_LIMIT),
        name=name,
    )(own_x, other_x, own_g, other_g)


def plain_halving(total, bit_order):
    parts = lax.axis_size("dp")
    place = lax.axis_index("dp")
    bits = parts.bit_length() - 1
    total = total.reshape((2,) * bits + (total.shape[0] // parts, total.shape[1]))
    left = list(range(bits))[::-1]
    terms = [total]
    for bit in bit_order:
        axis = left.index(bit)
        left.remove(bit)
        mine = (place >> bit) & 1
        sent = sum(lax.dynamic_index_in_dim(t, 1 - mine, axis, keepdims=False).astype(F32) for t in terms)
        terms = [lax.dynamic_index_in_dim(t, mine, axis, keepdims=False) for t in terms]
        terms.append(
            lax.ppermute(sent.astype(BF16), "dp", [(i, i ^ (1 << bit)) for i in range(parts)])
        )
    return sum(t.astype(F32) for t in terms)


def sum_everywhere(array):
    total = array + swap(array)
    parts = lax.axis_size("dp")
    for bit in range(parts.bit_length() - 1):
        total = total + lax.ppermute(total, "dp", [(i, i ^ (1 << bit)) for i in range(parts)])
    return total


def shards(
    tokens, crop_len, qkv_weight, query_bias, value_bias, out_weight, out_bias, first_gain, first_shift,
    second_gain, second_shift, up_weight, up_bias, down_weight, down_bias, cotangent,
):
    parts = lax.axis_size("dp")
    lens = crop_len.reshape(-1)
    core = lax.axis_index("seq")
    tiled = parts == 16
    matrices = (out_weight, up_weight, down_weight)
    came_tokens = swap(tokens)
    came_cot = swap(cotangent)
    kept = ahead(
        lens, tokens, came_tokens, cotangent, came_cot,
        (first_gain, first_shift, query_bias, value_bias, out_bias, second_gain, second_shift, up_bias, down_bias),
        (qkv_weight,) + matrices,
    )
    reductions = {}

    def product(name, operands, products, after=(), carry=(), with_sums=False, orders=EVEN):
        if not tiled:
            totals = []
            for at, (x_from, x_count, g_from, g_count) in enumerate(products):
                own_x, other_x, own_g, other_g = operands[4 * at : 4 * at + 4]
                x_at, g_at = slice(x_from, x_from + x_count), slice(g_from, g_from + g_count)
                total = plain_weight_gradient(
                    name, own_x[:, x_at], other_x[:, x_at], own_g[:ROWS, g_at], other_g[:ROWS, g_at]
                )
                totals.append(plain_halving(total, range(parts.bit_length() - 1)))
            reductions[name] = totals
            return (total, *carry)
        here, gone, *carried = weight_gradient(name, operands, products, orders, with_sums, after, carry)
        reductions[name] = Halving(name, here, orders)
        send([reductions[name]], gone)
        return (gone, *carried)

    def step(names, after=(), carry=()):
        if not tiled:
            return (*(after or (tokens,))[:1], *carry)
        group = [reductions[name] for name in names.split()]
        hop = group[0].hop
        count = parts >> (hop + 1)
        sums = [(halving.columns, halving.terms) for halving in group]
        sent, *carried = add(sums, count, count, "_".join(names.split()) + f"_hop{hop}", after, carry)
        send(group, sent)
        return (sent, *carried)

    def arrived(name):
        return (reductions[name].terms[-1][0],) if tiled else ()

    active1, xs1, xs0 = kept["active1"], kept["xs1"], kept["xs0"]
    own1, sent1 = kept["own1"], kept["sent1"]
    came_active1 = swap(active1)
    came_gs1 = swap(sent1)
    came_xs1 = swap(xs1)
    last, xs0 = product(
        "down1", (active1, came_active1, kept["grad_own1"], kept["grad_other1"]), ((0, FF, 0, D // 2),),
        carry=(xs0,),
    )
    came_xs0 = swap(xs0)
    (last,) = product(
        "up1", (xs1, came_xs1, own1, came_gs1, xs1, came_xs1, own1, came_gs1),
        ((LOW2, D, 0, FF // 2), (MERGED, D, FF // 2, D // 2)), after=(last,),
    )
    own_j1, sent_j1, own_g0, sent_g0, mid0, grad_merged0, sums_a1, sums_b0 = back1(
        lens,
        (kept["joint1"], kept["grad_merged1"], kept["log1"], kept["hidden1"], kept["mid1"], kept["slope0"],
         kept["middle0"]),
        first_gain, second_gain, (qkv_weight,) + matrices, after=(last,),
    )
    last, sent_j1, sent_g0 = step("down1", after=(own_j1,), carry=(sent_j1, sent_g0))
    came_j1 = swap(sent_j1)
    came_g0 = swap(sent_g0)
    (last,) = step("up1", after=(last,))
    (last,) = product("qkv1", (xs1, came_xs1, own_j1, came_j1), ((LOW1, D, 0, JS),), after=(last,))
    (last,) = product("down0", (xs0, came_xs0, own_j1, came_j1), ((0, FF, JS, D // 2),), after=(last,))
    (last,) = product(
        "up0", (xs0, came_xs0, own_g0, came_g0, xs0, came_xs0, own_g0, came_g0),
        ((FF + LOW2, D, 0, FF // 2), (FF + MERGED, D, FF // 2, D // 2)), after=(last,), orders=LATE,
    )
    (last,) = step("qkv1", after=(last,))
    own_j0, sent_j0, grad_tokens, moved_tokens = back0(
        lens, (kept["joint0"], grad_merged0, kept["log0"], kept["hidden0"], mid0), first_gain,
        (sums_b0, sums_a1, kept["sums_b1"]), qkv_weight, after=(last,),
    )
    last, sent_j0 = step("down1 up1", after=(own_j0,), carry=(sent_j0,))
    came_j0 = swap(sent_j0)
    (last,) = step("down0", after=(last,))
    (last,) = product(
        "qkv0", (xs0, came_xs0, own_j0, came_j0), ((FF + LOW1, D, 0, JS),), after=(last,), with_sums=True,
        orders=LATE,
    )
    (last,) = step("up0", after=(last,))
    last, moved_result, moved_tokens = step("down1 up1", after=(last,), carry=(kept["moved_result"], moved_tokens))
    (last,) = step("qkv1 down0", after=(last,))
    came_result = swap(moved_result)
    came_tokens = swap(moved_tokens)
    (last,) = step("qkv0", after=(last,))
    result, grad_tokens = call(
        assemble_kernel, "assemble", near(kept["result"], came_result, grad_tokens, came_tokens),
        [shaped(HALF, D)] * 2, [], out_specs=[whole((HALF, D))] * 2, after=(last,) + arrived("up1"),
    )
    (last,) = step("up0", after=(result,))
    (last,) = step("qkv1 down0", after=(last,))
    (last,) = step("qkv0", after=(last,))
    (last,) = step("up0", after=(last,))
    if tiled:
        (down_g,) = finish(
            "finish_down", (reductions["down0"], reductions["down1"]), ((0, D // 2, FF // parts),), after=(last,)
        )
        (last,) = step("qkv0", after=(down_g,))
        share = D // parts
        up_g, out_g = finish(
            "finish_up", (reductions["up0"], reductions["up1"]),
            ((0, FF // 2, share), (FF // 2, D // 2, share)), after=(last,),
        )
        qkv_g, *vectors = finish(
            "finish_qkv", (reductions["qkv0"], reductions["qkv1"]), ((0, JS, share),), parts, after=(up_g,)
        )
    else:
        down_g, up_g, out_g, qkv_g = (
            jnp.stack([reductions[name + "0"][at], reductions[name + "1"][at]])
            for name, at in (("down", 0), ("up", 0), ("up", 1), ("qkv", 0))
        )
        total = sum_everywhere(own_j0[ROWS:, :D].astype(F32))
        place = lax.axis_index("dp")
        width = D // parts
        narrow = lax.dynamic_slice(total[:16], (0, place * width), (16, width)).reshape(2, 8, width)
        vectors = [narrow[:, row] for row in (0, 1, 4, 2, 3, 5, 6, 7)]
        vectors.append(
            lax.dynamic_slice(total[16:24].reshape(2, FF), (0, place * (FF // parts)), (2, FF // parts))
        )
    query_b, value_b, out_b, gain1, shift1, gain2, shift2, down_b, up_b = vectors
    return (
        result, grad_tokens, qkv_g, query_b, value_b, out_g, out_b, gain1, shift1, gain2, shift2, up_g, up_b, down_g,
        down_b,
    )


def solution(mesh):
    rows = P(("dp", "seq"), None)
    matrix = P(None, "dp", "seq")
    narrow = P(None, "dp")
    return jax.shard_map(
        shards,
        mesh=mesh,
        in_specs=(rows, P("dp", None)) + (P(),) * 13 + (rows,),
        out_specs=(
            rows, rows, matrix, narrow, narrow, matrix, narrow, narrow, narrow, narrow, narrow, matrix, narrow,
            matrix, narrow,
        ),
        check_vma=False,
    )
```

```python
import jax
import jax.numpy as jnp
from jax import lax
from jax.experimental import pallas as pl
from jax.experimental.pallas import tpu as pltpu
from jax.sharding import PartitionSpec as P

HD = 64
GPAD = 198
LPAD = 38
HALF = 350
SPLIT = HALF - GPAD
REST = GPAD - SPLIT
WIDE = 208
SLOT = 40
LOCALS = 4
ROWS = WIDE + SLOT * LOCALS
MOVED = SLOT * LOCALS
HEADS = 12
D = 768
FF = 3072
BLOCK = 768
FFB = FF // BLOCK
X_BLOCK = 768
G_BLOCK = 1536

EPS = 1e-06
MASKED = -1e30
SCALE = HD ** (-0.5)
BF16 = jnp.bfloat16
F32 = jnp.float32

VMEM_LIMIT = 63 * 1024 * 1024


def dot(left, right):
    return jnp.dot(left, right, preferred_element_type=F32)


def dot_nt(left, right):
    return lax.dot_general(left, right, (((1,), (1,)), ((), ())), preferred_element_type=F32)


def dot_tn(left, right):
    return lax.dot_general(left, right, (((0,), (0,)), ((), ())), preferred_element_type=F32)


def normal_parts(values):
    mass = 0.5 + 0.5 * lax.erf(values * 0.7071067811865476)
    return mass, jnp.exp(-0.5 * values * values) * 0.3989422804014327


def norm_parts(hidden):
    row_mean = jnp.mean(hidden, axis=-1, keepdims=True)
    centered = hidden - row_mean
    inverse = lax.rsqrt(jnp.mean(centered * centered, axis=-1, keepdims=True) + EPS)
    return centered * inverse, inverse


def norm_back(upstream, normed, inverse, norm_gain):
    scaled = upstream * norm_gain
    centered = scaled - jnp.mean(scaled, axis=-1, keepdims=True)
    centered = centered - normed * jnp.mean(scaled * normed, axis=-1, keepdims=True)
    return centered * inverse


def column_sum(array):
    return jnp.sum(array.astype(F32), axis=0, keepdims=True)


def slot_row(position):
    crop = jnp.zeros_like(position)
    for at in range(1, LOCALS):
        crop = crop + (position >= SLOT * at).astype(jnp.int32)
    inner = position - SLOT * crop
    return jnp.where((position >= 0) & (inner < LPAD), LPAD * crop + inner, -4 * HALF)


def spread(own, came, core):
    position = lax.broadcasted_iota(jnp.int32, (ROWS, HALF), 0)
    column = lax.broadcasted_iota(jnp.int32, (ROWS, HALF), 1)
    local = slot_row(position - WIDE)
    own0 = jnp.where(position < GPAD, position, -1)
    came0 = local + REST
    own1 = jnp.where(
        (position >= SPLIT) & (position < GPAD), position - SPLIT, local + GPAD
    )
    came1 = jnp.where(position < SPLIT, position + GPAD, -1)
    own_from = own0 * (1 - core) + own1 * core
    came_from = came0 * (1 - core) + came1 * core
    return dot(jnp.where(own_from == column, 1.0, 0.0).astype(BF16), own) + dot(
        jnp.where(came_from == column, 1.0, 0.0).astype(BF16), came
    )


def gather_back(own, came, core):
    row = lax.broadcasted_iota(jnp.int32, (HALF, ROWS), 0)
    position = lax.broadcasted_iota(jnp.int32, (HALF, ROWS), 1)
    local = slot_row(position - WIDE)
    own0 = jnp.where(position < GPAD, position, -1)
    own1 = jnp.where(
        (position >= SPLIT) & (position < GPAD), position - SPLIT, local + GPAD
    )
    own_to = own0 * (1 - core) + own1 * core
    came_row = lax.broadcasted_iota(jnp.int32, (HALF, MOVED), 0)
    came_position = lax.broadcasted_iota(jnp.int32, (HALF, MOVED), 1)
    came0 = jnp.where(came_position < SPLIT, came_position + GPAD, -1)
    came1 = slot_row(came_position) + REST
    came_to = came0 * (1 - core) + came1 * core
    return (
        dot(jnp.where(own_to == row, 1.0, 0.0).astype(BF16), own)
        + dot(jnp.where(came_to == came_row, 1.0, 0.0).astype(BF16), came)
    ).astype(BF16)


def head_lanes():
    lane = lax.broadcasted_iota(jnp.int32, (1, 2 * HD), 1)
    left = jnp.where(lane < HD, 1.0, 0.0)
    return (left.astype(BF16), (1.0 - left).astype(BF16)), (
        (left * SCALE).astype(BF16),
        ((1.0 - left) * SCALE).astype(BF16),
    )


def both_heads(array, masks):
    return jnp.concatenate([array * masks[0], array * masks[1]], axis=0)


def own_lanes(stacked):
    rows = stacked.shape[0] // 2
    lane = lax.broadcasted_iota(jnp.int32, (rows, 2 * HD), 1)
    return jnp.where(lane < HD, stacked[:rows], stacked[rows:])


def pair(at, block):
    return slice(block * D + 2 * HD * at, block * D + 2 * HD * (at + 1))


def windows(lens_ref, core, pieces):
    column = lax.broadcasted_iota(jnp.int32, (2 * WIDE, WIDE), 1)
    plan = [(slice(0, WIDE), column < lens_ref[core])]
    count = LOCALS // pieces
    size = SLOT * count
    row = lax.broadcasted_iota(jnp.int32, (2 * size, size), 0)
    row = jnp.where(row >= size, row - size, row)
    column = lax.broadcasted_iota(jnp.int32, (2 * size, size), 1)
    for piece in range(pieces):
        allowed = None
        for at in range(count):
            begin = SLOT * at
            end = begin + lens_ref[2 + LOCALS * core + count * piece + at]
            mine = (row >= begin) & (row < begin + SLOT) & (column >= begin) & (column < end)
            allowed = mine if allowed is None else allowed | mine
        begin = WIDE + size * piece
        plan.append((slice(begin, begin + size), allowed))
    return plan


TOGETHER, PIECES = 3, 2
TOGETHER_BACK, PIECES_BACK = 3, 2


def attend(lens_ref, core, joint_ref, merged_ref, log_ref):
    _, scaled = head_lanes()
    lane = lax.broadcasted_iota(jnp.int32, (1, 128), 1)
    plan = windows(lens_ref, core, PIECES)
    logs = [jnp.zeros((rows.stop - rows.start, 128), F32) for rows, _ in plan]
    for begin in range(0, HEADS // 2, TOGETHER):
        chains = [(which, at) for at in range(begin, begin + TOGETHER) for which in range(len(plan))]
        scores = []
        for which, at in chains:
            rows, allowed = plan[which]
            queries = both_heads(joint_ref[rows, pair(at, 0)], scaled)
            scores.append(jnp.where(allowed, dot_nt(queries, joint_ref[rows, pair(at, 1)]), MASKED))
        row_max = [jnp.max(array, axis=-1, keepdims=True) for array in scores]
        exponent = [jnp.exp(array - top) for array, top in zip(scores, row_max)]
        totals = [jnp.sum(array, axis=-1, keepdims=True) for array in exponent]
        weights = [(array * (1.0 / total)).astype(BF16) for array, total in zip(exponent, totals)]
        for (which, at), array, top, total in zip(chains, weights, row_max, totals):
            rows, _ = plan[which]
            merged_ref[rows, pair(at, 0)] = own_lanes(dot(array, joint_ref[rows, pair(at, 2)])).astype(BF16)
            log_totals = top + jnp.log(total)
            count = rows.stop - rows.start
            for side in range(2):
                logs[which] = jnp.where(
                    lane == 2 * at + side, log_totals[count * side : count * (side + 1)], logs[which]
                )
    for (rows, _), array in zip(plan, logs):
        log_ref[rows, :] = array


def attend_back(lens_ref, core, joint_ref, up_ref, log_ref, grad_ref):
    plain, scaled = head_lanes()
    plan = windows(lens_ref, core, PIECES_BACK)
    for begin in range(0, HEADS // 2, TOGETHER_BACK):
        chains = [(which, at) for at in range(begin, begin + TOGETHER_BACK) for which in range(len(plan))]
        queries, upstream, weights, grad_weights = [], [], [], []
        for which, at in chains:
            rows, allowed = plan[which]
            queries.append(both_heads(joint_ref[rows, pair(at, 0)], scaled))
            upstream.append(both_heads(up_ref[rows, pair(at, 0)], plain))
            log_total = jnp.concatenate(
                [log_ref[rows, 2 * at + side : 2 * at + side + 1] for side in range(2)], axis=0
            )
            scores = jnp.where(allowed, dot_nt(queries[-1], joint_ref[rows, pair(at, 1)]), MASKED)
            weights.append(jnp.exp(scores - log_total))
            grad_weights.append(dot_nt(upstream[-1], joint_ref[rows, pair(at, 2)]))
        weighted = [one * two for one, two in zip(weights, grad_weights)]
        row_dot = [jnp.sum(array, axis=-1, keepdims=True) for array in weighted]
        grad_scores = [
            (array - one * dots).astype(BF16) for array, one, dots in zip(weighted, weights, row_dot)
        ]
        for (which, at), scores, one, query, up in zip(chains, grad_scores, weights, queries, upstream):
            rows, _ = plan[which]
            grad_ref[rows, pair(at, 2)] = dot_tn(one.astype(BF16), up).astype(BF16)
            grad_ref[rows, pair(at, 0)] = (
                own_lanes(dot(scores, joint_ref[rows, pair(at, 1)])) * SCALE
            ).astype(BF16)
            grad_ref[rows, pair(at, 1)] = dot_tn(scores, query).astype(BF16)


class Copies:
    def __init__(self, sems):
        self.sems = sems
        self.started = 0

    def start(self, source, target):
        copy = pltpu.make_async_copy(source, target, self.sems.at[self.started])
        self.started += 1
        copy.start()
        return copy


def wait_all(copies):
    for copy in copies:
        copy.wait()


def columns_of(ref, at):
    return ref.at[:, BLOCK * at : BLOCK * (at + 1)]


def core_half(ref, core):
    width = ref.shape[1] // 2
    return ref.at[:, pl.ds(pl.multiple_of(core * width, 128), width)]


def moved_rows(ref, core):
    return ref.at[pl.ds(pl.multiple_of(WIDE * (1 - core), 16), MOVED), :]


def vector(ref, layer):
    return ref[layer : layer + 1, :]


XS = FF + 3 * D
LOW2, MERGED, LOW1 = 0, D, 2 * D
GS = FF // 2 + D // 2
JS = 3 * D // 2
SUMS = 32


def ahead_kernel(
    lens, gain1, shift1, query_b, value_b, out_b, gain2, shift2, up_b, down_b,
    tokens_in, came_in, cot_in, came_cot_in, qkv_w, out_w, up_w, down_w, *refs,
):
    count = len(AHEAD)
    outs, held = refs[:count], refs[count : 2 * count]
    out_of = dict(zip((name for name, *_ in AHEAD), outs))
    ref_of = dict(zip((name for name, *_ in AHEAD), held))
    slope_ref, middle_ref, grad_ref, other_ref, grad_up_ref, branch_ref, *refs = refs[2 * count :]
    tokens, came, cot, came_cot, weights, weight_sems, out_sems = refs
    core = lax.axis_index("seq")
    loads = Copies(weight_sems)
    stores = Copies(out_sems)
    leaving = []

    def leave(name):
        leaving.append(stores.start(ref_of[name], out_of[name]))

    def load_columns(ref, layer, blocks, slot):
        return [loads.start(columns_of(ref.at[layer], at), weights.at[slot + at]) for at in range(blocks)]

    def load_rows(ref, layer, blocks, slot):
        return [
            loads.start(ref.at[layer, BLOCK * at : BLOCK * (at + 1), :], weights.at[slot + at])
            for at in range(blocks)
        ]

    rows_in = [loads.start(tokens_in, tokens), loads.start(came_in, came)]
    qkv = load_columns(qkv_w, 0, 3, 0)
    out = load_rows(out_w, 0, 1, 3)
    ups = load_columns(up_w, 0, FFB, 4)
    downs = load_rows(down_w, 0, FFB, 8)
    next_qkv = load_columns(qkv_w, 1, 3, 12)
    next_out = load_rows(out_w, 1, 1, 15)
    cots_in = [loads.start(cot_in, cot), loads.start(came_cot_in, came_cot)]

    wait_all(rows_in)
    hidden = spread(tokens[...], came[...], core)
    for layer in range(2):
        if layer == 0:
            low1_ref = ref_of["xs0"].at[:, FF + LOW1 : FF + LOW1 + D]
            low2_ref = ref_of["xs0"].at[:, FF + LOW2 : FF + LOW2 + D]
            merged_ref = ref_of["xs0"].at[:, FF + MERGED : FF + MERGED + D]
            active_ref = ref_of["xs0"].at[:, 0:FF]
            joint_ref, log_ref, mid_ref, gelu_slope_ref = (
                ref_of["joint0"], ref_of["log0"], ref_of["middle0"], ref_of["slope0"],
            )
            ref_of["hidden0"][...] = hidden.astype(BF16)
            leave("hidden0")
            slot = 0
        else:
            low1_ref = ref_of["xs1"].at[:, LOW1 : LOW1 + D]
            low2_ref = ref_of["xs1"].at[:, LOW2 : LOW2 + D]
            merged_ref = ref_of["xs1"].at[:, MERGED : MERGED + D]
            active_ref = ref_of["active1"]
            joint_ref, log_ref, mid_ref, gelu_slope_ref = ref_of["joint1"], ref_of["log1"], middle_ref, slope_ref
            ref_of["hidden1"][...] = hidden
            leave("hidden1")
            slot = 12
            qkv, out = next_qkv, next_out
            ups = load_columns(up_w, 1, FFB, 4)
            downs = load_rows(down_w, 1, FFB, 8)
        normed, _ = norm_parts(hidden)
        low1_ref[...] = (normed * vector(gain1, layer) + vector(shift1, layer)).astype(BF16)
        wait_all(qkv)
        for block, bias in enumerate((vector(query_b, layer), None, vector(value_b, layer))):
            joint = dot(low1_ref[...], weights[slot + block])
            if bias is not None:
                joint = joint + bias
            joint_ref[:, BLOCK * block : BLOCK * (block + 1)] = joint.astype(BF16)
        leave(f"joint{layer}")
        attend(lens, core, joint_ref, merged_ref, log_ref)
        leave(f"log{layer}")
        wait_all(out)
        middle = hidden + dot(merged_ref[...], weights[slot + 3]) + vector(out_b, layer)
        mid_ref[...] = middle
        if layer == 0:
            leave("middle0")
        normed, _ = norm_parts(middle)
        low2_ref[...] = (normed * vector(gain2, layer) + vector(shift2, layer)).astype(BF16)
        if layer == 1:
            leave("xs1")
        wait_all(ups)
        for block in range(FFB):
            columns = slice(BLOCK * block, BLOCK * (block + 1))
            up_values = dot(low2_ref[...], weights[4 + block]) + up_b[layer : layer + 1, columns]
            mass, bell = normal_parts(up_values)
            active_ref[:, columns] = (up_values * mass).astype(BF16)
            gelu_slope_ref[:, columns] = (mass + up_values * bell).astype(BF16)
        leave("active1" if layer == 1 else "xs0")
        if layer == 0:
            leave("slope0")
        wait_all(downs)
        hidden = mid_ref[...] + dot(active_ref[...], weights[8:12].reshape(FF, D)) + vector(down_b, layer)
    ref_of["result"][...] = hidden.astype(BF16)
    leave("result")
    leaving.append(stores.start(moved_rows(ref_of["result"], core), out_of["moved_result"]))
    wait_all(cots_in)
    grad_ref[...] = spread(cot[...], came_cot[...], core).astype(BF16)
    other_ref[...] = spread(came_cot[...], cot[...], 1 - core).astype(BF16)
    leaving.append(stores.start(core_half(grad_ref, core), out_of["grad_own1"]))
    leaving.append(stores.start(core_half(other_ref, core), out_of["grad_other1"]))
    mlp_back_part(
        core, grad_ref[...], grad_ref[...].astype(F32), slope_ref, middle_ref, vector(gain2, 1),
        [weights[8 + at] for at in range(FFB)], [weights[4 + at] for at in range(FFB)], weights[15],
        grad_up_ref, branch_ref, ref_of["mid1"], ref_of["grad_merged1"], ref_of["sums_b1"], out_of["own1"],
        out_of["sent1"], stores, leaving,
    )
    for name in ("mid1", "grad_merged1", "sums_b1"):
        leave(name)
    wait_all(leaving)


def mlp_back_part(
    core, grad, upstream, slope_ref, middle_ref, gain, downs, ups, out_weight, grad_up_ref, branch_ref, mid_ref,
    grad_merged_ref, sums_ref, own, sent, stores, leaving,
):
    sums_ref[3:4, :] = column_sum(grad)
    back = 0.0
    for block in range(FFB):
        columns = slice(BLOCK * block, BLOCK * (block + 1))
        grad_up = (dot_nt(grad, downs[block]) * slope_ref[:, columns].astype(F32)).astype(BF16)
        grad_up_ref[:, columns] = grad_up
        sums_ref[4 + block : 5 + block, :] = column_sum(grad_up)
        back = back + dot_nt(grad_up, ups[block])
    leaving.append(stores.start(core_half(grad_up_ref, 1 - core), sent.at[:, 0 : FF // 2]))
    leaving.append(stores.start(core_half(grad_up_ref, core), own.at[:, 0 : FF // 2]))
    normed, inverse = norm_parts(middle_ref[...])
    sums_ref[1:2, :] = column_sum(back * normed)
    sums_ref[2:3, :] = column_sum(back)
    grad_mid = norm_back(back, normed, inverse, gain) + upstream
    mid_ref[...] = grad_mid
    branch = grad_mid.astype(BF16)
    branch_ref[...] = branch
    leaving.append(stores.start(core_half(branch_ref, 1 - core), sent.at[:, FF // 2 : GS]))
    leaving.append(stores.start(core_half(branch_ref, core), own.at[:, FF // 2 : GS]))
    sums_ref[0:1, :] = column_sum(branch)
    grad_merged_ref[...] = dot_nt(branch, out_weight).astype(BF16)


def attention_back_part(
    layer, lens, core, coming, qkv, held, gain1, weights, grad_joint_ref, sums_ref, sums_at, own, sent, stores, leaving
):
    joint_ref, up_ref, log_ref, hidden_ref, mid_ref = held
    wait_all(coming[:3])
    attend_back(lens, core, joint_ref, up_ref, log_ref, grad_joint_ref)
    leaving.append(stores.start(core_half(grad_joint_ref, 1 - core), sent.at[0:ROWS, 0:JS]))
    leaving.append(stores.start(core_half(grad_joint_ref, core), own.at[0:ROWS, 0:JS]))
    sums_ref[sums_at : sums_at + 1, :] = column_sum(grad_joint_ref[:, 0:D])
    sums_ref[sums_at + 1 : sums_at + 2, :] = column_sum(grad_joint_ref[:, 2 * D : 3 * D])
    wait_all(qkv)
    grad_first = 0.0
    for block in range(3):
        grad_first = grad_first + dot_nt(
            grad_joint_ref[:, BLOCK * block : BLOCK * (block + 1)], weights[block]
        )
    wait_all(coming[3:])
    normed, inverse = norm_parts(hidden_ref[...].astype(F32))
    sums_ref[sums_at + 2 : sums_at + 3, :] = column_sum(grad_first * normed)
    sums_ref[sums_at + 3 : sums_at + 4, :] = column_sum(grad_first)
    return norm_back(grad_first, normed, inverse, vector(gain1, layer)) + mid_ref[...]


def back1_kernel(
    lens, gain1, gain2, qkv_w, out_w, up_w, down_w, joint, grad_merged, log, hidden, mid, slope, middle,
    own_j, sent_j, own_g, sent_g, mid_out, grad_merged_out, sums_a_out, sums_b_out,
    joint_ref, up_ref, log_ref, hidden_ref, mid_ref, slope_ref, middle_ref, grad_joint_ref, sums_a_ref, grad_ref,
    upstream_ref, grad_up_ref, mid0_ref, branch_ref, grad_merged_ref, sums_b_ref, weights, load_sems, out_sems,
):
    core = lax.axis_index("seq")
    loads = Copies(load_sems)
    stores = Copies(out_sems)
    held = (joint_ref, up_ref, log_ref, hidden_ref, mid_ref)
    coming = [
        loads.start(source, target) for source, target in ((joint, joint_ref), (grad_merged, up_ref), (log, log_ref))
    ]
    qkv = [loads.start(columns_of(qkv_w.at[1], at), weights.at[at]) for at in range(3)]
    coming += [loads.start(hidden, hidden_ref), loads.start(mid, mid_ref)]
    later = [
        loads.start(down_w.at[0, BLOCK * at : BLOCK * (at + 1), :], weights.at[3 + at]) for at in range(FFB)
    ]
    later += [loads.start(slope, slope_ref)]
    later += [loads.start(columns_of(up_w.at[0], at), weights.at[3 + FFB + at]) for at in range(FFB)]
    later += [loads.start(middle, middle_ref), loads.start(out_w.at[0], weights.at[3 + 2 * FFB])]
    leaving = []
    sums_a_ref[...] = jnp.zeros_like(sums_a_ref)
    upstream = attention_back_part(
        1, lens, core, coming, qkv, held, gain1, weights, grad_joint_ref, sums_a_ref, 0, own_j, sent_j, stores, leaving
    )
    upstream_ref[...] = upstream
    grad = upstream.astype(BF16)
    grad_ref[...] = grad
    leaving.append(stores.start(core_half(grad_ref, 1 - core), sent_j.at[:, JS : JS + D // 2]))
    leaving.append(stores.start(core_half(grad_ref, core), own_j.at[:, JS : JS + D // 2]))
    leaving.append(stores.start(sums_a_ref, sums_a_out))
    wait_all(later)
    mlp_back_part(
        core, grad_ref[...], upstream_ref[...], slope_ref, middle_ref, vector(gain2, 0),
        [weights[3 + at] for at in range(FFB)], [weights[3 + FFB + at] for at in range(FFB)], weights[3 + 2 * FFB],
        grad_up_ref, branch_ref, mid0_ref, grad_merged_ref, sums_b_ref, own_g, sent_g, stores, leaving,
    )
    for source, target in ((mid0_ref, mid_out), (grad_merged_ref, grad_merged_out), (sums_b_ref, sums_b_out)):
        leaving.append(stores.start(source, target))
    wait_all(leaving)


def back0_kernel(
    lens, gain1, sums_b0, sums_a1, sums_b1, qkv_w, joint, grad_merged, log, hidden, mid,
    own_j, sent_j, tokens_out, moved_out,
    joint_ref, up_ref, log_ref, hidden_ref, mid_ref, grad_joint_ref, sums_ref, low_sums_ref, out_ref, weights,
    load_sems, out_sems,
):
    core = lax.axis_index("seq")
    loads = Copies(load_sems)
    stores = Copies(out_sems)
    held = (joint_ref, up_ref, log_ref, hidden_ref, mid_ref)
    sources = (joint, grad_merged, log, hidden, mid)
    coming = [loads.start(source, target) for source, target in zip(sources[:3], held[:3])]
    qkv = [loads.start(columns_of(qkv_w.at[0], at), weights.at[at]) for at in range(3)]
    coming += [loads.start(source, target) for source, target in zip(sources[3:], held[3:])]
    leaving = []
    sums_ref[...] = jnp.zeros_like(sums_ref)
    grad_in = attention_back_part(
        0, lens, core, coming, qkv, held, gain1, weights, grad_joint_ref, sums_ref, 0, own_j, sent_j, stores, leaving
    )
    sums_ref[4:8, :] = sums_b0[0:4, :]
    sums_ref[8:12, :] = sums_a1[0:4, :]
    sums_ref[12:16, :] = sums_b1[0:4, :]
    sums_ref[16:20, :] = sums_b0[4:8, :]
    sums_ref[20:24, :] = sums_b1[4:8, :]
    low_sums_ref[...] = sums_ref[...].astype(BF16)
    for target in (own_j, sent_j):
        leaving.append(stores.start(low_sums_ref, target.at[ROWS : ROWS + SUMS, 0:D]))
    out_ref[...] = grad_in.astype(BF16)
    leaving.append(stores.start(out_ref, tokens_out))
    leaving.append(stores.start(moved_rows(out_ref, core), moved_out))
    wait_all(leaving)


def hop_position(parts, core_orders, part, place, core):
    bits = parts.bit_length() - 1
    distance = part ^ place
    position = [0, 0]
    for side in range(2):
        for hop, bit in enumerate(core_orders[side]):
            position[side] |= ((distance >> bit) & 1) << (bits - 1 - hop)
    return position[0] * (1 - core) + position[1] * core


def g_blocks(count):
    return [(begin, min(G_BLOCK, count - begin)) for begin in range(0, count, G_BLOCK)]


def weight_kernel(parts, core_orders, products, with_sums, *refs):
    sources, refs = refs[: 4 * len(products)], refs[4 * len(products) :]
    kept, sent, *refs = refs
    inputs, refs = refs[: 2 * len(products)], refs[2 * len(products) :]
    if with_sums:
        own_sums, other_sums, *refs = refs
    stage, load_sems, out_sems = refs
    core = lax.axis_index("seq")
    place = lax.axis_index("dp")
    loads = Copies(load_sems)
    first, second = slice(0, ROWS), slice(ROWS, 2 * ROWS)
    rows = stage.shape[1]
    half = parts // 2
    coming = []
    for at, (x_from, x_count, g_from, g_count) in enumerate(products):
        own_x, other_x, own_g, other_g = sources[4 * at : 4 * at + 4]
        x_ref, g_ref = inputs[2 * at : 2 * at + 2]
        x_coming, g_coming = [], []

        def load_x(block):
            columns = slice(x_from + X_BLOCK * block, x_from + X_BLOCK * (block + 1))
            place_at = slice(X_BLOCK * block, X_BLOCK * (block + 1))
            x_coming.append(
                (
                    loads.start(own_x.at[:, columns], x_ref.at[first, place_at]),
                    loads.start(other_x.at[:, columns], x_ref.at[second, place_at]),
                )
            )

        load_x(0)
        for begin, width in g_blocks(g_count):
            columns = slice(g_from + begin, g_from + begin + width)
            place_at = slice(begin, begin + width)
            g_coming.append(
                (
                    loads.start(own_g.at[0:ROWS, columns], g_ref.at[first, place_at]),
                    loads.start(other_g.at[0:ROWS, columns], g_ref.at[second, place_at]),
                )
            )
        for block in range(1, x_count // X_BLOCK):
            load_x(block)
        coming.append((x_coming, g_coming))
    if with_sums:
        below = slice(ROWS, ROWS + SUMS)
        sums_coming = (
            loads.start(sources[2].at[below, 0:D], own_sums),
            loads.start(sources[3].at[below, 0:D], other_sums),
        )
    leaving = []

    def leave(part, begin, width):
        columns = slice(begin, begin + width)
        source = stage.at[part, :, columns]
        sem = out_sems.at[len(leaving)]
        position = hop_position(parts, core_orders, part, place, core)

        @pl.when(position >= half)
        def _():
            pltpu.make_async_copy(source, sent.at[position - half, :, columns], sem).start()

        @pl.when(position < half)
        def _():
            pltpu.make_async_copy(source, kept.at[position, :, columns], sem).start()

        leaving.append(pltpu.make_async_copy(source, kept.at[0, :, columns], sem))

    done = 0
    for at, (x_from, x_count, g_from, g_count) in enumerate(products):
        x_ref, g_ref = inputs[2 * at : 2 * at + 2]
        x_coming, g_coming = coming[at]
        share = x_count // parts
        pieces = share // rows
        count = X_BLOCK // share
        for block in range(x_count // X_BLOCK):
            wait_all(x_coming[block])
            for (first_g, width), arriving in zip(g_blocks(g_count), g_coming):
                if block == 0:
                    wait_all(arriving)
                total = dot_tn(
                    x_ref[:, X_BLOCK * block : X_BLOCK * (block + 1)], g_ref[:, first_g : first_g + width]
                ).astype(BF16)
                total = total.reshape(count, pieces, rows, width)
                for piece in range(pieces):
                    begin = done + g_count * piece + first_g
                    stage[count * block : count * (block + 1), :, begin : begin + width] = total[:, piece]
            for part in range(count * block, count * (block + 1)):
                leave(part, done, g_count * pieces)
        done += g_count * pieces
    if with_sums:
        wait_all(sums_coming)
        width = D // parts
        sums = (own_sums[...].astype(F32) + other_sums[...].astype(F32)).astype(BF16)
        begin = sum(g_count for _, _, _, g_count in products)
        for part in range(parts):
            stage[part, 0:16, begin : begin + width] = sums[0:16, width * part : width * (part + 1)]
            wide = FF // parts
            for layer in range(2):
                row = 16 + 4 * layer + part * wide // D
                for side in range(2):
                    lanes = part * wide % D + side * wide // 2
                    stage[part, 16 + 2 * layer + side : 17 + 2 * layer + side, begin : begin + wide // 2] = sums[
                        row : row + 1, lanes : lanes + wide // 2
                    ]
            leave(part, begin, 128)
    wait_all(leaving)


def plain_weight_kernel(own_x, other_x, own_g, other_g, out):
    total = dot_tn(own_x[...], own_g[...]) + dot_tn(other_x[...], other_g[...])
    out[...] = total.astype(BF16)


def add_kernel(*refs):
    total = 0.0
    for ref in refs[:-1]:
        total = total + ref[...].astype(F32)
    refs[-1][...] = total.astype(refs[-1].dtype)


def finish_kernel(layers, splits, parts, terms, outs):
    for layer, columns in enumerate(layers):
        total = 0.0
        for ref, first in terms[layer]:
            total = total + ref[0, :, first : first + columns].astype(F32)
        rows = total.shape[0]
        for out, (begin, count) in zip(outs, splits):
            for piece in range(out.shape[1] // rows):
                at = begin + count * piece
                out[layer, rows * piece : rows * (piece + 1), :] = total[:, at : at + count]
        if parts is not None and layer == 0:
            sums = total[0:SUMS, columns - 128 : columns]
            width = D // parts
            for to in range(2):
                for out, row in zip(outs[len(splits) :], (0, 1, 4, 2, 3, 5, 6, 7)):
                    row += 8 * to
                    out[to : to + 1, :] = sums[row : row + 1, 0:width]
                half_wide = FF // parts // 2
                for side in range(2):
                    row = 16 + 2 * to + side
                    outs[-1][to : to + 1, half_wide * side : half_wide * (side + 1)] = sums[
                        row : row + 1, 0:half_wide
                    ]


def assemble_kernel(result, came_result, tokens, came_tokens, result_out, tokens_out):
    core = lax.axis_index("seq")
    result_out[...] = gather_back(result[...], came_result[...], core)
    tokens_out[...] = gather_back(tokens[...], came_tokens[...], core)


ANY = pl.BlockSpec(memory_space=pl.ANY)
def shaped(*dims, dtype=BF16):
    return jax.ShapeDtypeStruct(dims, dtype)


def held(*dims, dtype=BF16):
    return pltpu.VMEM(dims, dtype)


def sems(count):
    return pltpu.SemaphoreType.DMA((count,))


def whole(shape):
    return pl.BlockSpec(shape, lambda: (0,) * len(shape))


EXPECTED_US = {
    "ahead": 33.0, "down1": 6.4, "up1": 6.6, "qkv1": 5.0, "down0": 6.4, "up0": 6.6, "qkv0": 0.05, "back1": 20.0,
    "back0": 13.6, "assemble": 3.3,
}


def expected(name):
    time = 4.0 * EXPECTED_US.get(name, 2.0)
    return pl.CostEstimate(flops=int(time * 1.15e9), bytes_accessed=int(time * 3.69e6), transcendentals=0)


def call(kernel, name, operands, outs, scratch, lens=None, after=(), carry=(), out_specs=None):
    first = [] if lens is None else [lens]
    first_specs = [] if lens is None else [pl.BlockSpec(memory_space=pltpu.SMEM)]
    skip = len(first) + len(after) + len(carry)
    inputs = skip + len(operands)

    def body(*refs):
        kernel(
            *refs[: len(first)], *refs[skip:inputs], *refs[inputs : inputs + len(outs)],
            *refs[inputs + len(outs) + len(carry) :],
        )

    return pl.pallas_call(
        body,
        in_specs=first_specs
        + [ANY] * (len(after) + len(carry))
        + [whole(array.shape) if near else ANY for array, near in operands],
        out_specs=(out_specs or [ANY] * len(outs)) + [ANY] * len(carry),
        out_shape=list(outs) + [shaped(*array.shape, dtype=array.dtype) for array in carry],
        input_output_aliases={len(first) + len(after) + at: len(outs) + at for at in range(len(carry))},
        scratch_shapes=list(scratch),
        compiler_params=pltpu.CompilerParams(vmem_limit_bytes=VMEM_LIMIT),
        cost_estimate=expected(name),
        name=name,
    )(*first, *after, *carry, *(array for array, _ in operands))


def near(*arrays):
    return [(array, True) for array in arrays]


def far(*arrays):
    return [(array, False) for array in arrays]


AHEAD = (
    ("hidden0", ROWS, D, BF16), ("xs0", ROWS, XS, BF16), ("joint0", ROWS, 3 * D, BF16), ("log0", ROWS, 128, F32),
    ("middle0", ROWS, D, F32), ("slope0", ROWS, FF, BF16), ("hidden1", ROWS, D, F32), ("xs1", ROWS, 3 * D, BF16),
    ("joint1", ROWS, 3 * D, BF16), ("log1", ROWS, 128, F32), ("active1", ROWS, FF, BF16), ("result", ROWS, D, BF16),
    ("moved_result", MOVED, D, BF16),
    ("grad_own1", ROWS, D // 2, BF16), ("grad_other1", ROWS, D // 2, BF16), ("own1", ROWS, GS, BF16),
    ("sent1", ROWS, GS, BF16), ("mid1", ROWS, D, F32), ("grad_merged1", ROWS, D, BF16), ("sums_b1", 8, D, F32),
)


def ahead(lens, tokens, came, cot, came_cot, vectors, matrices):
    direct = ("moved_result", "grad_own1", "grad_other1", "own1", "sent1")
    outs = call(
        ahead_kernel, "ahead", near(*vectors) + far(tokens, came, cot, came_cot, *matrices),
        [shaped(r, c, dtype=t) for _, r, c, t in AHEAD],
        [held(8, 128) if name in direct else held(r, c, dtype=t) for name, r, c, t in AHEAD]
        + [held(ROWS, FF), held(ROWS, D, dtype=F32), held(ROWS, D), held(ROWS, D), held(ROWS, FF), held(ROWS, D),
           held(HALF, D), held(HALF, D), held(HALF, D), held(HALF, D), held(16, D, BLOCK), sems(28), sems(24)],
        lens=lens,
    )
    return {name: out for (name, *_), out in zip(AHEAD, outs)}


def back1(lens, operands, gain1, gain2, matrices, after=()):
    sums = shaped(8, D, dtype=F32)
    return call(
        back1_kernel, "back1", near(gain1, gain2) + far(*matrices, *operands),
        [shaped(ROWS, JS + D // 2), shaped(ROWS, JS + D // 2), shaped(ROWS, GS), shaped(ROWS, GS),
         shaped(ROWS, D, dtype=F32), shaped(ROWS, D), sums, sums],
        [held(ROWS, 3 * D), held(ROWS, D), held(ROWS, 128, dtype=F32), held(ROWS, D, dtype=F32),
         held(ROWS, D, dtype=F32), held(ROWS, FF), held(ROWS, D, dtype=F32), held(ROWS, 3 * D),
         held(8, D, dtype=F32), held(ROWS, D), held(ROWS, D, dtype=F32), held(ROWS, FF), held(ROWS, D, dtype=F32),
         held(ROWS, D), held(ROWS, D), held(8, D, dtype=F32),
         held(4 + 2 * FFB, D, BLOCK), sems(11 + 2 * FFB), sems(12)],
        lens=lens, after=after,
    )


def back0(lens, operands, gain1, sums, qkv_w, after=()):
    return call(
        back0_kernel, "back0", near(gain1, *sums) + far(qkv_w, *operands),
        [shaped(ROWS + SUMS, JS), shaped(ROWS + SUMS, JS), shaped(ROWS, D), shaped(MOVED, D)],
        [held(ROWS, 3 * D), held(ROWS, D), held(ROWS, 128, dtype=F32), held(ROWS, D), held(ROWS, D, dtype=F32),
         held(ROWS, 3 * D), held(SUMS, D, dtype=F32), held(SUMS, D), held(ROWS, D), held(3, D, BLOCK), sems(8),
         sems(6)],
        lens=lens, after=after,
    )


def add(sums, begin, count, name, after=(), carry=()):
    arrays = []
    for _, terms in sums:
        for array, _ in terms:
            if not any(array is seen for seen in arrays):
                arrays.append(array)
    index = {id(array): at for at, array in enumerate(arrays)}
    share = arrays[0].shape[1]
    total = sum(columns for columns, _ in sums)
    skip = len(after) + len(carry)
    pieces = min(count, 2)
    size = count // pieces

    def body(*refs):
        out = refs[skip + len(arrays)]
        done = 0
        for columns, terms in sums:
            value = 0.0
            for array, first in terms:
                value = value + refs[skip + index[id(array)]][:, :, first : first + columns].astype(F32)
            out[:, :, done : done + columns] = value.astype(BF16)
            done += columns

    return pl.pallas_call(
        body,
        grid=(pieces,),
        in_specs=[ANY] * skip
        + [
            pl.BlockSpec((size, share, array.shape[2]), lambda step: (begin // size + step, 0, 0))
            for array in arrays
        ],
        out_specs=[pl.BlockSpec((size, share, total), lambda step: (step, 0, 0))] + [ANY] * len(carry),
        out_shape=[shaped(count, share, total)]
        + [shaped(*array.shape, dtype=array.dtype) for array in carry],
        input_output_aliases={len(after) + at: 1 + at for at in range(len(carry))},
        compiler_params=pltpu.CompilerParams(vmem_limit_bytes=VMEM_LIMIT),
        cost_estimate=expected(name),
        name=name,
    )(*after, *carry, *arrays)


def swap(array):
    return lax.ppermute(array, "seq", [(0, 1), (1, 0)])


EVEN = ((0, 2, 1, 3), (1, 2, 0, 3))
LATE = ((0, 1, 2, 3), (1, 0, 2, 3))


class Halving:
    def __init__(self, name, kept, orders):
        self.name, self.orders = name, orders
        self.hop = 0
        self.columns = kept.shape[2]
        self.terms = [(kept, 0)]


def send(halvings, sent):
    hop, orders = halvings[0].hop, halvings[0].orders
    pairs = []
    for place in range(lax.axis_size("dp")):
        for core in range(2):
            other = place ^ (1 << orders[core][hop])
            pairs.append((2 * place + core, 2 * other + core))
    came = lax.ppermute(sent, ("dp", "seq"), pairs)
    first = 0
    for halving in halvings:
        halving.terms.append((came, first))
        halving.hop += 1
        first += halving.columns
    return came


def weight_gradient(name, operands, products, orders, with_sums, after=(), carry=()):
    parts = lax.axis_size("dp")
    columns = sum(g_count * (x_count // D) for _, x_count, _, g_count in products) + (128 if with_sums else 0)
    share = D // parts
    scratch = []
    copies = 2
    for _, x_count, _, g_count in products:
        scratch += [held(2 * ROWS, x_count), held(2 * ROWS, g_count)]
        copies += 2 * len(g_blocks(g_count)) + 2 * (x_count // X_BLOCK)
    if with_sums:
        scratch += [held(SUMS, D), held(SUMS, D)]
    return call(
        lambda *refs: weight_kernel(parts, orders, products, with_sums, *refs), name, far(*operands),
        [shaped(parts // 2, share, columns)] * 2,
        scratch
        + [held(parts, share, columns), sems(copies), sems(parts * (len(products) + int(with_sums)))],
        after=after, carry=carry,
    )


def finish(name, halvings, splits, parts=None, after=()):
    arrays = []
    for halving in halvings:
        for array, _ in halving.terms:
            if not any(array is seen for seen in arrays):
                arrays.append(array)
    index = {id(array): at for at, array in enumerate(arrays)}
    outs = [shaped(2, rows, count, dtype=F32) for _, count, rows in splits]
    if parts is not None:
        outs += [shaped(2, D // parts, dtype=F32)] * 8 + [shaped(2, FF // parts, dtype=F32)]

    def body(*refs):
        refs = refs[len(after) :]
        terms = [
            [(refs[index[id(array)]], first) for array, first in halving.terms] for halving in halvings
        ]
        finish_kernel(
            [halving.columns for halving in halvings], [split[:2] for split in splits], parts, terms,
            refs[len(arrays) :],
        )

    return pl.pallas_call(
        body,
        grid=(1,),
        in_specs=[ANY] * len(after)
        + [pl.BlockSpec((1,) + array.shape[1:], lambda step: (0, 0, 0)) for array in arrays],
        out_specs=[
            pl.BlockSpec(out.shape, lambda step, rank=len(out.shape): (0,) * rank) for out in outs
        ],
        out_shape=outs,
        compiler_params=pltpu.CompilerParams(vmem_limit_bytes=VMEM_LIMIT),
        cost_estimate=expected(name),
        name=name,
    )(*after, *arrays)


def plain_weight_gradient(name, own_x, other_x, own_g, other_g):
    rows, columns = own_x.shape[1], own_g.shape[1]
    x_spec = pl.BlockSpec((ROWS, BLOCK), lambda step: (0, step))
    g_spec = pl.BlockSpec((ROWS, columns), lambda step: (0, 0))
    return pl.pallas_call(
        plain_weight_kernel,
        grid=(rows // BLOCK,),
        in_specs=[x_spec, x_spec, g_spec, g_spec],
        out_specs=pl.BlockSpec((BLOCK, columns), lambda step: (step, 0)),
        out_shape=shaped(rows, columns),
        compiler_params=pltpu.CompilerParams(vmem_limit_bytes=VMEM_LIMIT),
        name=name,
    )(own_x, other_x, own_g, other_g)


def plain_halving(total, bit_order):
    parts = lax.axis_size("dp")
    place = lax.axis_index("dp")
    bits = parts.bit_length() - 1
    total = total.reshape((2,) * bits + (total.shape[0] // parts, total.shape[1]))
    left = list(range(bits))[::-1]
    terms = [total]
    for bit in bit_order:
        axis = left.index(bit)
        left.remove(bit)
        mine = (place >> bit) & 1
        sent = sum(lax.dynamic_index_in_dim(t, 1 - mine, axis, keepdims=False).astype(F32) for t in terms)
        terms = [lax.dynamic_index_in_dim(t, mine, axis, keepdims=False) for t in terms]
        terms.append(
            lax.ppermute(sent.astype(BF16), "dp", [(i, i ^ (1 << bit)) for i in range(parts)])
        )
    return sum(t.astype(F32) for t in terms)


def sum_everywhere(array):
    total = array + swap(array)
    parts = lax.axis_size("dp")
    for bit in range(parts.bit_length() - 1):
        total = total + lax.ppermute(total, "dp", [(i, i ^ (1 << bit)) for i in range(parts)])
    return total


def shards(
    tokens, crop_len, qkv_weight, query_bias, value_bias, out_weight, out_bias, first_gain, first_shift,
    second_gain, second_shift, up_weight, up_bias, down_weight, down_bias, cotangent,
):
    parts = lax.axis_size("dp")
    lens = crop_len.reshape(-1)
    core = lax.axis_index("seq")
    tiled = parts == 16
    matrices = (out_weight, up_weight, down_weight)
    came_tokens = swap(tokens)
    came_cot = swap(cotangent)
    kept = ahead(
        lens, tokens, came_tokens, cotangent, came_cot,
        (first_gain, first_shift, query_bias, value_bias, out_bias, second_gain, second_shift, up_bias, down_bias),
        (qkv_weight,) + matrices,
    )
    reductions = {}

    def product(name, operands, products, after=(), carry=(), with_sums=False, orders=EVEN):
        if not tiled:
            totals = []
            for at, (x_from, x_count, g_from, g_count) in enumerate(products):
                own_x, other_x, own_g, other_g = operands[4 * at : 4 * at + 4]
                x_at, g_at = slice(x_from, x_from + x_count), slice(g_from, g_from + g_count)
                total = plain_weight_gradient(
                    name, own_x[:, x_at], other_x[:, x_at], own_g[:ROWS, g_at], other_g[:ROWS, g_at]
                )
                totals.append(plain_halving(total, range(parts.bit_length() - 1)))
            reductions[name] = totals
            return (total, *carry)
        here, gone, *carried = weight_gradient(name, operands, products, orders, with_sums, after, carry)
        reductions[name] = Halving(name, here, orders)
        send([reductions[name]], gone)
        return (gone, *carried)

    def step(names, after=(), carry=()):
        if not tiled:
            return (*(after or (tokens,))[:1], *carry)
        group = [reductions[name] for name in names.split()]
        hop = group[0].hop
        count = parts >> (hop + 1)
        sums = [(halving.columns, halving.terms) for halving in group]
        sent, *carried = add(sums, count, count, "_".join(names.split()) + f"_hop{hop}", after, carry)
        send(group, sent)
        return (sent, *carried)

    def arrived(name):
        return (reductions[name].terms[-1][0],) if tiled else ()

    active1, xs1, xs0 = kept["active1"], kept["xs1"], kept["xs0"]
    own1, sent1 = kept["own1"], kept["sent1"]
    came_active1 = swap(active1)
    came_gs1 = swap(sent1)
    came_xs1 = swap(xs1)
    last, xs0 = product(
        "down1", (active1, came_active1, kept["grad_own1"], kept["grad_other1"]), ((0, FF, 0, D // 2),),
        carry=(xs0,),
    )
    came_xs0 = swap(xs0)
    (last,) = product(
        "up1", (xs1, came_xs1, own1, came_gs1, xs1, came_xs1, own1, came_gs1),
        ((LOW2, D, 0, FF // 2), (MERGED, D, FF // 2, D // 2)), after=(last,),
    )
    own_j1, sent_j1, own_g0, sent_g0, mid0, grad_merged0, sums_a1, sums_b0 = back1(
        lens,
        (kept["joint1"], kept["grad_merged1"], kept["log1"], kept["hidden1"], kept["mid1"], kept["slope0"],
         kept["middle0"]),
        first_gain, second_gain, (qkv_weight,) + matrices, after=(last,),
    )
    last, sent_j1, sent_g0 = step("down1", after=(own_j1,), carry=(sent_j1, sent_g0))
    came_j1 = swap(sent_j1)
    came_g0 = swap(sent_g0)
    (last,) = product(
        "qkv1", (xs1, came_xs1, own_j1, came_j1), ((LOW1, D, 0, JS),), after=(last,) + arrived("up1")
    )
    (last,) = step("up1", after=(last,))
    (last,) = product("down0", (xs0, came_xs0, own_j1, came_j1), ((0, FF, JS, D // 2),), after=(last,))
    (last,) = product(
        "up0", (xs0, came_xs0, own_g0, came_g0, xs0, came_xs0, own_g0, came_g0),
        ((FF + LOW2, D, 0, FF // 2), (FF + MERGED, D, FF // 2, D // 2)), after=(last,), orders=EVEN,
    )
    (last,) = step("qkv1", after=(last,))
    own_j0, sent_j0, grad_tokens, moved_tokens = back0(
        lens, (kept["joint0"], grad_merged0, kept["log0"], kept["hidden0"], mid0), first_gain,
        (sums_b0, sums_a1, kept["sums_b1"]), qkv_weight, after=(last,),
    )
    last, sent_j0 = step("down1 up1", after=(own_j0,), carry=(sent_j0,))
    came_j0 = swap(sent_j0)
    (last,) = step("down0", after=(last,) + arrived("qkv1"))
    (last,) = product(
        "qkv0", (xs0, came_xs0, own_j0, came_j0), ((FF + LOW1, D, 0, JS),), after=(last,), with_sums=True, orders=LATE,
    )
    (last,) = step("up0", after=(last,))
    last, moved_result, moved_tokens = step("down1 up1", after=(last,), carry=(kept["moved_result"], moved_tokens))
    came_result = swap(moved_result)
    came_tokens = swap(moved_tokens)
    (last,) = step("qkv1 down0", after=(last,))
    (last,) = step("qkv0", after=(last, came_result, came_tokens))
    (last,) = step("qkv1 down0", after=(last,))
    (last,) = step("qkv0", after=(last,))
    (last,) = step("up0", after=(last,))
    result, grad_tokens = call(
        assemble_kernel, "assemble", near(kept["result"], came_result, grad_tokens, came_tokens),
        [shaped(HALF, D)] * 2, [], out_specs=[whole((HALF, D))] * 2, after=(last,),
    )
    (last,) = step("qkv0", after=(result,) + arrived("up1"))
    (last,) = step("up0", after=(last,))
    if tiled:
        share = D // parts
        (down_g,) = finish(
            "finish_down", (reductions["down0"], reductions["down1"]), ((0, D // 2, FF // parts),), after=(last,)
        )
        qkv_g, *vectors = finish(
            "finish_qkv", (reductions["qkv0"], reductions["qkv1"]), ((0, JS, share),), parts, after=(down_g,)
        )
        up_g, out_g = finish(
            "finish_up", (reductions["up0"], reductions["up1"]),
            ((0, FF // 2, share), (FF // 2, D // 2, share)), after=(qkv_g,),
        )
    else:
        down_g, up_g, out_g, qkv_g = (
            jnp.stack([reductions[name + "0"][at], reductions[name + "1"][at]])
            for name, at in (("down", 0), ("up", 0), ("up", 1), ("qkv", 0))
        )
        total = sum_everywhere(own_j0[ROWS:, :D].astype(F32))
        place = lax.axis_index("dp")
        width = D // parts
        narrow = lax.dynamic_slice(total[:16], (0, place * width), (16, width)).reshape(2, 8, width)
        vectors = [narrow[:, row] for row in (0, 1, 4, 2, 3, 5, 6, 7)]
        vectors.append(
            lax.dynamic_slice(total[16:24].reshape(2, FF), (0, place * (FF // parts)), (2, FF // parts))
        )
    query_b, value_b, out_b, gain1, shift1, gain2, shift2, down_b, up_b = vectors
    return (
        result, grad_tokens, qkv_g, query_b, value_b, out_g, out_b, gain1, shift1, gain2, shift2, up_g, up_b, down_g,
        down_b,
    )


def solution(mesh):
    rows = P(("dp", "seq"), None)
    matrix = P(None, "dp", "seq")
    narrow = P(None, "dp")
    return jax.shard_map(
        shards,
        mesh=mesh,
        in_specs=(rows, P("dp", None)) + (P(),) * 13 + (rows,),
        out_specs=(
            rows, rows, matrix, narrow, narrow, matrix, narrow, narrow, narrow, narrow, narrow, matrix, narrow,
            matrix, narrow,
        ),
        check_vma=False,
    )
```

```python
import jax
import jax.numpy as jnp
from jax import lax
from jax.experimental import pallas as pl
from jax.experimental.pallas import tpu as pltpu
from jax.sharding import PartitionSpec as P

HD = 64
GPAD = 198
LPAD = 38
HALF = 350
SPLIT = HALF - GPAD
REST = GPAD - SPLIT
WIDE = 208
SLOT = 40
LOCALS = 4
ROWS = WIDE + SLOT * LOCALS
MOVED = SLOT * LOCALS
HEADS = 12
D = 768
FF = 3072
BLOCK = 768
FFB = FF // BLOCK
X_BLOCK = 768
G_BLOCK = 1536

EPS = 1e-06
MASKED = -1e30
SCALE = HD ** (-0.5)
BF16 = jnp.bfloat16
F32 = jnp.float32

VMEM_LIMIT = 64 * 1024 * 1024 - 64 * 1024


def dot(left, right):
    return jnp.dot(left, right, preferred_element_type=F32)


def dot_nt(left, right):
    return lax.dot_general(left, right, (((1,), (1,)), ((), ())), preferred_element_type=F32)


def dot_tn(left, right):
    return lax.dot_general(left, right, (((0,), (0,)), ((), ())), preferred_element_type=F32)


def normal_parts(values):
    mass = 0.5 + 0.5 * lax.erf(values * 0.7071067811865476)
    return mass, jnp.exp(-0.5 * values * values) * 0.3989422804014327


def norm_parts(hidden):
    row_mean = jnp.mean(hidden, axis=-1, keepdims=True)
    centered = hidden - row_mean
    inverse = lax.rsqrt(jnp.mean(centered * centered, axis=-1, keepdims=True) + EPS)
    return centered * inverse, inverse


def norm_back(upstream, normed, inverse, norm_gain):
    scaled = upstream * norm_gain
    centered = scaled - jnp.mean(scaled, axis=-1, keepdims=True)
    centered = centered - normed * jnp.mean(scaled * normed, axis=-1, keepdims=True)
    return centered * inverse


def column_sum(array):
    return jnp.sum(array.astype(F32), axis=0, keepdims=True)


def slot_row(position):
    crop = jnp.zeros_like(position)
    for at in range(1, LOCALS):
        crop = crop + (position >= SLOT * at).astype(jnp.int32)
    inner = position - SLOT * crop
    return jnp.where((position >= 0) & (inner < LPAD), LPAD * crop + inner, -4 * HALF)


def spread(own, came, core):
    position = lax.broadcasted_iota(jnp.int32, (ROWS, HALF), 0)
    column = lax.broadcasted_iota(jnp.int32, (ROWS, HALF), 1)
    local = slot_row(position - WIDE)
    own0 = jnp.where(position < GPAD, position, -1)
    came0 = local + REST
    own1 = jnp.where(
        (position >= SPLIT) & (position < GPAD), position - SPLIT, local + GPAD
    )
    came1 = jnp.where(position < SPLIT, position + GPAD, -1)
    own_from = own0 * (1 - core) + own1 * core
    came_from = came0 * (1 - core) + came1 * core
    return dot(jnp.where(own_from == column, 1.0, 0.0).astype(BF16), own) + dot(
        jnp.where(came_from == column, 1.0, 0.0).astype(BF16), came
    )


def gather_back(own, came, core):
    row = lax.broadcasted_iota(jnp.int32, (HALF, ROWS), 0)
    position = lax.broadcasted_iota(jnp.int32, (HALF, ROWS), 1)
    local = slot_row(position - WIDE)
    own0 = jnp.where(position < GPAD, position, -1)
    own1 = jnp.where(
        (position >= SPLIT) & (position < GPAD), position - SPLIT, local + GPAD
    )
    own_to = own0 * (1 - core) + own1 * core
    came_row = lax.broadcasted_iota(jnp.int32, (HALF, MOVED), 0)
    came_position = lax.broadcasted_iota(jnp.int32, (HALF, MOVED), 1)
    came0 = jnp.where(came_position < SPLIT, came_position + GPAD, -1)
    came1 = slot_row(came_position) + REST
    came_to = came0 * (1 - core) + came1 * core
    return (
        dot(jnp.where(own_to == row, 1.0, 0.0).astype(BF16), own)
        + dot(jnp.where(came_to == came_row, 1.0, 0.0).astype(BF16), came)
    ).astype(BF16)


def head_lanes():
    lane = lax.broadcasted_iota(jnp.int32, (1, 2 * HD), 1)
    left = jnp.where(lane < HD, 1.0, 0.0)
    return (left.astype(BF16), (1.0 - left).astype(BF16)), (
        (left * SCALE).astype(BF16),
        ((1.0 - left) * SCALE).astype(BF16),
    )


def both_heads(array, masks):
    return jnp.concatenate([array * masks[0], array * masks[1]], axis=0)


def own_lanes(stacked):
    rows = stacked.shape[0] // 2
    lane = lax.broadcasted_iota(jnp.int32, (rows, 2 * HD), 1)
    return jnp.where(lane < HD, stacked[:rows], stacked[rows:])


def pair(at, block):
    return slice(block * D + 2 * HD * at, block * D + 2 * HD * (at + 1))


def windows(lens_ref, core, pieces):
    column = lax.broadcasted_iota(jnp.int32, (2 * WIDE, WIDE), 1)
    plan = [(slice(0, WIDE), column < lens_ref[core])]
    count = LOCALS // pieces
    size = SLOT * count
    row = lax.broadcasted_iota(jnp.int32, (2 * size, size), 0)
    row = jnp.where(row >= size, row - size, row)
    column = lax.broadcasted_iota(jnp.int32, (2 * size, size), 1)
    for piece in range(pieces):
        allowed = None
        for at in range(count):
            begin = SLOT * at
            end = begin + lens_ref[2 + LOCALS * core + count * piece + at]
            mine = (row >= begin) & (row < begin + SLOT) & (column >= begin) & (column < end)
            allowed = mine if allowed is None else allowed | mine
        begin = WIDE + size * piece
        plan.append((slice(begin, begin + size), allowed))
    return plan


TOGETHER, PIECES = 3, 2
TOGETHER_BACK, PIECES_BACK = 3, 2


def attend(lens_ref, core, joint_ref, merged_ref, log_ref):
    _, scaled = head_lanes()
    lane = lax.broadcasted_iota(jnp.int32, (1, 128), 1)
    plan = windows(lens_ref, core, PIECES)
    logs = [jnp.zeros((rows.stop - rows.start, 128), F32) for rows, _ in plan]
    for begin in range(0, HEADS // 2, TOGETHER):
        chains = [(which, at) for at in range(begin, begin + TOGETHER) for which in range(len(plan))]
        scores = []
        for which, at in chains:
            rows, allowed = plan[which]
            queries = both_heads(joint_ref[rows, pair(at, 0)], scaled)
            scores.append(jnp.where(allowed, dot_nt(queries, joint_ref[rows, pair(at, 1)]), MASKED))
        row_max = [jnp.max(array, axis=-1, keepdims=True) for array in scores]
        exponent = [jnp.exp(array - top) for array, top in zip(scores, row_max)]
        totals = [jnp.sum(array, axis=-1, keepdims=True) for array in exponent]
        weights = [(array * (1.0 / total)).astype(BF16) for array, total in zip(exponent, totals)]
        for (which, at), array, top, total in zip(chains, weights, row_max, totals):
            rows, _ = plan[which]
            merged_ref[rows, pair(at, 0)] = own_lanes(dot(array, joint_ref[rows, pair(at, 2)])).astype(BF16)
            log_totals = top + jnp.log(total)
            count = rows.stop - rows.start
            for side in range(2):
                logs[which] = jnp.where(
                    lane == 2 * at + side, log_totals[count * side : count * (side + 1)], logs[which]
                )
    for (rows, _), array in zip(plan, logs):
        log_ref[rows, :] = array


def attend_back(lens_ref, core, joint_ref, up_ref, log_ref, grad_ref):
    plain, scaled = head_lanes()
    plan = windows(lens_ref, core, PIECES_BACK)
    for begin in range(0, HEADS // 2, TOGETHER_BACK):
        chains = [(which, at) for at in range(begin, begin + TOGETHER_BACK) for which in range(len(plan))]
        queries, upstream, weights, grad_weights = [], [], [], []
        for which, at in chains:
            rows, allowed = plan[which]
            queries.append(both_heads(joint_ref[rows, pair(at, 0)], scaled))
            upstream.append(both_heads(up_ref[rows, pair(at, 0)], plain))
            log_total = jnp.concatenate(
                [log_ref[rows, 2 * at + side : 2 * at + side + 1] for side in range(2)], axis=0
            )
            scores = jnp.where(allowed, dot_nt(queries[-1], joint_ref[rows, pair(at, 1)]), MASKED)
            weights.append(jnp.exp(scores - log_total))
            grad_weights.append(dot_nt(upstream[-1], joint_ref[rows, pair(at, 2)]))
        weighted = [one * two for one, two in zip(weights, grad_weights)]
        row_dot = [jnp.sum(array, axis=-1, keepdims=True) for array in weighted]
        grad_scores = [
            (array - one * dots).astype(BF16) for array, one, dots in zip(weighted, weights, row_dot)
        ]
        for (which, at), scores, one, query, up in zip(chains, grad_scores, weights, queries, upstream):
            rows, _ = plan[which]
            grad_ref[rows, pair(at, 2)] = dot_tn(one.astype(BF16), up).astype(BF16)
            grad_ref[rows, pair(at, 0)] = (
                own_lanes(dot(scores, joint_ref[rows, pair(at, 1)])) * SCALE
            ).astype(BF16)
            grad_ref[rows, pair(at, 1)] = dot_tn(scores, query).astype(BF16)


class Copies:
    def __init__(self, sems):
        self.sems = sems
        self.started = 0

    def start(self, source, target):
        copy = pltpu.make_async_copy(source, target, self.sems.at[self.started])
        self.started += 1
        copy.start()
        return copy


def wait_all(copies):
    for copy in copies:
        copy.wait()


def columns_of(ref, at):
    return ref.at[:, BLOCK * at : BLOCK * (at + 1)]


def core_half(ref, core):
    width = ref.shape[1] // 2
    return ref.at[:, pl.ds(pl.multiple_of(core * width, 128), width)]


def moved_rows(ref, core):
    return ref.at[pl.ds(pl.multiple_of(WIDE * (1 - core), 16), MOVED), :]


def vector(ref, layer):
    return ref[layer : layer + 1, :]


XS = FF + 3 * D
LOW2, MERGED, LOW1 = 0, D, 2 * D
GS = FF // 2 + D // 2
JS = 3 * D // 2
SUMS = 32


def ahead_kernel(
    lens, gain1, shift1, query_b, value_b, out_b, gain2, shift2, up_b, down_b,
    tokens_in, came_in, cot_in, came_cot_in, qkv_w, out_w, up_w, down_w, *refs,
):
    count = len(AHEAD)
    outs, held = refs[:count], refs[count : 2 * count]
    out_of = dict(zip((name for name, *_ in AHEAD), outs))
    ref_of = dict(zip((name for name, *_ in AHEAD), held))
    slope_ref, grad_ref, other_ref, grad_up_ref, branch_ref, *refs = refs[2 * count :]
    tokens, came, cot, came_cot, weights, weight_sems, out_sems = refs
    core = lax.axis_index("seq")
    loads = Copies(weight_sems)
    stores = Copies(out_sems)
    leaving = []

    def leave(name):
        leaving.append(stores.start(ref_of[name], out_of[name]))

    def load_columns(ref, layer, blocks, slot):
        return [loads.start(columns_of(ref.at[layer], at), weights.at[slot + at]) for at in range(blocks)]

    def load_rows(ref, layer, blocks, slot):
        return [
            loads.start(ref.at[layer, BLOCK * at : BLOCK * (at + 1), :], weights.at[slot + at])
            for at in range(blocks)
        ]

    rows_in = [loads.start(tokens_in, tokens), loads.start(came_in, came)]
    qkv = load_columns(qkv_w, 0, 3, 0)
    out = load_rows(out_w, 0, 1, 3)
    ups = load_columns(up_w, 0, FFB, 4)
    downs = load_rows(down_w, 0, FFB, 8)
    next_qkv = load_columns(qkv_w, 1, 3, 12)
    next_out = load_rows(out_w, 1, 1, 15)
    cots_in = [loads.start(cot_in, cot), loads.start(came_cot_in, came_cot)]

    wait_all(rows_in)
    hidden = spread(tokens[...], came[...], core)
    for layer in range(2):
        if layer == 0:
            low1_ref = ref_of["xs0"].at[:, FF + LOW1 : FF + LOW1 + D]
            low2_ref = ref_of["xs0"].at[:, FF + LOW2 : FF + LOW2 + D]
            merged_ref = ref_of["xs0"].at[:, FF + MERGED : FF + MERGED + D]
            active_ref = ref_of["xs0"].at[:, 0:FF]
            joint_ref, log_ref, mid_ref, gelu_slope_ref = (
                ref_of["joint0"], ref_of["log0"], ref_of["middle0"], ref_of["slope0"],
            )
            ref_of["hidden0"][...] = hidden.astype(BF16)
            leave("hidden0")
            slot = 0
        else:
            low1_ref = ref_of["xs1"].at[:, LOW1 : LOW1 + D]
            low2_ref = ref_of["xs1"].at[:, LOW2 : LOW2 + D]
            merged_ref = ref_of["xs1"].at[:, MERGED : MERGED + D]
            active_ref = ref_of["active1"]
            joint_ref, log_ref, mid_ref, gelu_slope_ref = ref_of["joint1"], ref_of["log1"], ref_of["middle1"], slope_ref
            ref_of["hidden1"][...] = hidden
            leave("hidden1")
            slot = 12
            qkv, out = next_qkv, next_out
            ups = load_columns(up_w, 1, FFB, 4)
            downs = load_rows(down_w, 1, FFB, 8)
        normed, _ = norm_parts(hidden)
        low1_ref[...] = (normed * vector(gain1, layer) + vector(shift1, layer)).astype(BF16)
        wait_all(qkv)
        for block, bias in enumerate((vector(query_b, layer), None, vector(value_b, layer))):
            joint = dot(low1_ref[...], weights[slot + block])
            if bias is not None:
                joint = joint + bias
            joint_ref[:, BLOCK * block : BLOCK * (block + 1)] = joint.astype(BF16)
        leave(f"joint{layer}")
        attend(lens, core, joint_ref, merged_ref, log_ref)
        leave(f"log{layer}")
        wait_all(out)
        middle = hidden + dot(merged_ref[...], weights[slot + 3]) + vector(out_b, layer)
        mid_ref[...] = middle
        leave(f"middle{layer}")
        if layer == 1:
            leaving.append(stores.start(moved_rows(mid_ref, core), out_of["moved_middle1"]))
        normed, _ = norm_parts(middle)
        low2_ref[...] = (normed * vector(gain2, layer) + vector(shift2, layer)).astype(BF16)
        if layer == 1:
            leave("xs1")
        wait_all(ups)
        for block in range(FFB):
            columns = slice(BLOCK * block, BLOCK * (block + 1))
            up_values = dot(low2_ref[...], weights[4 + block]) + up_b[layer : layer + 1, columns]
            mass, bell = normal_parts(up_values)
            active_ref[:, columns] = (up_values * mass).astype(BF16)
            gelu_slope_ref[:, columns] = (mass + up_values * bell).astype(BF16)
        leave("active1" if layer == 1 else "xs0")
        if layer == 0:
            leave("slope0")
        wait_all(downs)
        if layer == 0:
            hidden = mid_ref[...] + dot(active_ref[...], weights[8:12].reshape(FF, D)) + vector(down_b, layer)
    wait_all(cots_in)
    grad_ref[...] = spread(cot[...], came_cot[...], core).astype(BF16)
    other_ref[...] = spread(came_cot[...], cot[...], 1 - core).astype(BF16)
    leaving.append(stores.start(core_half(grad_ref, core), out_of["grad_own1"]))
    leaving.append(stores.start(core_half(other_ref, core), out_of["grad_other1"]))
    mlp_back_part(
        core, grad_ref[...], grad_ref[...].astype(F32), slope_ref, ref_of["middle1"], vector(gain2, 1),
        [weights[8 + at] for at in range(FFB)], [weights[4 + at] for at in range(FFB)], weights[15],
        grad_up_ref, branch_ref, ref_of["mid1"], ref_of["grad_merged1"], ref_of["sums_b1"], out_of["own1"],
        out_of["sent1"], stores, leaving,
    )
    for name in ("mid1", "grad_merged1", "sums_b1"):
        leave(name)
    wait_all(leaving)


def result_kernel(
    down_b, active, came_active, middle, came_middle, down_w, out,
    active_ref, came_active_ref, middle_ref, came_middle_ref, weights, load_sems,
):
    core = lax.axis_index("seq")
    loads = Copies(load_sems)
    coming = []
    for at in range(FFB):
        columns = slice(BLOCK * at, BLOCK * (at + 1))
        coming.append(
            (
                loads.start(down_w.at[1, columns, :], weights.at[columns, :]),
                loads.start(active.at[:, columns], active_ref.at[:, columns]),
                loads.start(moved_rows(came_active, 1 - core).at[:, columns], came_active_ref.at[:, columns]),
            )
        )
    rest = [loads.start(middle, middle_ref), loads.start(came_middle, came_middle_ref)]
    own = came = vector(down_b, 1)
    for at in range(FFB):
        columns = slice(BLOCK * at, BLOCK * (at + 1))
        wait_all(coming[at])
        own = own + dot(active_ref[:, columns], weights[columns, :])
        came = came + dot(came_active_ref[:, columns], weights[columns, :])
    wait_all(rest)
    own = (middle_ref[...] + own).astype(BF16)
    out[...] = gather_back(own, (came_middle_ref[...] + came).astype(BF16), core)


def mlp_back_part(
    core, grad, upstream, slope_ref, middle_ref, gain, downs, ups, out_weight, grad_up_ref, branch_ref, mid_ref,
    grad_merged_ref, sums_ref, own, sent, stores, leaving,
):
    sums_ref[3:4, :] = column_sum(grad)
    back = 0.0
    for block in range(FFB):
        columns = slice(BLOCK * block, BLOCK * (block + 1))
        grad_up = (dot_nt(grad, downs[block]) * slope_ref[:, columns].astype(F32)).astype(BF16)
        grad_up_ref[:, columns] = grad_up
        sums_ref[4 + block : 5 + block, :] = column_sum(grad_up)
        back = back + dot_nt(grad_up, ups[block])
    leaving.append(stores.start(core_half(grad_up_ref, 1 - core), sent.at[:, 0 : FF // 2]))
    leaving.append(stores.start(core_half(grad_up_ref, core), own.at[:, 0 : FF // 2]))
    normed, inverse = norm_parts(middle_ref[...])
    sums_ref[1:2, :] = column_sum(back * normed)
    sums_ref[2:3, :] = column_sum(back)
    grad_mid = norm_back(back, normed, inverse, gain) + upstream
    mid_ref[...] = grad_mid
    branch = grad_mid.astype(BF16)
    branch_ref[...] = branch
    leaving.append(stores.start(core_half(branch_ref, 1 - core), sent.at[:, FF // 2 : GS]))
    leaving.append(stores.start(core_half(branch_ref, core), own.at[:, FF // 2 : GS]))
    sums_ref[0:1, :] = column_sum(branch)
    grad_merged_ref[...] = dot_nt(branch, out_weight).astype(BF16)


def attention_back_part(
    layer, lens, core, coming, qkv, held, gain1, weights, grad_joint_ref, sums_ref, sums_at, own, sent, stores, leaving
):
    joint_ref, up_ref, log_ref, hidden_ref, mid_ref = held
    wait_all(coming[:3])
    attend_back(lens, core, joint_ref, up_ref, log_ref, grad_joint_ref)
    leaving.append(stores.start(core_half(grad_joint_ref, 1 - core), sent.at[0:ROWS, 0:JS]))
    leaving.append(stores.start(core_half(grad_joint_ref, core), own.at[0:ROWS, 0:JS]))
    sums_ref[sums_at : sums_at + 1, :] = column_sum(grad_joint_ref[:, 0:D])
    sums_ref[sums_at + 1 : sums_at + 2, :] = column_sum(grad_joint_ref[:, 2 * D : 3 * D])
    wait_all(qkv)
    grad_first = 0.0
    for block in range(3):
        grad_first = grad_first + dot_nt(
            grad_joint_ref[:, BLOCK * block : BLOCK * (block + 1)], weights[block]
        )
    wait_all(coming[3:])
    normed, inverse = norm_parts(hidden_ref[...].astype(F32))
    sums_ref[sums_at + 2 : sums_at + 3, :] = column_sum(grad_first * normed)
    sums_ref[sums_at + 3 : sums_at + 4, :] = column_sum(grad_first)
    return norm_back(grad_first, normed, inverse, vector(gain1, layer)) + mid_ref[...]


def back1_kernel(
    lens, gain1, gain2, qkv_w, out_w, up_w, down_w, joint, grad_merged, log, hidden, mid, slope, middle,
    own_j, sent_j, own_g, sent_g, mid_out, grad_merged_out, sums_a_out, sums_b_out,
    joint_ref, up_ref, log_ref, hidden_ref, mid_ref, slope_ref, middle_ref, grad_joint_ref, sums_a_ref, grad_ref,
    upstream_ref, grad_up_ref, mid0_ref, branch_ref, grad_merged_ref, sums_b_ref, weights, load_sems, out_sems,
):
    core = lax.axis_index("seq")
    loads = Copies(load_sems)
    stores = Copies(out_sems)
    held = (joint_ref, up_ref, log_ref, hidden_ref, mid_ref)
    coming = [
        loads.start(source, target) for source, target in ((joint, joint_ref), (grad_merged, up_ref), (log, log_ref))
    ]
    qkv = [loads.start(columns_of(qkv_w.at[1], at), weights.at[at]) for at in range(3)]
    coming += [loads.start(hidden, hidden_ref), loads.start(mid, mid_ref)]
    later = [
        loads.start(down_w.at[0, BLOCK * at : BLOCK * (at + 1), :], weights.at[3 + at]) for at in range(FFB)
    ]
    later += [loads.start(slope, slope_ref)]
    later += [loads.start(columns_of(up_w.at[0], at), weights.at[3 + FFB + at]) for at in range(FFB)]
    later += [loads.start(middle, middle_ref), loads.start(out_w.at[0], weights.at[3 + 2 * FFB])]
    leaving = []
    sums_a_ref[...] = jnp.zeros_like(sums_a_ref)
    upstream = attention_back_part(
        1, lens, core, coming, qkv, held, gain1, weights, grad_joint_ref, sums_a_ref, 0, own_j, sent_j, stores, leaving
    )
    upstream_ref[...] = upstream
    grad = upstream.astype(BF16)
    grad_ref[...] = grad
    leaving.append(stores.start(core_half(grad_ref, 1 - core), sent_j.at[:, JS : JS + D // 2]))
    leaving.append(stores.start(core_half(grad_ref, core), own_j.at[:, JS : JS + D // 2]))
    leaving.append(stores.start(sums_a_ref, sums_a_out))
    wait_all(later)
    mlp_back_part(
        core, grad_ref[...], upstream_ref[...], slope_ref, middle_ref, vector(gain2, 0),
        [weights[3 + at] for at in range(FFB)], [weights[3 + FFB + at] for at in range(FFB)], weights[3 + 2 * FFB],
        grad_up_ref, branch_ref, mid0_ref, grad_merged_ref, sums_b_ref, own_g, sent_g, stores, leaving,
    )
    for source, target in ((mid0_ref, mid_out), (grad_merged_ref, grad_merged_out), (sums_b_ref, sums_b_out)):
        leaving.append(stores.start(source, target))
    wait_all(leaving)


def back0_kernel(
    lens, gain1, sums_b0, sums_a1, sums_b1, qkv_w, joint, grad_merged, log, hidden, mid,
    own_j, sent_j, tokens_out, moved_out,
    joint_ref, up_ref, log_ref, hidden_ref, mid_ref, grad_joint_ref, sums_ref, low_sums_ref, out_ref, weights,
    load_sems, out_sems,
):
    core = lax.axis_index("seq")
    loads = Copies(load_sems)
    stores = Copies(out_sems)
    held = (joint_ref, up_ref, log_ref, hidden_ref, mid_ref)
    sources = (joint, grad_merged, log, hidden, mid)
    coming = [loads.start(source, target) for source, target in zip(sources[:3], held[:3])]
    qkv = [loads.start(columns_of(qkv_w.at[0], at), weights.at[at]) for at in range(3)]
    coming += [loads.start(source, target) for source, target in zip(sources[3:], held[3:])]
    leaving = []
    sums_ref[...] = jnp.zeros_like(sums_ref)
    grad_in = attention_back_part(
        0, lens, core, coming, qkv, held, gain1, weights, grad_joint_ref, sums_ref, 0, own_j, sent_j, stores, leaving
    )
    sums_ref[4:8, :] = sums_b0[0:4, :]
    sums_ref[8:12, :] = sums_a1[0:4, :]
    sums_ref[12:16, :] = sums_b1[0:4, :]
    sums_ref[16:20, :] = sums_b0[4:8, :]
    sums_ref[20:24, :] = sums_b1[4:8, :]
    low_sums_ref[...] = sums_ref[...].astype(BF16)
    for target in (own_j, sent_j):
        leaving.append(stores.start(low_sums_ref, target.at[ROWS : ROWS + SUMS, 0:D]))
    out_ref[...] = grad_in.astype(BF16)
    leaving.append(stores.start(out_ref, tokens_out))
    leaving.append(stores.start(moved_rows(out_ref, core), moved_out))
    wait_all(leaving)


def hop_position(parts, core_orders, part, place, core):
    bits = parts.bit_length() - 1
    distance = part ^ place
    position = [0, 0]
    for side in range(2):
        for hop, bit in enumerate(core_orders[side]):
            position[side] |= ((distance >> bit) & 1) << (bits - 1 - hop)
    return position[0] * (1 - core) + position[1] * core


def g_blocks(count):
    return [(begin, min(G_BLOCK, count - begin)) for begin in range(0, count, G_BLOCK)]


def weight_kernel(parts, core_orders, products, with_sums, *refs):
    sources, refs = refs[: 4 * len(products)], refs[4 * len(products) :]
    kept, sent, *refs = refs
    inputs, refs = refs[: 2 * len(products)], refs[2 * len(products) :]
    if with_sums:
        own_sums, other_sums, *refs = refs
    stage, load_sems, out_sems = refs
    core = lax.axis_index("seq")
    place = lax.axis_index("dp")
    loads = Copies(load_sems)
    first, second = slice(0, ROWS), slice(ROWS, 2 * ROWS)
    rows = stage.shape[1]
    half = parts // 2
    coming = []
    for at, (x_from, x_count, g_from, g_count) in enumerate(products):
        own_x, other_x, own_g, other_g = sources[4 * at : 4 * at + 4]
        x_ref, g_ref = inputs[2 * at : 2 * at + 2]
        x_coming, g_coming = [], []

        def load_x(block):
            columns = slice(x_from + X_BLOCK * block, x_from + X_BLOCK * (block + 1))
            place_at = slice(X_BLOCK * block, X_BLOCK * (block + 1))
            x_coming.append(
                (
                    loads.start(own_x.at[:, columns], x_ref.at[first, place_at]),
                    loads.start(other_x.at[:, columns], x_ref.at[second, place_at]),
                )
            )

        load_x(0)
        for begin, width in g_blocks(g_count):
            columns = slice(g_from + begin, g_from + begin + width)
            place_at = slice(begin, begin + width)
            g_coming.append(
                (
                    loads.start(own_g.at[0:ROWS, columns], g_ref.at[first, place_at]),
                    loads.start(other_g.at[0:ROWS, columns], g_ref.at[second, place_at]),
                )
            )
        for block in range(1, x_count // X_BLOCK):
            load_x(block)
        coming.append((x_coming, g_coming))
    if with_sums:
        below = slice(ROWS, ROWS + SUMS)
        sums_coming = (
            loads.start(sources[2].at[below, 0:D], own_sums),
            loads.start(sources[3].at[below, 0:D], other_sums),
        )
    leaving = []

    def leave(part, begin, width):
        columns = slice(begin, begin + width)
        source = stage.at[part, :, columns]
        sem = out_sems.at[len(leaving)]
        position = hop_position(parts, core_orders, part, place, core)

        @pl.when(position >= half)
        def _():
            pltpu.make_async_copy(source, sent.at[position - half, :, columns], sem).start()

        @pl.when(position < half)
        def _():
            pltpu.make_async_copy(source, kept.at[position, :, columns], sem).start()

        leaving.append(pltpu.make_async_copy(source, kept.at[0, :, columns], sem))

    done = 0
    for at, (x_from, x_count, g_from, g_count) in enumerate(products):
        x_ref, g_ref = inputs[2 * at : 2 * at + 2]
        x_coming, g_coming = coming[at]
        share = x_count // parts
        pieces = share // rows
        count = X_BLOCK // share
        for block in range(x_count // X_BLOCK):
            wait_all(x_coming[block])
            for (first_g, width), arriving in zip(g_blocks(g_count), g_coming):
                if block == 0:
                    wait_all(arriving)
                total = dot_tn(
                    x_ref[:, X_BLOCK * block : X_BLOCK * (block + 1)], g_ref[:, first_g : first_g + width]
                ).astype(BF16)
                total = total.reshape(count, pieces, rows, width)
                for piece in range(pieces):
                    begin = done + g_count * piece + first_g
                    stage[count * block : count * (block + 1), :, begin : begin + width] = total[:, piece]
            for part in range(count * block, count * (block + 1)):
                leave(part, done, g_count * pieces)
        done += g_count * pieces
    if with_sums:
        wait_all(sums_coming)
        width = D // parts
        sums = (own_sums[...].astype(F32) + other_sums[...].astype(F32)).astype(BF16)
        begin = sum(g_count for _, _, _, g_count in products)
        for part in range(parts):
            stage[part, 0:16, begin : begin + width] = sums[0:16, width * part : width * (part + 1)]
            wide = FF // parts
            for layer in range(2):
                row = 16 + 4 * layer + part * wide // D
                for side in range(2):
                    lanes = part * wide % D + side * wide // 2
                    stage[part, 16 + 2 * layer + side : 17 + 2 * layer + side, begin : begin + wide // 2] = sums[
                        row : row + 1, lanes : lanes + wide // 2
                    ]
            leave(part, begin, 128)
    wait_all(leaving)


def plain_weight_kernel(own_x, other_x, own_g, other_g, out):
    total = dot_tn(own_x[...], own_g[...]) + dot_tn(other_x[...], other_g[...])
    out[...] = total.astype(BF16)


def add_kernel(*refs):
    total = 0.0
    for ref in refs[:-1]:
        total = total + ref[...].astype(F32)
    refs[-1][...] = total.astype(refs[-1].dtype)


def finish_kernel(layers, splits, parts, terms, outs):
    for layer, columns in enumerate(layers):
        total = 0.0
        for ref, first in terms[layer]:
            total = total + ref[0, :, first : first + columns].astype(F32)
        rows = total.shape[0]
        for out, (begin, count) in zip(outs, splits):
            for piece in range(out.shape[1] // rows):
                at = begin + count * piece
                out[layer, rows * piece : rows * (piece + 1), :] = total[:, at : at + count]
        if parts is not None and layer == 0:
            sums = total[0:SUMS, columns - 128 : columns]
            width = D // parts
            for to in range(2):
                for out, row in zip(outs[len(splits) :], (0, 1, 4, 2, 3, 5, 6, 7)):
                    row += 8 * to
                    out[to : to + 1, :] = sums[row : row + 1, 0:width]
                half_wide = FF // parts // 2
                for side in range(2):
                    row = 16 + 2 * to + side
                    outs[-1][to : to + 1, half_wide * side : half_wide * (side + 1)] = sums[
                        row : row + 1, 0:half_wide
                    ]


def assemble_kernel(tokens, came_tokens, tokens_out):
    tokens_out[...] = gather_back(tokens[...], came_tokens[...], lax.axis_index("seq"))


ANY = pl.BlockSpec(memory_space=pl.ANY)
FAR = pl.BlockSpec(memory_space=pltpu.HBM)
def shaped(*dims, dtype=BF16):
    return jax.ShapeDtypeStruct(dims, dtype)


def held(*dims, dtype=BF16):
    return pltpu.VMEM(dims, dtype)


def sems(count):
    return pltpu.SemaphoreType.DMA((count,))


def whole(shape):
    return pl.BlockSpec(shape, lambda: (0,) * len(shape))


EXPECTED_US = {
    "ahead": 33.0, "down1": 6.4, "up1": 6.6, "qkv1": 0.05, "down0": 6.4, "up0": 6.6, "qkv0": 0.05, "back1": 20.0,
    "back0": 13.6, "assemble": 3.3,
}


def expected(name):
    time = 4.0 * EXPECTED_US.get(name, 2.0)
    return pl.CostEstimate(flops=int(time * 1.15e9), bytes_accessed=int(time * 3.69e6), transcendentals=0)


def call(kernel, name, operands, outs, scratch, lens=None, after=(), carry=(), out_specs=None):
    first = [] if lens is None else [lens]
    first_specs = [] if lens is None else [pl.BlockSpec(memory_space=pltpu.SMEM)]
    skip = len(first) + len(after) + len(carry)
    inputs = skip + len(operands)

    def body(*refs):
        kernel(
            *refs[: len(first)], *refs[skip:inputs], *refs[inputs : inputs + len(outs)],
            *refs[inputs + len(outs) + len(carry) :],
        )

    return pl.pallas_call(
        body,
        in_specs=first_specs
        + [ANY] * (len(after) + len(carry))
        + [whole(array.shape) if near else ANY for array, near in operands],
        out_specs=(out_specs or [ANY] * len(outs)) + [ANY] * len(carry),
        out_shape=list(outs) + [shaped(*array.shape, dtype=array.dtype) for array in carry],
        input_output_aliases={len(first) + len(after) + at: len(outs) + at for at in range(len(carry))},
        scratch_shapes=list(scratch),
        compiler_params=pltpu.CompilerParams(vmem_limit_bytes=VMEM_LIMIT),
        cost_estimate=expected(name),
        name=name,
    )(*first, *after, *carry, *(array for array, _ in operands))


def near(*arrays):
    return [(array, True) for array in arrays]


def far(*arrays):
    return [(array, False) for array in arrays]


AHEAD = (
    ("hidden0", ROWS, D, BF16), ("xs0", ROWS, XS, BF16), ("joint0", ROWS, 3 * D, BF16), ("log0", ROWS, 128, F32),
    ("middle0", ROWS, D, F32), ("slope0", ROWS, FF, BF16), ("hidden1", ROWS, D, F32), ("xs1", ROWS, 3 * D, BF16),
    ("joint1", ROWS, 3 * D, BF16), ("log1", ROWS, 128, F32), ("active1", ROWS, FF, BF16), ("middle1", ROWS, D, F32),
    ("moved_middle1", MOVED, D, F32),
    ("grad_own1", ROWS, D // 2, BF16), ("grad_other1", ROWS, D // 2, BF16), ("own1", ROWS, GS, BF16),
    ("sent1", ROWS, GS, BF16), ("mid1", ROWS, D, F32), ("grad_merged1", ROWS, D, BF16), ("sums_b1", 8, D, F32),
)


def ahead(lens, tokens, came, cot, came_cot, vectors, matrices):
    direct = ("moved_middle1", "grad_own1", "grad_other1", "own1", "sent1")
    outs = call(
        ahead_kernel, "ahead", near(*vectors) + far(tokens, came, cot, came_cot, *matrices),
        [shaped(r, c, dtype=t) for _, r, c, t in AHEAD],
        [held(8, 128) if name in direct else held(r, c, dtype=t) for name, r, c, t in AHEAD]
        + [held(ROWS, FF), held(ROWS, D), held(ROWS, D), held(ROWS, FF), held(ROWS, D),
           held(HALF, D), held(HALF, D), held(HALF, D), held(HALF, D), held(16, D, BLOCK), sems(28), sems(24)],
        lens=lens,
    )
    return {name: out for (name, *_), out in zip(AHEAD, outs)}


def last_forward(active, came_active, middle, came_middle, down_w, down_b, after=()):
    return call(
        result_kernel, "result", near(down_b) + far(active, came_active, middle, came_middle, down_w),
        [shaped(HALF, D)],
        [held(ROWS, FF), held(MOVED, FF), held(ROWS, D, dtype=F32), held(MOVED, D, dtype=F32), held(FF, D),
         sems(3 * FFB + 2)],
        after=after, out_specs=[whole((HALF, D))],
    )[0]


def back1(lens, operands, gain1, gain2, matrices, after=()):
    sums = shaped(8, D, dtype=F32)
    return call(
        back1_kernel, "back1", near(gain1, gain2) + far(*matrices, *operands),
        [shaped(ROWS, JS + D // 2), shaped(ROWS, JS + D // 2), shaped(ROWS, GS), shaped(ROWS, GS),
         shaped(ROWS, D, dtype=F32), shaped(ROWS, D), sums, sums],
        [held(ROWS, 3 * D), held(ROWS, D), held(ROWS, 128, dtype=F32), held(ROWS, D, dtype=F32),
         held(ROWS, D, dtype=F32), held(ROWS, FF), held(ROWS, D, dtype=F32), held(ROWS, 3 * D),
         held(8, D, dtype=F32), held(ROWS, D), held(ROWS, D, dtype=F32), held(ROWS, FF), held(ROWS, D, dtype=F32),
         held(ROWS, D), held(ROWS, D), held(8, D, dtype=F32),
         held(4 + 2 * FFB, D, BLOCK), sems(11 + 2 * FFB), sems(12)],
        lens=lens, after=after,
    )


def back0(lens, operands, gain1, sums, qkv_w, after=()):
    return call(
        back0_kernel, "back0", near(gain1, *sums) + far(qkv_w, *operands),
        [shaped(ROWS + SUMS, JS), shaped(ROWS + SUMS, JS), shaped(ROWS, D), shaped(MOVED, D)],
        [held(ROWS, 3 * D), held(ROWS, D), held(ROWS, 128, dtype=F32), held(ROWS, D), held(ROWS, D, dtype=F32),
         held(ROWS, 3 * D), held(SUMS, D, dtype=F32), held(SUMS, D), held(ROWS, D), held(3, D, BLOCK), sems(8),
         sems(6)],
        lens=lens, after=after,
    )


def add(sums, begin, count, name, after=(), carry=()):
    arrays = []
    for _, terms in sums:
        for array, _ in terms:
            if not any(array is seen for seen in arrays):
                arrays.append(array)
    index = {id(array): at for at, array in enumerate(arrays)}
    share = arrays[0].shape[1]
    total = sum(columns for columns, _ in sums)
    skip = len(after) + len(carry)
    pieces = min(count, 2)
    size = count // pieces

    places = [
        (at, index[id(array)], first, columns)
        for at, (columns, terms) in enumerate(sums)
        for array, first in terms
    ]

    def body(*refs):
        sources, refs = refs[skip : skip + len(arrays)], refs[skip + len(arrays) :]
        out, *refs = refs[:1] + refs[1 + len(carry) :]
        *buffers, total_ref, load_sems, out_sems = refs
        loads, stores = Copies(load_sems), Copies(out_sems)
        coming, leaving = [], []
        for piece in range(pieces):
            parts_of = slice(size * piece, size * (piece + 1))
            coming.append(
                [
                    loads.start(
                        sources[source].at[begin + size * piece : begin + size * (piece + 1), :, first : first + columns],
                        buffer.at[parts_of],
                    )
                    for (_, source, first, columns), buffer in zip(places, buffers)
                ]
            )
        for piece in range(pieces):
            parts_of = slice(size * piece, size * (piece + 1))
            wait_all(coming[piece])
            done = 0
            for at, (columns, _) in enumerate(sums):
                value = 0.0
                for (which, *_), buffer in zip(places, buffers):
                    if which == at:
                        value = value + buffer[parts_of].astype(F32)
                total_ref[parts_of, :, done : done + columns] = value.astype(BF16)
                done += columns
            leaving.append(stores.start(total_ref.at[parts_of], out.at[parts_of]))
        wait_all(leaving)

    return pl.pallas_call(
        body,
        in_specs=[ANY] * skip + [FAR] * len(arrays),
        out_specs=[FAR] + [ANY] * len(carry),
        out_shape=[shaped(count, share, total)]
        + [shaped(*array.shape, dtype=array.dtype) for array in carry],
        input_output_aliases={len(after) + at: 1 + at for at in range(len(carry))},
        scratch_shapes=[held(count, share, columns) for *_, columns in places]
        + [held(count, share, total), sems(pieces * len(places)), sems(pieces)],
        compiler_params=pltpu.CompilerParams(vmem_limit_bytes=VMEM_LIMIT),
        cost_estimate=expected(name),
        name=name,
    )(*after, *carry, *arrays)


def swap(array):
    return lax.ppermute(array, "seq", [(0, 1), (1, 0)])


EVEN = ((0, 2, 1, 3), (1, 2, 0, 3))
LATE = ((0, 1, 2, 3), (1, 0, 2, 3))


class Halving:
    def __init__(self, name, kept, orders):
        self.name, self.orders = name, orders
        self.hop = 0
        self.columns = kept.shape[2]
        self.terms = [(kept, 0)]


def send(halvings, sent):
    hop, orders = halvings[0].hop, halvings[0].orders
    pairs = []
    for place in range(lax.axis_size("dp")):
        for core in range(2):
            other = place ^ (1 << orders[core][hop])
            pairs.append((2 * place + core, 2 * other + core))
    came = lax.ppermute(sent, ("dp", "seq"), pairs)
    first = 0
    for halving in halvings:
        halving.terms.append((came, first))
        halving.hop += 1
        first += halving.columns
    return came


def weight_gradient(name, operands, products, orders, with_sums, after=(), carry=()):
    parts = lax.axis_size("dp")
    columns = sum(g_count * (x_count // D) for _, x_count, _, g_count in products) + (128 if with_sums else 0)
    share = D // parts
    scratch = []
    copies = 2
    for _, x_count, _, g_count in products:
        scratch += [held(2 * ROWS, x_count), held(2 * ROWS, g_count)]
        copies += 2 * len(g_blocks(g_count)) + 2 * (x_count // X_BLOCK)
    if with_sums:
        scratch += [held(SUMS, D), held(SUMS, D)]
    return call(
        lambda *refs: weight_kernel(parts, orders, products, with_sums, *refs), name, far(*operands),
        [shaped(parts // 2, share, columns)] * 2,
        scratch
        + [held(parts, share, columns), sems(copies), sems(parts * (len(products) + int(with_sums)))],
        after=after, carry=carry,
    )


def finish(name, halvings, splits, parts=None, after=()):
    arrays = []
    for halving in halvings:
        for array, _ in halving.terms:
            if not any(array is seen for seen in arrays):
                arrays.append(array)
    index = {id(array): at for at, array in enumerate(arrays)}
    outs = [shaped(2, rows, count, dtype=F32) for _, count, rows in splits]
    if parts is not None:
        outs += [shaped(2, D // parts, dtype=F32)] * 8 + [shaped(2, FF // parts, dtype=F32)]

    places = [
        (index[id(array)], first, halving.columns) for halving in halvings for array, first in halving.terms
    ]

    def body(*refs):
        sources, refs = refs[len(after) : len(after) + len(arrays)], refs[len(after) + len(arrays) :]
        results, refs = refs[: len(outs)], refs[len(outs) :]
        *buffers, load_sems = refs
        loads = Copies(load_sems)
        wait_all(
            [
                loads.start(sources[source].at[0:1, :, first : first + columns], buffer)
                for (source, first, columns), buffer in zip(places, buffers)
            ]
        )
        terms, used = [], 0
        for halving in halvings:
            terms.append([(buffer, 0) for buffer in buffers[used : used + len(halving.terms)]])
            used += len(halving.terms)
        finish_kernel(
            [halving.columns for halving in halvings], [split[:2] for split in splits], parts, terms, results
        )

    return pl.pallas_call(
        body,
        in_specs=[ANY] * len(after) + [FAR] * len(arrays),
        out_specs=[whole(out.shape) for out in outs],
        out_shape=outs,
        scratch_shapes=[held(1, arrays[0].shape[1], columns) for *_, columns in places] + [sems(len(places))],
        compiler_params=pltpu.CompilerParams(vmem_limit_bytes=VMEM_LIMIT),
        cost_estimate=expected(name),
        name=name,
    )(*after, *arrays)


def plain_weight_gradient(name, own_x, other_x, own_g, other_g):
    rows, columns = own_x.shape[1], own_g.shape[1]
    x_spec = pl.BlockSpec((ROWS, BLOCK), lambda step: (0, step))
    g_spec = pl.BlockSpec((ROWS, columns), lambda step: (0, 0))
    return pl.pallas_call(
        plain_weight_kernel,
        grid=(rows // BLOCK,),
        in_specs=[x_spec, x_spec, g_spec, g_spec],
        out_specs=pl.BlockSpec((BLOCK, columns), lambda step: (step, 0)),
        out_shape=shaped(rows, columns),
        compiler_params=pltpu.CompilerParams(vmem_limit_bytes=VMEM_LIMIT),
        name=name,
    )(own_x, other_x, own_g, other_g)


def plain_halving(total, bit_order):
    parts = lax.axis_size("dp")
    place = lax.axis_index("dp")
    bits = parts.bit_length() - 1
    total = total.reshape((2,) * bits + (total.shape[0] // parts, total.shape[1]))
    left = list(range(bits))[::-1]
    terms = [total]
    for bit in bit_order:
        axis = left.index(bit)
        left.remove(bit)
        mine = (place >> bit) & 1
        sent = sum(lax.dynamic_index_in_dim(t, 1 - mine, axis, keepdims=False).astype(F32) for t in terms)
        terms = [lax.dynamic_index_in_dim(t, mine, axis, keepdims=False) for t in terms]
        terms.append(
            lax.ppermute(sent.astype(BF16), "dp", [(i, i ^ (1 << bit)) for i in range(parts)])
        )
    return sum(t.astype(F32) for t in terms)


def sum_everywhere(array):
    total = array + swap(array)
    parts = lax.axis_size("dp")
    for bit in range(parts.bit_length() - 1):
        total = total + lax.ppermute(total, "dp", [(i, i ^ (1 << bit)) for i in range(parts)])
    return total


def shards(
    tokens, crop_len, qkv_weight, query_bias, value_bias, out_weight, out_bias, first_gain, first_shift,
    second_gain, second_shift, up_weight, up_bias, down_weight, down_bias, cotangent,
):
    parts = lax.axis_size("dp")
    lens = crop_len.reshape(-1)
    core = lax.axis_index("seq")
    tiled = parts == 16
    matrices = (out_weight, up_weight, down_weight)
    came_tokens = swap(tokens)
    came_cot = swap(cotangent)
    kept = ahead(
        lens, tokens, came_tokens, cotangent, came_cot,
        (first_gain, first_shift, query_bias, value_bias, out_bias, second_gain, second_shift, up_bias, down_bias),
        (qkv_weight,) + matrices,
    )
    reductions = {}

    def product(name, operands, products, after=(), carry=(), with_sums=False, orders=EVEN):
        if not tiled:
            totals = []
            for at, (x_from, x_count, g_from, g_count) in enumerate(products):
                own_x, other_x, own_g, other_g = operands[4 * at : 4 * at + 4]
                x_at, g_at = slice(x_from, x_from + x_count), slice(g_from, g_from + g_count)
                total = plain_weight_gradient(
                    name, own_x[:, x_at], other_x[:, x_at], own_g[:ROWS, g_at], other_g[:ROWS, g_at]
                )
                totals.append(plain_halving(total, range(parts.bit_length() - 1)))
            reductions[name] = totals
            return (total, *carry)
        here, gone, *carried = weight_gradient(name, operands, products, orders, with_sums, after, carry)
        reductions[name] = Halving(name, here, orders)
        send([reductions[name]], gone)
        return (gone, *carried)

    def step(names, after=(), carry=()):
        if not tiled:
            return (*(after or (tokens,))[:1], *carry)
        group = [reductions[name] for name in names.split()]
        hop = group[0].hop
        count = parts >> (hop + 1)
        sums = [(halving.columns, halving.terms) for halving in group]
        sent, *carried = add(sums, count, count, "_".join(names.split()) + f"_hop{hop}", after, carry)
        send(group, sent)
        return (sent, *carried)

    def arrived(name):
        return (reductions[name].terms[-1][0],) if tiled else ()

    active1, xs1, xs0 = kept["active1"], kept["xs1"], kept["xs0"]
    own1, sent1 = kept["own1"], kept["sent1"]
    came_active1 = swap(active1)
    came_gs1 = swap(sent1)
    came_xs1 = swap(xs1)
    came_middle1 = swap(kept["moved_middle1"])
    last, xs0 = product(
        "down1", (active1, came_active1, kept["grad_own1"], kept["grad_other1"]), ((0, FF, 0, D // 2),),
        carry=(xs0,),
    )
    came_xs0 = swap(xs0)
    (last,) = product(
        "up1", (xs1, came_xs1, own1, came_gs1, xs1, came_xs1, own1, came_gs1),
        ((LOW2, D, 0, FF // 2), (MERGED, D, FF // 2, D // 2)), after=(last, came_middle1),
    )
    own_j1, sent_j1, own_g0, sent_g0, mid0, grad_merged0, sums_a1, sums_b0 = back1(
        lens,
        (kept["joint1"], kept["grad_merged1"], kept["log1"], kept["hidden1"], kept["mid1"], kept["slope0"],
         kept["middle0"]),
        first_gain, second_gain, (qkv_weight,) + matrices, after=(last,),
    )
    last, sent_j1, sent_g0 = step("down1", after=(own_j1,), carry=(sent_j1, sent_g0))
    came_j1 = swap(sent_j1)
    came_g0 = swap(sent_g0)
    (last,) = product(
        "qkv1", (xs1, came_xs1, own_j1, came_j1), ((LOW1, D, 0, JS),), after=(last,)
    )
    (last,) = step("up1", after=(last,))
    (last,) = product("down0", (xs0, came_xs0, own_j1, came_j1), ((0, FF, JS, D // 2),), after=(last,))
    (last,) = product(
        "up0", (xs0, came_xs0, own_g0, came_g0, xs0, came_xs0, own_g0, came_g0),
        ((FF + LOW2, D, 0, FF // 2), (FF + MERGED, D, FF // 2, D // 2)), after=(last,), orders=EVEN,
    )
    (last,) = step("qkv1", after=(last,))
    own_j0, sent_j0, grad_tokens, moved_tokens = back0(
        lens, (kept["joint0"], grad_merged0, kept["log0"], kept["hidden0"], mid0), first_gain,
        (sums_b0, sums_a1, kept["sums_b1"]), qkv_weight, after=(last,),
    )
    last, sent_j0 = step("down1 up1", after=(own_j0,), carry=(sent_j0,))
    came_j0 = swap(sent_j0)
    (last,) = step("down0", after=(last,) + arrived("qkv1"))
    (last,) = product(
        "qkv0", (xs0, came_xs0, own_j0, came_j0), ((FF + LOW1, D, 0, JS),), after=(last,), with_sums=True, orders=LATE,
    )
    (last,) = step("up0", after=(last,))
    last, moved_tokens = step("down1 up1", after=(last,), carry=(moved_tokens,))
    came_tokens = swap(moved_tokens)
    (last,) = step("qkv1 down0", after=(last,))
    (last,) = step("qkv0", after=(last, came_tokens))
    (last,) = step("qkv1 down0", after=(last,))
    (last,) = step("qkv0", after=(last,))
    (last,) = step("up0", after=(last,))
    (grad_tokens,) = call(
        assemble_kernel, "assemble", near(grad_tokens, came_tokens), [shaped(HALF, D)], [],
        out_specs=[whole((HALF, D))], after=(last,),
    )
    (last,) = step("up0", after=(grad_tokens,))
    (last,) = step("qkv0", after=(last,))
    result = last_forward(
        active1, came_active1, kept["middle1"], came_middle1, down_weight, down_bias, after=(last,)
    )
    if tiled:
        share = D // parts
        (down_g,) = finish(
            "finish_down", (reductions["down0"], reductions["down1"]), ((0, D // 2, FF // parts),), after=(result,)
        )
        up_g, out_g = finish(
            "finish_up", (reductions["up0"], reductions["up1"]),
            ((0, FF // 2, share), (FF // 2, D // 2, share)), after=(down_g,),
        )
        qkv_g, *vectors = finish(
            "finish_qkv", (reductions["qkv0"], reductions["qkv1"]), ((0, JS, share),), parts, after=(up_g,)
        )
    else:
        down_g, up_g, out_g, qkv_g = (
            jnp.stack([reductions[name + "0"][at], reductions[name + "1"][at]])
            for name, at in (("down", 0), ("up", 0), ("up", 1), ("qkv", 0))
        )
        total = sum_everywhere(own_j0[ROWS:, :D].astype(F32))
        place = lax.axis_index("dp")
        width = D // parts
        narrow = lax.dynamic_slice(total[:16], (0, place * width), (16, width)).reshape(2, 8, width)
        vectors = [narrow[:, row] for row in (0, 1, 4, 2, 3, 5, 6, 7)]
        vectors.append(
            lax.dynamic_slice(total[16:24].reshape(2, FF), (0, place * (FF // parts)), (2, FF // parts))
        )
    query_b, value_b, out_b, gain1, shift1, gain2, shift2, down_b, up_b = vectors
    return (
        result, grad_tokens, qkv_g, query_b, value_b, out_g, out_b, gain1, shift1, gain2, shift2, up_g, up_b, down_g,
        down_b,
    )


def solution(mesh):
    rows = P(("dp", "seq"), None)
    matrix = P(None, "dp", "seq")
    narrow = P(None, "dp")
    return jax.shard_map(
        shards,
        mesh=mesh,
        in_specs=(rows, P("dp", None)) + (P(),) * 13 + (rows,),
        out_specs=(
            rows, rows, matrix, narrow, narrow, matrix, narrow, narrow, narrow, narrow, narrow, matrix, narrow,
            matrix, narrow,
        ),
        check_vma=False,
    )
```

```python
import jax
import jax.numpy as jnp
from jax import lax
from jax.experimental import pallas as pl
from jax.experimental.pallas import tpu as pltpu
from jax.sharding import PartitionSpec as P

HD = 64
GPAD = 198
LPAD = 38
HALF = 350
SPLIT = HALF - GPAD
REST = GPAD - SPLIT
WIDE = 208
SLOT = 40
LOCALS = 4
ROWS = WIDE + SLOT * LOCALS
MOVED = SLOT * LOCALS
HEADS = 12
D = 768
FF = 3072
BLOCK = 768
FFB = FF // BLOCK
X_BLOCK = 768
G_BLOCK = 1536

EPS = 1e-06
MASKED = -1e30
SCALE = HD ** (-0.5)
BF16 = jnp.bfloat16
F32 = jnp.float32

VMEM_LIMIT = 64 * 1024 * 1024 - 64 * 1024


def dot(left, right):
    return jnp.dot(left, right, preferred_element_type=F32)


def dot_nt(left, right):
    return lax.dot_general(left, right, (((1,), (1,)), ((), ())), preferred_element_type=F32)


def dot_tn(left, right):
    return lax.dot_general(left, right, (((0,), (0,)), ((), ())), preferred_element_type=F32)


def normal_parts(values):
    mass = 0.5 + 0.5 * lax.erf(values * 0.7071067811865476)
    return mass, jnp.exp(-0.5 * values * values) * 0.3989422804014327


def norm_parts(hidden):
    row_mean = jnp.mean(hidden, axis=-1, keepdims=True)
    centered = hidden - row_mean
    inverse = lax.rsqrt(jnp.mean(centered * centered, axis=-1, keepdims=True) + EPS)
    return centered * inverse, inverse


def norm_back(upstream, normed, inverse, norm_gain):
    scaled = upstream * norm_gain
    centered = scaled - jnp.mean(scaled, axis=-1, keepdims=True)
    centered = centered - normed * jnp.mean(scaled * normed, axis=-1, keepdims=True)
    return centered * inverse


def column_sum(array):
    return jnp.sum(array.astype(F32), axis=0, keepdims=True)


def slot_row(position):
    crop = jnp.zeros_like(position)
    for at in range(1, LOCALS):
        crop = crop + (position >= SLOT * at).astype(jnp.int32)
    inner = position - SLOT * crop
    return jnp.where((position >= 0) & (inner < LPAD), LPAD * crop + inner, -4 * HALF)


def spread(own, came, core):
    position = lax.broadcasted_iota(jnp.int32, (ROWS, HALF), 0)
    column = lax.broadcasted_iota(jnp.int32, (ROWS, HALF), 1)
    local = slot_row(position - WIDE)
    own0 = jnp.where(position < GPAD, position, -1)
    came0 = local + REST
    own1 = jnp.where(
        (position >= SPLIT) & (position < GPAD), position - SPLIT, local + GPAD
    )
    came1 = jnp.where(position < SPLIT, position + GPAD, -1)
    own_from = own0 * (1 - core) + own1 * core
    came_from = came0 * (1 - core) + came1 * core
    return dot(jnp.where(own_from == column, 1.0, 0.0).astype(BF16), own) + dot(
        jnp.where(came_from == column, 1.0, 0.0).astype(BF16), came
    )


def gather_back(own, came, core):
    row = lax.broadcasted_iota(jnp.int32, (HALF, ROWS), 0)
    position = lax.broadcasted_iota(jnp.int32, (HALF, ROWS), 1)
    local = slot_row(position - WIDE)
    own0 = jnp.where(position < GPAD, position, -1)
    own1 = jnp.where(
        (position >= SPLIT) & (position < GPAD), position - SPLIT, local + GPAD
    )
    own_to = own0 * (1 - core) + own1 * core
    came_row = lax.broadcasted_iota(jnp.int32, (HALF, MOVED), 0)
    came_position = lax.broadcasted_iota(jnp.int32, (HALF, MOVED), 1)
    came0 = jnp.where(came_position < SPLIT, came_position + GPAD, -1)
    came1 = slot_row(came_position) + REST
    came_to = came0 * (1 - core) + came1 * core
    return (
        dot(jnp.where(own_to == row, 1.0, 0.0).astype(BF16), own)
        + dot(jnp.where(came_to == came_row, 1.0, 0.0).astype(BF16), came)
    ).astype(BF16)


def head_lanes():
    lane = lax.broadcasted_iota(jnp.int32, (1, 2 * HD), 1)
    left = jnp.where(lane < HD, 1.0, 0.0)
    return (left.astype(BF16), (1.0 - left).astype(BF16)), (
        (left * SCALE).astype(BF16),
        ((1.0 - left) * SCALE).astype(BF16),
    )


def both_heads(array, masks):
    return jnp.concatenate([array * masks[0], array * masks[1]], axis=0)


def own_lanes(stacked):
    rows = stacked.shape[0] // 2
    lane = lax.broadcasted_iota(jnp.int32, (rows, 2 * HD), 1)
    return jnp.where(lane < HD, stacked[:rows], stacked[rows:])


def pair(at, block):
    return slice(block * D + 2 * HD * at, block * D + 2 * HD * (at + 1))


def windows(lens_ref, core, pieces):
    column = lax.broadcasted_iota(jnp.int32, (2 * WIDE, WIDE), 1)
    plan = [(slice(0, WIDE), column < lens_ref[core])]
    count = LOCALS // pieces
    size = SLOT * count
    row = lax.broadcasted_iota(jnp.int32, (2 * size, size), 0)
    row = jnp.where(row >= size, row - size, row)
    column = lax.broadcasted_iota(jnp.int32, (2 * size, size), 1)
    for piece in range(pieces):
        allowed = None
        for at in range(count):
            begin = SLOT * at
            end = begin + lens_ref[2 + LOCALS * core + count * piece + at]
            mine = (row >= begin) & (row < begin + SLOT) & (column >= begin) & (column < end)
            allowed = mine if allowed is None else allowed | mine
        begin = WIDE + size * piece
        plan.append((slice(begin, begin + size), allowed))
    return plan


TOGETHER, PIECES = 3, 2
TOGETHER_BACK, PIECES_BACK = 3, 2


def attend(lens_ref, core, joint_ref, merged_ref, log_ref):
    _, scaled = head_lanes()
    lane = lax.broadcasted_iota(jnp.int32, (1, 128), 1)
    plan = windows(lens_ref, core, PIECES)
    logs = [jnp.zeros((rows.stop - rows.start, 128), F32) for rows, _ in plan]
    for begin in range(0, HEADS // 2, TOGETHER):
        chains = [(which, at) for at in range(begin, begin + TOGETHER) for which in range(len(plan))]
        scores = []
        for which, at in chains:
            rows, allowed = plan[which]
            queries = both_heads(joint_ref[rows, pair(at, 0)], scaled)
            scores.append(jnp.where(allowed, dot_nt(queries, joint_ref[rows, pair(at, 1)]), MASKED))
        row_max = [jnp.max(array, axis=-1, keepdims=True) for array in scores]
        exponent = [jnp.exp(array - top) for array, top in zip(scores, row_max)]
        totals = [jnp.sum(array, axis=-1, keepdims=True) for array in exponent]
        weights = [(array * (1.0 / total)).astype(BF16) for array, total in zip(exponent, totals)]
        for (which, at), array, top, total in zip(chains, weights, row_max, totals):
            rows, _ = plan[which]
            merged_ref[rows, pair(at, 0)] = own_lanes(dot(array, joint_ref[rows, pair(at, 2)])).astype(BF16)
            log_totals = top + jnp.log(total)
            count = rows.stop - rows.start
            for side in range(2):
                logs[which] = jnp.where(
                    lane == 2 * at + side, log_totals[count * side : count * (side + 1)], logs[which]
                )
    for (rows, _), array in zip(plan, logs):
        log_ref[rows, :] = array


def attend_back(lens_ref, core, joint_ref, up_ref, log_ref, grad_ref):
    plain, scaled = head_lanes()
    plan = windows(lens_ref, core, PIECES_BACK)
    for begin in range(0, HEADS // 2, TOGETHER_BACK):
        chains = [(which, at) for at in range(begin, begin + TOGETHER_BACK) for which in range(len(plan))]
        queries, upstream, weights, grad_weights = [], [], [], []
        for which, at in chains:
            rows, allowed = plan[which]
            queries.append(both_heads(joint_ref[rows, pair(at, 0)], scaled))
            upstream.append(both_heads(up_ref[rows, pair(at, 0)], plain))
            log_total = jnp.concatenate(
                [log_ref[rows, 2 * at + side : 2 * at + side + 1] for side in range(2)], axis=0
            )
            scores = jnp.where(allowed, dot_nt(queries[-1], joint_ref[rows, pair(at, 1)]), MASKED)
            weights.append(jnp.exp(scores - log_total))
            grad_weights.append(dot_nt(upstream[-1], joint_ref[rows, pair(at, 2)]))
        weighted = [one * two for one, two in zip(weights, grad_weights)]
        row_dot = [jnp.sum(array, axis=-1, keepdims=True) for array in weighted]
        grad_scores = [
            (array - one * dots).astype(BF16) for array, one, dots in zip(weighted, weights, row_dot)
        ]
        for (which, at), scores, one, query, up in zip(chains, grad_scores, weights, queries, upstream):
            rows, _ = plan[which]
            grad_ref[rows, pair(at, 2)] = dot_tn(one.astype(BF16), up).astype(BF16)
            grad_ref[rows, pair(at, 0)] = (
                own_lanes(dot(scores, joint_ref[rows, pair(at, 1)])) * SCALE
            ).astype(BF16)
            grad_ref[rows, pair(at, 1)] = dot_tn(scores, query).astype(BF16)


class Copies:
    def __init__(self, sems):
        self.sems = sems
        self.started = 0

    def start(self, source, target):
        copy = pltpu.make_async_copy(source, target, self.sems.at[self.started])
        self.started += 1
        copy.start()
        return copy


def wait_all(copies):
    for copy in copies:
        copy.wait()


def columns_of(ref, at):
    return ref.at[:, BLOCK * at : BLOCK * (at + 1)]


def core_half(ref, core):
    width = ref.shape[1] // 2
    return ref.at[:, pl.ds(pl.multiple_of(core * width, 128), width)]


def moved_rows(ref, core):
    return ref.at[pl.ds(pl.multiple_of(WIDE * (1 - core), 16), MOVED), :]


def vector(ref, layer):
    return ref[layer : layer + 1, :]


XS = FF + 3 * D
LOW2, MERGED, LOW1 = 0, D, 2 * D
GS = FF // 2 + D // 2
JS = 3 * D // 2
SUMS = 32


def ahead_kernel(
    lens, tokens, came, cot, came_cot, gain1, shift1, query_b, value_b, out_b, gain2, shift2, up_b, down_b,
    qkv_w, out_w, up_w, down_w, *refs,
):
    count = len(AHEAD)
    outs, held = refs[:count], refs[count : 2 * count]
    out_of = dict(zip((name for name, *_ in AHEAD), outs))
    ref_of = dict(zip((name for name, *_ in AHEAD), held))
    slope_ref, grad_ref, other_ref, grad_up_ref, branch_ref, *refs = refs[2 * count :]
    weights, weight_sems, out_sems = refs
    core = lax.axis_index("seq")
    loads = Copies(weight_sems)
    stores = Copies(out_sems)
    leaving = []

    def leave(name):
        leaving.append(stores.start(ref_of[name], out_of[name]))

    def load_columns(ref, layer, blocks, slot):
        return [loads.start(columns_of(ref.at[layer], at), weights.at[slot + at]) for at in range(blocks)]

    def load_rows(ref, layer, blocks, slot):
        return [
            loads.start(ref.at[layer, BLOCK * at : BLOCK * (at + 1), :], weights.at[slot + at])
            for at in range(blocks)
        ]

    qkv = load_columns(qkv_w, 0, 3, 0)
    out = load_rows(out_w, 0, 1, 3)
    ups = load_columns(up_w, 0, FFB, 4)
    downs = load_rows(down_w, 0, FFB, 8)
    next_qkv = load_columns(qkv_w, 1, 3, 12)
    next_out = load_rows(out_w, 1, 1, 15)

    hidden = spread(tokens[...], came[...], core)
    for layer in range(2):
        if layer == 0:
            low1_ref = ref_of["xs0"].at[:, FF + LOW1 : FF + LOW1 + D]
            low2_ref = ref_of["xs0"].at[:, FF + LOW2 : FF + LOW2 + D]
            merged_ref = ref_of["xs0"].at[:, FF + MERGED : FF + MERGED + D]
            active_ref = ref_of["xs0"].at[:, 0:FF]
            joint_ref, log_ref, mid_ref, gelu_slope_ref = (
                ref_of["joint0"], ref_of["log0"], ref_of["middle0"], ref_of["slope0"],
            )
            ref_of["hidden0"][...] = hidden.astype(BF16)
            leave("hidden0")
            slot = 0
        else:
            low1_ref = ref_of["xs1"].at[:, LOW1 : LOW1 + D]
            low2_ref = ref_of["xs1"].at[:, LOW2 : LOW2 + D]
            merged_ref = ref_of["xs1"].at[:, MERGED : MERGED + D]
            active_ref = ref_of["active1"]
            joint_ref, log_ref, mid_ref, gelu_slope_ref = ref_of["joint1"], ref_of["log1"], ref_of["middle1"], slope_ref
            ref_of["hidden1"][...] = hidden
            leave("hidden1")
            slot = 12
            qkv, out = next_qkv, next_out
            ups = load_columns(up_w, 1, FFB, 4)
            downs = load_rows(down_w, 1, FFB, 8)
        normed, _ = norm_parts(hidden)
        low1_ref[...] = (normed * vector(gain1, layer) + vector(shift1, layer)).astype(BF16)
        wait_all(qkv)
        for block, bias in enumerate((vector(query_b, layer), None, vector(value_b, layer))):
            joint = dot(low1_ref[...], weights[slot + block])
            if bias is not None:
                joint = joint + bias
            joint_ref[:, BLOCK * block : BLOCK * (block + 1)] = joint.astype(BF16)
        leave(f"joint{layer}")
        attend(lens, core, joint_ref, merged_ref, log_ref)
        leave(f"log{layer}")
        wait_all(out)
        middle = hidden + dot(merged_ref[...], weights[slot + 3]) + vector(out_b, layer)
        mid_ref[...] = middle
        leave(f"middle{layer}")
        if layer == 1:
            leaving.append(stores.start(moved_rows(mid_ref, core), out_of["moved_middle1"]))
        normed, _ = norm_parts(middle)
        low2_ref[...] = (normed * vector(gain2, layer) + vector(shift2, layer)).astype(BF16)
        if layer == 1:
            leave("xs1")
        wait_all(ups)
        for block in range(FFB):
            columns = slice(BLOCK * block, BLOCK * (block + 1))
            up_values = dot(low2_ref[...], weights[4 + block]) + up_b[layer : layer + 1, columns]
            mass, bell = normal_parts(up_values)
            active_ref[:, columns] = (up_values * mass).astype(BF16)
            gelu_slope_ref[:, columns] = (mass + up_values * bell).astype(BF16)
        leave("active1" if layer == 1 else "xs0")
        if layer == 0:
            leave("slope0")
        wait_all(downs)
        if layer == 0:
            hidden = mid_ref[...] + dot(active_ref[...], weights[8:12].reshape(FF, D)) + vector(down_b, layer)
    grad_ref[...] = spread(cot[...], came_cot[...], core).astype(BF16)
    other_ref[...] = spread(came_cot[...], cot[...], 1 - core).astype(BF16)
    leaving.append(stores.start(core_half(grad_ref, core), out_of["grad_own1"]))
    leaving.append(stores.start(core_half(other_ref, core), out_of["grad_other1"]))
    mlp_back_part(
        core, grad_ref[...], grad_ref[...].astype(F32), slope_ref, ref_of["middle1"], vector(gain2, 1),
        [weights[8 + at] for at in range(FFB)], [weights[4 + at] for at in range(FFB)], weights[15],
        grad_up_ref, branch_ref, ref_of["mid1"], ref_of["grad_merged1"], ref_of["sums_b1"], out_of["own1"],
        out_of["sent1"], stores, leaving,
    )
    for name in ("mid1", "grad_merged1", "sums_b1"):
        leave(name)
    wait_all(leaving)


def result_kernel(
    down_b, active, came_active, middle, came_middle, down_w, out,
    active_ref, came_active_ref, middle_ref, came_middle_ref, weights, load_sems,
):
    core = lax.axis_index("seq")
    loads = Copies(load_sems)
    coming = []
    for at in range(FFB):
        columns = slice(BLOCK * at, BLOCK * (at + 1))
        coming.append(
            (
                loads.start(down_w.at[1, columns, :], weights.at[columns, :]),
                loads.start(active.at[:, columns], active_ref.at[:, columns]),
                loads.start(moved_rows(came_active, 1 - core).at[:, columns], came_active_ref.at[:, columns]),
            )
        )
    rest = [loads.start(middle, middle_ref), loads.start(came_middle, came_middle_ref)]
    own = came = vector(down_b, 1)
    for at in range(FFB):
        columns = slice(BLOCK * at, BLOCK * (at + 1))
        wait_all(coming[at])
        own = own + dot(active_ref[:, columns], weights[columns, :])
        came = came + dot(came_active_ref[:, columns], weights[columns, :])
    wait_all(rest)
    own = (middle_ref[...] + own).astype(BF16)
    out[...] = gather_back(own, (came_middle_ref[...] + came).astype(BF16), core)


def mlp_back_part(
    core, grad, upstream, slope_ref, middle_ref, gain, downs, ups, out_weight, grad_up_ref, branch_ref, mid_ref,
    grad_merged_ref, sums_ref, own, sent, stores, leaving,
):
    sums_ref[3:4, :] = column_sum(grad)
    back = 0.0
    for block in range(FFB):
        columns = slice(BLOCK * block, BLOCK * (block + 1))
        grad_up = (dot_nt(grad, downs[block]) * slope_ref[:, columns].astype(F32)).astype(BF16)
        grad_up_ref[:, columns] = grad_up
        sums_ref[4 + block : 5 + block, :] = column_sum(grad_up)
        back = back + dot_nt(grad_up, ups[block])
    leaving.append(stores.start(core_half(grad_up_ref, 1 - core), sent.at[:, 0 : FF // 2]))
    leaving.append(stores.start(core_half(grad_up_ref, core), own.at[:, 0 : FF // 2]))
    normed, inverse = norm_parts(middle_ref[...])
    sums_ref[1:2, :] = column_sum(back * normed)
    sums_ref[2:3, :] = column_sum(back)
    grad_mid = norm_back(back, normed, inverse, gain) + upstream
    mid_ref[...] = grad_mid
    branch = grad_mid.astype(BF16)
    branch_ref[...] = branch
    leaving.append(stores.start(core_half(branch_ref, 1 - core), sent.at[:, FF // 2 : GS]))
    leaving.append(stores.start(core_half(branch_ref, core), own.at[:, FF // 2 : GS]))
    sums_ref[0:1, :] = column_sum(branch)
    grad_merged_ref[...] = dot_nt(branch, out_weight).astype(BF16)


def attention_back_part(
    layer, lens, core, coming, qkv, held, gain1, weights, grad_joint_ref, sums_ref, sums_at, own, sent, stores, leaving
):
    joint_ref, up_ref, log_ref, hidden_ref, mid_ref = held
    wait_all(coming[:3])
    attend_back(lens, core, joint_ref, up_ref, log_ref, grad_joint_ref)
    leaving.append(stores.start(core_half(grad_joint_ref, 1 - core), sent.at[0:ROWS, 0:JS]))
    leaving.append(stores.start(core_half(grad_joint_ref, core), own.at[0:ROWS, 0:JS]))
    sums_ref[sums_at : sums_at + 1, :] = column_sum(grad_joint_ref[:, 0:D])
    sums_ref[sums_at + 1 : sums_at + 2, :] = column_sum(grad_joint_ref[:, 2 * D : 3 * D])
    wait_all(qkv)
    grad_first = 0.0
    for block in range(3):
        grad_first = grad_first + dot_nt(
            grad_joint_ref[:, BLOCK * block : BLOCK * (block + 1)], weights[block]
        )
    wait_all(coming[3:])
    normed, inverse = norm_parts(hidden_ref[...].astype(F32))
    sums_ref[sums_at + 2 : sums_at + 3, :] = column_sum(grad_first * normed)
    sums_ref[sums_at + 3 : sums_at + 4, :] = column_sum(grad_first)
    return norm_back(grad_first, normed, inverse, vector(gain1, layer)) + mid_ref[...]


def back1_kernel(
    lens, gain1, gain2, qkv_w, out_w, up_w, down_w, joint, grad_merged, log, hidden, mid, slope, middle,
    own_j, sent_j, own_g, sent_g, mid_out, grad_merged_out, sums_a_out, sums_b_out,
    joint_ref, up_ref, log_ref, hidden_ref, mid_ref, slope_ref, middle_ref, grad_joint_ref, sums_a_ref, grad_ref,
    upstream_ref, grad_up_ref, mid0_ref, branch_ref, grad_merged_ref, sums_b_ref, weights, load_sems, out_sems,
):
    core = lax.axis_index("seq")
    loads = Copies(load_sems)
    stores = Copies(out_sems)
    held = (joint_ref, up_ref, log_ref, hidden_ref, mid_ref)
    coming = [
        loads.start(source, target) for source, target in ((joint, joint_ref), (grad_merged, up_ref), (log, log_ref))
    ]
    qkv = [loads.start(columns_of(qkv_w.at[1], at), weights.at[at]) for at in range(3)]
    coming += [loads.start(hidden, hidden_ref), loads.start(mid, mid_ref)]
    later = [
        loads.start(down_w.at[0, BLOCK * at : BLOCK * (at + 1), :], weights.at[3 + at]) for at in range(FFB)
    ]
    later += [loads.start(slope, slope_ref)]
    later += [loads.start(columns_of(up_w.at[0], at), weights.at[3 + FFB + at]) for at in range(FFB)]
    later += [loads.start(middle, middle_ref), loads.start(out_w.at[0], weights.at[3 + 2 * FFB])]
    leaving = []
    sums_a_ref[...] = jnp.zeros_like(sums_a_ref)
    upstream = attention_back_part(
        1, lens, core, coming, qkv, held, gain1, weights, grad_joint_ref, sums_a_ref, 0, own_j, sent_j, stores, leaving
    )
    upstream_ref[...] = upstream
    grad = upstream.astype(BF16)
    grad_ref[...] = grad
    leaving.append(stores.start(core_half(grad_ref, 1 - core), sent_j.at[:, JS : JS + D // 2]))
    leaving.append(stores.start(core_half(grad_ref, core), own_j.at[:, JS : JS + D // 2]))
    leaving.append(stores.start(sums_a_ref, sums_a_out))
    wait_all(later)
    mlp_back_part(
        core, grad_ref[...], upstream_ref[...], slope_ref, middle_ref, vector(gain2, 0),
        [weights[3 + at] for at in range(FFB)], [weights[3 + FFB + at] for at in range(FFB)], weights[3 + 2 * FFB],
        grad_up_ref, branch_ref, mid0_ref, grad_merged_ref, sums_b_ref, own_g, sent_g, stores, leaving,
    )
    for source, target in ((mid0_ref, mid_out), (grad_merged_ref, grad_merged_out), (sums_b_ref, sums_b_out)):
        leaving.append(stores.start(source, target))
    wait_all(leaving)


def back0_kernel(
    lens, gain1, sums_b0, sums_a1, sums_b1, qkv_w, joint, grad_merged, log, hidden, mid,
    own_j, sent_j, tokens_out, moved_out,
    joint_ref, up_ref, log_ref, hidden_ref, mid_ref, grad_joint_ref, sums_ref, low_sums_ref, out_ref, weights,
    load_sems, out_sems,
):
    core = lax.axis_index("seq")
    loads = Copies(load_sems)
    stores = Copies(out_sems)
    held = (joint_ref, up_ref, log_ref, hidden_ref, mid_ref)
    sources = (joint, grad_merged, log, hidden, mid)
    coming = [loads.start(source, target) for source, target in zip(sources[:3], held[:3])]
    qkv = [loads.start(columns_of(qkv_w.at[0], at), weights.at[at]) for at in range(3)]
    coming += [loads.start(source, target) for source, target in zip(sources[3:], held[3:])]
    leaving = []
    sums_ref[...] = jnp.zeros_like(sums_ref)
    grad_in = attention_back_part(
        0, lens, core, coming, qkv, held, gain1, weights, grad_joint_ref, sums_ref, 0, own_j, sent_j, stores, leaving
    )
    sums_ref[4:8, :] = sums_b0[0:4, :]
    sums_ref[8:12, :] = sums_a1[0:4, :]
    sums_ref[12:16, :] = sums_b1[0:4, :]
    sums_ref[16:20, :] = sums_b0[4:8, :]
    sums_ref[20:24, :] = sums_b1[4:8, :]
    low_sums_ref[...] = sums_ref[...].astype(BF16)
    for target in (own_j, sent_j):
        leaving.append(stores.start(low_sums_ref, target.at[ROWS : ROWS + SUMS, 0:D]))
    out_ref[...] = grad_in.astype(BF16)
    leaving.append(stores.start(out_ref, tokens_out))
    leaving.append(stores.start(moved_rows(out_ref, core), moved_out))
    wait_all(leaving)


def hop_position(parts, core_orders, part, place, core):
    bits = parts.bit_length() - 1
    distance = part ^ place
    position = [0, 0]
    for side in range(2):
        for hop, bit in enumerate(core_orders[side]):
            position[side] |= ((distance >> bit) & 1) << (bits - 1 - hop)
    return position[0] * (1 - core) + position[1] * core


def g_blocks(count):
    return [(begin, min(G_BLOCK, count - begin)) for begin in range(0, count, G_BLOCK)]


def weight_kernel(parts, core_orders, products, with_sums, *refs):
    sources, refs = refs[: 4 * len(products)], refs[4 * len(products) :]
    kept, sent, *refs = refs
    inputs, refs = refs[: 2 * len(products)], refs[2 * len(products) :]
    if with_sums:
        own_sums, other_sums, block_ref, *refs = refs
    stage, load_sems, out_sems = refs
    core = lax.axis_index("seq")
    place = lax.axis_index("dp")
    loads = Copies(load_sems)
    first, second = slice(0, ROWS), slice(ROWS, 2 * ROWS)
    rows = stage.shape[1]
    half = parts // 2
    coming = []
    for at, (x_from, x_count, g_from, g_count) in enumerate(products):
        own_x, other_x, own_g, other_g = sources[4 * at : 4 * at + 4]
        x_ref, g_ref = inputs[2 * at : 2 * at + 2]
        x_coming, g_coming = [], []

        def load_x(block):
            columns = slice(x_from + X_BLOCK * block, x_from + X_BLOCK * (block + 1))
            place_at = slice(X_BLOCK * block, X_BLOCK * (block + 1))
            x_coming.append(
                (
                    loads.start(own_x.at[:, columns], x_ref.at[first, place_at]),
                    loads.start(other_x.at[:, columns], x_ref.at[second, place_at]),
                )
            )

        load_x(0)
        for begin, width in g_blocks(g_count):
            columns = slice(g_from + begin, g_from + begin + width)
            place_at = slice(begin, begin + width)
            g_coming.append(
                (
                    loads.start(own_g.at[0:ROWS, columns], g_ref.at[first, place_at]),
                    loads.start(other_g.at[0:ROWS, columns], g_ref.at[second, place_at]),
                )
            )
        for block in range(1, x_count // X_BLOCK):
            load_x(block)
        coming.append((x_coming, g_coming))
    if with_sums:
        below = slice(ROWS, ROWS + SUMS)
        sums_coming = (
            loads.start(sources[2].at[below, 0:D], own_sums),
            loads.start(sources[3].at[below, 0:D], other_sums),
        )
    leaving = []

    def leave(part, begin, width):
        columns = slice(begin, begin + width)
        source = stage.at[part, :, columns]
        sem = out_sems.at[len(leaving)]
        position = hop_position(parts, core_orders, part, place, core)

        @pl.when(position >= half)
        def _():
            pltpu.make_async_copy(source, sent.at[position - half, :, columns], sem).start()

        @pl.when(position < half)
        def _():
            pltpu.make_async_copy(source, kept.at[position, :, columns], sem).start()

        leaving.append(pltpu.make_async_copy(source, kept.at[0, :, columns], sem))

    done = 0
    for at, (x_from, x_count, g_from, g_count) in enumerate(products):
        x_ref, g_ref = inputs[2 * at : 2 * at + 2]
        x_coming, g_coming = coming[at]
        share = x_count // parts
        pieces = share // rows
        count = X_BLOCK // share
        for block in range(x_count // X_BLOCK):
            wait_all(x_coming[block])
            for (first_g, width), arriving in zip(g_blocks(g_count), g_coming):
                if block == 0:
                    wait_all(arriving)
                total = dot_tn(
                    x_ref[:, X_BLOCK * block : X_BLOCK * (block + 1)], g_ref[:, first_g : first_g + width]
                ).astype(BF16)
                total = total.reshape(count, pieces, rows, width)
                for piece in range(pieces):
                    begin = done + g_count * piece + first_g
                    stage[count * block : count * (block + 1), :, begin : begin + width] = total[:, piece]
            for part in range(count * block, count * (block + 1)):
                leave(part, done, g_count * pieces)
        done += g_count * pieces
    if with_sums:
        wait_all(sums_coming)
        width = D // parts
        sums = own_sums[...].astype(F32) + other_sums[...].astype(F32)
        begin = sum(g_count for _, _, _, g_count in products)
        half_wide = FF // parts // 2
        block_ref[...] = jnp.zeros_like(block_ref)
        for part in range(parts):
            block_ref[0:16, 0:width] = sums[0:16, width * part : width * (part + 1)]
            for layer in range(2):
                for side in range(2):
                    column = half_wide * (2 * part + side)
                    row = 16 + 4 * layer + column // D
                    to = 16 + 2 * layer + side
                    block_ref[to : to + 1, 0:half_wide] = sums[
                        row : row + 1, column % D : column % D + half_wide
                    ]
            stage[part, 0:SUMS, begin : begin + 128] = block_ref[...].astype(BF16)
            leave(part, begin, 128)
    wait_all(leaving)


def plain_weight_kernel(own_x, other_x, own_g, other_g, out):
    total = dot_tn(own_x[...], own_g[...]) + dot_tn(other_x[...], other_g[...])
    out[...] = total.astype(BF16)


def add_kernel(*refs):
    total = 0.0
    for ref in refs[:-1]:
        total = total + ref[...].astype(F32)
    refs[-1][...] = total.astype(refs[-1].dtype)


def finish_kernel(layers, splits, parts, terms, outs):
    for layer, columns in enumerate(layers):
        total = 0.0
        for ref, first in terms[layer]:
            total = total + ref[0, :, first : first + columns].astype(F32)
        rows = total.shape[0]
        for out, (begin, count) in zip(outs, splits):
            for piece in range(out.shape[1] // rows):
                at = begin + count * piece
                out[layer, rows * piece : rows * (piece + 1), :] = total[:, at : at + count]
        if parts is not None and layer == 0:
            sums = total[0:SUMS, columns - 128 : columns]
            width = D // parts
            for to in range(2):
                for out, row in zip(outs[len(splits) :], (0, 1, 4, 2, 3, 5, 6, 7)):
                    row += 8 * to
                    out[to : to + 1, :] = sums[row : row + 1, 0:width]
                half_wide = FF // parts // 2
                for side in range(2):
                    row = 16 + 2 * to + side
                    outs[-1][to : to + 1, half_wide * side : half_wide * (side + 1)] = sums[
                        row : row + 1, 0:half_wide
                    ]


def assemble_kernel(tokens, came_tokens, tokens_out):
    tokens_out[...] = gather_back(tokens[...], came_tokens[...], lax.axis_index("seq"))


ANY = pl.BlockSpec(memory_space=pl.ANY)
FAR = pl.BlockSpec(memory_space=pltpu.HBM)
def shaped(*dims, dtype=BF16):
    return jax.ShapeDtypeStruct(dims, dtype)


def held(*dims, dtype=BF16):
    return pltpu.VMEM(dims, dtype)


def sems(count):
    return pltpu.SemaphoreType.DMA((count,))


def whole(shape):
    return pl.BlockSpec(shape, lambda: (0,) * len(shape))


EXPECTED_US = {
    "ahead": 33.0, "down1": 6.4, "up1": 6.6, "qkv1": 0.05, "down0": 6.4, "up0": 6.6, "qkv0": 0.05, "back1": 20.0,
    "back0": 13.6, "assemble": 3.3,
}


def expected(name):
    time = 4.0 * EXPECTED_US.get(name, 2.0)
    return pl.CostEstimate(flops=int(time * 1.15e9), bytes_accessed=int(time * 3.69e6), transcendentals=0)


def call(kernel, name, operands, outs, scratch, lens=None, after=(), carry=(), out_specs=None):
    first = [] if lens is None else [lens]
    first_specs = [] if lens is None else [pl.BlockSpec(memory_space=pltpu.SMEM)]
    skip = len(first) + len(after) + len(carry)
    inputs = skip + len(operands)

    def body(*refs):
        kernel(
            *refs[: len(first)], *refs[skip:inputs], *refs[inputs : inputs + len(outs)],
            *refs[inputs + len(outs) + len(carry) :],
        )

    return pl.pallas_call(
        body,
        in_specs=first_specs
        + [ANY] * (len(after) + len(carry))
        + [whole(array.shape) if near else ANY for array, near in operands],
        out_specs=(out_specs or [ANY] * len(outs)) + [ANY] * len(carry),
        out_shape=list(outs) + [shaped(*array.shape, dtype=array.dtype) for array in carry],
        input_output_aliases={len(first) + len(after) + at: len(outs) + at for at in range(len(carry))},
        scratch_shapes=list(scratch),
        compiler_params=pltpu.CompilerParams(vmem_limit_bytes=VMEM_LIMIT),
        cost_estimate=expected(name),
        name=name,
    )(*first, *after, *carry, *(array for array, _ in operands))


def near(*arrays):
    return [(array, True) for array in arrays]


def far(*arrays):
    return [(array, False) for array in arrays]


AHEAD = (
    ("hidden0", ROWS, D, BF16), ("xs0", ROWS, XS, BF16), ("joint0", ROWS, 3 * D, BF16), ("log0", ROWS, 128, F32),
    ("middle0", ROWS, D, F32), ("slope0", ROWS, FF, BF16), ("hidden1", ROWS, D, F32), ("xs1", ROWS, 3 * D, BF16),
    ("joint1", ROWS, 3 * D, BF16), ("log1", ROWS, 128, F32), ("active1", ROWS, FF, BF16), ("middle1", ROWS, D, F32),
    ("moved_middle1", MOVED, D, F32),
    ("grad_own1", ROWS, D // 2, BF16), ("grad_other1", ROWS, D // 2, BF16), ("own1", ROWS, GS, BF16),
    ("sent1", ROWS, GS, BF16), ("mid1", ROWS, D, F32), ("grad_merged1", ROWS, D, BF16), ("sums_b1", 8, D, F32),
)


def ahead(lens, tokens, came, cot, came_cot, vectors, matrices):
    direct = ("moved_middle1", "grad_own1", "grad_other1", "own1", "sent1")
    outs = call(
        ahead_kernel, "ahead", near(tokens, came, cot, came_cot, *vectors) + far(*matrices),
        [shaped(r, c, dtype=t) for _, r, c, t in AHEAD],
        [held(8, 128) if name in direct else held(r, c, dtype=t) for name, r, c, t in AHEAD]
        + [held(ROWS, FF), held(ROWS, D), held(ROWS, D), held(ROWS, FF), held(ROWS, D),
           held(16, D, BLOCK), sems(24), sems(24)],
        lens=lens,
    )
    return {name: out for (name, *_), out in zip(AHEAD, outs)}


def last_forward(active, came_active, middle, came_middle, down_w, down_b, after=()):
    return call(
        result_kernel, "result", near(down_b) + far(active, came_active, middle, came_middle, down_w),
        [shaped(HALF, D)],
        [held(ROWS, FF), held(MOVED, FF), held(ROWS, D, dtype=F32), held(MOVED, D, dtype=F32), held(FF, D),
         sems(3 * FFB + 2)],
        after=after, out_specs=[whole((HALF, D))],
    )[0]


def back1(lens, operands, gain1, gain2, matrices, after=()):
    sums = shaped(8, D, dtype=F32)
    return call(
        back1_kernel, "back1", near(gain1, gain2) + far(*matrices, *operands),
        [shaped(ROWS, JS + D // 2), shaped(ROWS, JS + D // 2), shaped(ROWS, GS), shaped(ROWS, GS),
         shaped(ROWS, D, dtype=F32), shaped(ROWS, D), sums, sums],
        [held(ROWS, 3 * D), held(ROWS, D), held(ROWS, 128, dtype=F32), held(ROWS, D, dtype=F32),
         held(ROWS, D, dtype=F32), held(ROWS, FF), held(ROWS, D, dtype=F32), held(ROWS, 3 * D),
         held(8, D, dtype=F32), held(ROWS, D), held(ROWS, D, dtype=F32), held(ROWS, FF), held(ROWS, D, dtype=F32),
         held(ROWS, D), held(ROWS, D), held(8, D, dtype=F32),
         held(4 + 2 * FFB, D, BLOCK), sems(11 + 2 * FFB), sems(12)],
        lens=lens, after=after,
    )


def back0(lens, operands, gain1, sums, qkv_w, after=()):
    return call(
        back0_kernel, "back0", near(gain1, *sums) + far(qkv_w, *operands),
        [shaped(ROWS + SUMS, JS), shaped(ROWS + SUMS, JS), shaped(ROWS, D), shaped(MOVED, D)],
        [held(ROWS, 3 * D), held(ROWS, D), held(ROWS, 128, dtype=F32), held(ROWS, D), held(ROWS, D, dtype=F32),
         held(ROWS, 3 * D), held(SUMS, D, dtype=F32), held(SUMS, D), held(ROWS, D), held(3, D, BLOCK), sems(8),
         sems(6)],
        lens=lens, after=after,
    )


def add(sums, begin, count, name, after=(), carry=()):
    arrays = []
    for _, terms in sums:
        for array, _ in terms:
            if not any(array is seen for seen in arrays):
                arrays.append(array)
    index = {id(array): at for at, array in enumerate(arrays)}
    share = arrays[0].shape[1]
    total = sum(columns for columns, _ in sums)
    skip = len(after) + len(carry)
    pieces = min(count, 2)
    size = count // pieces

    places = [
        (at, index[id(array)], first, columns)
        for at, (columns, terms) in enumerate(sums)
        for array, first in terms
    ]

    def body(*refs):
        sources, refs = refs[skip : skip + len(arrays)], refs[skip + len(arrays) :]
        out, *refs = refs[:1] + refs[1 + len(carry) :]
        *buffers, total_ref, load_sems, out_sems = refs
        loads, stores = Copies(load_sems), Copies(out_sems)
        coming, leaving = [], []
        for piece in range(pieces):
            parts_of = slice(size * piece, size * (piece + 1))
            coming.append(
                [
                    loads.start(
                        sources[source].at[begin + size * piece : begin + size * (piece + 1), :, first : first + columns],
                        buffer.at[parts_of],
                    )
                    for (_, source, first, columns), buffer in zip(places, buffers)
                ]
            )
        for piece in range(pieces):
            parts_of = slice(size * piece, size * (piece + 1))
            wait_all(coming[piece])
            done = 0
            for at, (columns, _) in enumerate(sums):
                value = 0.0
                for (which, *_), buffer in zip(places, buffers):
                    if which == at:
                        value = value + buffer[parts_of].astype(F32)
                total_ref[parts_of, :, done : done + columns] = value.astype(BF16)
                done += columns
            leaving.append(stores.start(total_ref.at[parts_of], out.at[parts_of]))
        wait_all(leaving)

    return pl.pallas_call(
        body,
        in_specs=[ANY] * skip + [FAR] * len(arrays),
        out_specs=[FAR] + [ANY] * len(carry),
        out_shape=[shaped(count, share, total)]
        + [shaped(*array.shape, dtype=array.dtype) for array in carry],
        input_output_aliases={len(after) + at: 1 + at for at in range(len(carry))},
        scratch_shapes=[held(count, share, columns) for *_, columns in places]
        + [held(count, share, total), sems(pieces * len(places)), sems(pieces)],
        compiler_params=pltpu.CompilerParams(vmem_limit_bytes=VMEM_LIMIT),
        cost_estimate=expected(name),
        name=name,
    )(*after, *carry, *arrays)


def swap(array):
    return lax.ppermute(array, "seq", [(0, 1), (1, 0)])


EVEN = ((0, 2, 1, 3), (1, 2, 0, 3))
LATE = ((0, 1, 2, 3), (1, 0, 2, 3))


class Halving:
    def __init__(self, name, kept, orders):
        self.name, self.orders = name, orders
        self.hop = 0
        self.columns = kept.shape[2]
        self.terms = [(kept, 0)]


def send(halvings, sent):
    hop, orders = halvings[0].hop, halvings[0].orders
    pairs = []
    for place in range(lax.axis_size("dp")):
        for core in range(2):
            other = place ^ (1 << orders[core][hop])
            pairs.append((2 * place + core, 2 * other + core))
    came = lax.ppermute(sent, ("dp", "seq"), pairs)
    first = 0
    for halving in halvings:
        halving.terms.append((came, first))
        halving.hop += 1
        first += halving.columns
    return came


def weight_gradient(name, operands, products, orders, with_sums, after=(), carry=()):
    parts = lax.axis_size("dp")
    columns = sum(g_count * (x_count // D) for _, x_count, _, g_count in products) + (128 if with_sums else 0)
    share = D // parts
    scratch = []
    copies = 2
    for _, x_count, _, g_count in products:
        scratch += [held(2 * ROWS, x_count), held(2 * ROWS, g_count)]
        copies += 2 * len(g_blocks(g_count)) + 2 * (x_count // X_BLOCK)
    if with_sums:
        scratch += [held(SUMS, D), held(SUMS, D), held(SUMS, 128, dtype=F32)]
    return call(
        lambda *refs: weight_kernel(parts, orders, products, with_sums, *refs), name, far(*operands),
        [shaped(parts // 2, share, columns)] * 2,
        scratch
        + [held(parts, share, columns), sems(copies), sems(parts * (len(products) + int(with_sums)))],
        after=after, carry=carry,
    )


def finish(name, groups, after=()):
    arrays = []
    for halvings, _, _ in groups:
        for halving in halvings:
            for array, _ in halving.terms:
                if not any(array is seen for seen in arrays):
                    arrays.append(array)
    index = {id(array): at for at, array in enumerate(arrays)}
    outs, counts = [], []
    for _, splits, parts in groups:
        mine = [shaped(2, rows, count, dtype=F32) for _, count, rows in splits]
        if parts is not None:
            mine += [shaped(2, D // parts, dtype=F32)] * 8 + [shaped(2, FF // parts, dtype=F32)]
        outs += mine
        counts.append(len(mine))
    places = [
        (index[id(array)], first, halving.columns)
        for halvings, _, _ in groups
        for halving in halvings
        for array, first in halving.terms
    ]

    def body(*refs):
        sources, refs = refs[len(after) : len(after) + len(arrays)], refs[len(after) + len(arrays) :]
        results, refs = refs[: len(outs)], refs[len(outs) :]
        *buffers, load_sems = refs
        loads = Copies(load_sems)
        coming = [
            loads.start(sources[source].at[0:1, :, first : first + columns], buffer)
            for (source, first, columns), buffer in zip(places, buffers)
        ]
        used = 0
        for (halvings, splits, parts), count in zip(groups, counts):
            terms = []
            for halving in halvings:
                wait_all(coming[used : used + len(halving.terms)])
                terms.append([(buffer, 0) for buffer in buffers[used : used + len(halving.terms)]])
                used += len(halving.terms)
            finish_kernel(
                [halving.columns for halving in halvings], [split[:2] for split in splits], parts, terms,
                results[:count],
            )
            results = results[count:]

    return pl.pallas_call(
        body,
        in_specs=[ANY] * len(after) + [FAR] * len(arrays),
        out_specs=[whole(out.shape) for out in outs],
        out_shape=outs,
        scratch_shapes=[held(1, arrays[0].shape[1], columns) for *_, columns in places] + [sems(len(places))],
        compiler_params=pltpu.CompilerParams(vmem_limit_bytes=VMEM_LIMIT),
        cost_estimate=expected(name),
        name=name,
    )(*after, *arrays)


def plain_weight_gradient(name, own_x, other_x, own_g, other_g):
    rows, columns = own_x.shape[1], own_g.shape[1]
    x_spec = pl.BlockSpec((ROWS, BLOCK), lambda step: (0, step))
    g_spec = pl.BlockSpec((ROWS, columns), lambda step: (0, 0))
    return pl.pallas_call(
        plain_weight_kernel,
        grid=(rows // BLOCK,),
        in_specs=[x_spec, x_spec, g_spec, g_spec],
        out_specs=pl.BlockSpec((BLOCK, columns), lambda step: (step, 0)),
        out_shape=shaped(rows, columns),
        compiler_params=pltpu.CompilerParams(vmem_limit_bytes=VMEM_LIMIT),
        name=name,
    )(own_x, other_x, own_g, other_g)


def plain_halving(total, bit_order):
    parts = lax.axis_size("dp")
    place = lax.axis_index("dp")
    bits = parts.bit_length() - 1
    total = total.reshape((2,) * bits + (total.shape[0] // parts, total.shape[1]))
    left = list(range(bits))[::-1]
    terms = [total]
    for bit in bit_order:
        axis = left.index(bit)
        left.remove(bit)
        mine = (place >> bit) & 1
        sent = sum(lax.dynamic_index_in_dim(t, 1 - mine, axis, keepdims=False).astype(F32) for t in terms)
        terms = [lax.dynamic_index_in_dim(t, mine, axis, keepdims=False) for t in terms]
        terms.append(
            lax.ppermute(sent.astype(BF16), "dp", [(i, i ^ (1 << bit)) for i in range(parts)])
        )
    return sum(t.astype(F32) for t in terms)


def sum_everywhere(array):
    total = array + swap(array)
    parts = lax.axis_size("dp")
    for bit in range(parts.bit_length() - 1):
        total = total + lax.ppermute(total, "dp", [(i, i ^ (1 << bit)) for i in range(parts)])
    return total


def shards(
    tokens, crop_len, qkv_weight, query_bias, value_bias, out_weight, out_bias, first_gain, first_shift,
    second_gain, second_shift, up_weight, up_bias, down_weight, down_bias, cotangent,
):
    parts = lax.axis_size("dp")
    lens = crop_len.reshape(-1)
    core = lax.axis_index("seq")
    tiled = parts == 16
    matrices = (out_weight, up_weight, down_weight)
    came_tokens = swap(tokens)
    came_cot = swap(cotangent)
    kept = ahead(
        lens, tokens, came_tokens, cotangent, came_cot,
        (first_gain, first_shift, query_bias, value_bias, out_bias, second_gain, second_shift, up_bias, down_bias),
        (qkv_weight,) + matrices,
    )
    reductions = {}

    def product(name, operands, products, after=(), carry=(), with_sums=False, orders=EVEN):
        if not tiled:
            totals = []
            for at, (x_from, x_count, g_from, g_count) in enumerate(products):
                own_x, other_x, own_g, other_g = operands[4 * at : 4 * at + 4]
                x_at, g_at = slice(x_from, x_from + x_count), slice(g_from, g_from + g_count)
                total = plain_weight_gradient(
                    name, own_x[:, x_at], other_x[:, x_at], own_g[:ROWS, g_at], other_g[:ROWS, g_at]
                )
                totals.append(plain_halving(total, range(parts.bit_length() - 1)))
            reductions[name] = totals
            return (total, *carry)
        here, gone, *carried = weight_gradient(name, operands, products, orders, with_sums, after, carry)
        reductions[name] = Halving(name, here, orders)
        send([reductions[name]], gone)
        return (gone, *carried)

    def step(names, after=(), carry=()):
        if not tiled:
            return (*(after or (tokens,))[:1], *carry)
        group = [reductions[name] for name in names.split()]
        hop = group[0].hop
        count = parts >> (hop + 1)
        sums = [(halving.columns, halving.terms) for halving in group]
        sent, *carried = add(sums, count, count, "_".join(names.split()) + f"_hop{hop}", after, carry)
        send(group, sent)
        return (sent, *carried)

    def arrived(name):
        return (reductions[name].terms[-1][0],) if tiled else ()

    active1, xs1, xs0 = kept["active1"], kept["xs1"], kept["xs0"]
    own1, sent1 = kept["own1"], kept["sent1"]
    came_active1 = swap(active1)
    came_gs1 = swap(sent1)
    came_xs1 = swap(xs1)
    came_middle1 = swap(kept["moved_middle1"])
    last, xs0 = product(
        "down1", (active1, came_active1, kept["grad_own1"], kept["grad_other1"]), ((0, FF, 0, D // 2),),
        carry=(xs0,),
    )
    came_xs0 = swap(xs0)
    (last,) = product(
        "up1", (xs1, came_xs1, own1, came_gs1, xs1, came_xs1, own1, came_gs1),
        ((LOW2, D, 0, FF // 2), (MERGED, D, FF // 2, D // 2)), after=(last, came_middle1),
    )
    own_j1, sent_j1, own_g0, sent_g0, mid0, grad_merged0, sums_a1, sums_b0 = back1(
        lens,
        (kept["joint1"], kept["grad_merged1"], kept["log1"], kept["hidden1"], kept["mid1"], kept["slope0"],
         kept["middle0"]),
        first_gain, second_gain, (qkv_weight,) + matrices, after=(last,),
    )
    last, sent_j1, sent_g0 = step("down1", after=(own_j1,), carry=(sent_j1, sent_g0))
    came_j1 = swap(sent_j1)
    came_g0 = swap(sent_g0)
    (last,) = product(
        "qkv1", (xs1, came_xs1, own_j1, came_j1), ((LOW1, D, 0, JS),), after=(last,)
    )
    (last,) = step("up1", after=(last,))
    (last,) = product("down0", (xs0, came_xs0, own_j1, came_j1), ((0, FF, JS, D // 2),), after=(last,))
    (last,) = product(
        "up0", (xs0, came_xs0, own_g0, came_g0, xs0, came_xs0, own_g0, came_g0),
        ((FF + LOW2, D, 0, FF // 2), (FF + MERGED, D, FF // 2, D // 2)), after=(last,), orders=EVEN,
    )
    (last,) = step("qkv1", after=(last,))
    own_j0, sent_j0, grad_tokens, moved_tokens = back0(
        lens, (kept["joint0"], grad_merged0, kept["log0"], kept["hidden0"], mid0), first_gain,
        (sums_b0, sums_a1, kept["sums_b1"]), qkv_weight, after=(last,),
    )
    last, sent_j0 = step("down0", after=(own_j0,) + arrived("qkv1"), carry=(sent_j0,))
    came_j0 = swap(sent_j0)
    (last,) = step("down1 up1", after=(last,))
    (last,) = product(
        "qkv0", (xs0, came_xs0, own_j0, came_j0), ((FF + LOW1, D, 0, JS),), after=(last,), with_sums=True, orders=LATE,
    )
    (last,) = step("up0", after=(last,))
    last, moved_tokens = step("down1 up1", after=(last,), carry=(moved_tokens,))
    came_tokens = swap(moved_tokens)
    (last,) = step("qkv1 down0", after=(last,))
    (last,) = step("qkv0", after=(last, came_tokens))
    (last,) = step("qkv1 down0", after=(last,))
    (last,) = step("qkv0", after=(last,))
    (last,) = step("up0", after=(last,))
    (grad_tokens,) = call(
        assemble_kernel, "assemble", near(grad_tokens, came_tokens), [shaped(HALF, D)], [],
        out_specs=[whole((HALF, D))], after=(last,),
    )
    (last,) = step("up0", after=(grad_tokens,))
    (last,) = step("qkv0", after=(last,))
    result = last_forward(
        active1, came_active1, kept["middle1"], came_middle1, down_weight, down_bias, after=(last,)
    )
    if tiled:
        share = D // parts

        def layers(name):
            return reductions[name + "0"], reductions[name + "1"]

        down_g, qkv_g, *vectors, up_g, out_g = finish(
            "finish",
            (
                (layers("down"), ((0, D // 2, FF // parts),), None),
                (layers("qkv"), ((0, JS, share),), parts),
                (layers("up"), ((0, FF // 2, share), (FF // 2, D // 2, share)), None),
            ),
            after=(result,),
        )
    else:
        down_g, up_g, out_g, qkv_g = (
            jnp.stack([reductions[name + "0"][at], reductions[name + "1"][at]])
            for name, at in (("down", 0), ("up", 0), ("up", 1), ("qkv", 0))
        )
        total = sum_everywhere(own_j0[ROWS:, :D].astype(F32))
        place = lax.axis_index("dp")
        width = D // parts
        narrow = lax.dynamic_slice(total[:16], (0, place * width), (16, width)).reshape(2, 8, width)
        vectors = [narrow[:, row] for row in (0, 1, 4, 2, 3, 5, 6, 7)]
        vectors.append(
            lax.dynamic_slice(total[16:24].reshape(2, FF), (0, place * (FF // parts)), (2, FF // parts))
        )
    query_b, value_b, out_b, gain1, shift1, gain2, shift2, down_b, up_b = vectors
    return (
        result, grad_tokens, qkv_g, query_b, value_b, out_g, out_b, gain1, shift1, gain2, shift2, up_g, up_b, down_g,
        down_b,
    )


def solution(mesh):
    rows = P(("dp", "seq"), None)
    matrix = P(None, "dp", "seq")
    narrow = P(None, "dp")
    return jax.shard_map(
        shards,
        mesh=mesh,
        in_specs=(rows, P("dp", None)) + (P(),) * 13 + (rows,),
        out_specs=(
            rows, rows, matrix, narrow, narrow, matrix, narrow, narrow, narrow, narrow, narrow, matrix, narrow,
            matrix, narrow,
        ),
        check_vma=False,
    )
```

```python
import jax
import jax.numpy as jnp
from jax import lax
from jax.experimental import pallas as pl
from jax.experimental.pallas import tpu as pltpu
from jax.sharding import PartitionSpec as P

HD = 64
GPAD = 198
LPAD = 38
HALF = 350
SPLIT = HALF - GPAD
REST = GPAD - SPLIT
WIDE = 208
SLOT = 40
LOCALS = 4
ROWS = WIDE + SLOT * LOCALS
MOVED = SLOT * LOCALS
HEADS = 12
D = 768
FF = 3072
BLOCK = 768
FFB = FF // BLOCK
X_BLOCK = 768
G_BLOCK = 1536

EPS = 1e-06
MASKED = -1e30
SCALE = HD ** (-0.5)
BF16 = jnp.bfloat16
F32 = jnp.float32

VMEM_LIMIT = 64 * 1024 * 1024 - 64 * 1024


def dot(left, right):
    return jnp.dot(left, right, preferred_element_type=F32)


def dot_nt(left, right):
    return lax.dot_general(left, right, (((1,), (1,)), ((), ())), preferred_element_type=F32)


def dot_tn(left, right):
    return lax.dot_general(left, right, (((0,), (0,)), ((), ())), preferred_element_type=F32)


def normal_parts(values):
    mass = 0.5 + 0.5 * lax.erf(values * 0.7071067811865476)
    return mass, jnp.exp(-0.5 * values * values) * 0.3989422804014327


def norm_parts(hidden):
    row_mean = jnp.mean(hidden, axis=-1, keepdims=True)
    centered = hidden - row_mean
    inverse = lax.rsqrt(jnp.mean(centered * centered, axis=-1, keepdims=True) + EPS)
    return centered * inverse, inverse


def norm_back(upstream, normed, inverse, norm_gain):
    scaled = upstream * norm_gain
    centered = scaled - jnp.mean(scaled, axis=-1, keepdims=True)
    centered = centered - normed * jnp.mean(scaled * normed, axis=-1, keepdims=True)
    return centered * inverse


def column_sum(array):
    return jnp.sum(array.astype(F32), axis=0, keepdims=True)


def slot_row(position):
    crop = jnp.zeros_like(position)
    for at in range(1, LOCALS):
        crop = crop + (position >= SLOT * at).astype(jnp.int32)
    inner = position - SLOT * crop
    return jnp.where((position >= 0) & (inner < LPAD), LPAD * crop + inner, -4 * HALF)


def spread(own, came, core):
    position = lax.broadcasted_iota(jnp.int32, (ROWS, HALF), 0)
    column = lax.broadcasted_iota(jnp.int32, (ROWS, HALF), 1)
    local = slot_row(position - WIDE)
    own0 = jnp.where(position < GPAD, position, -1)
    came0 = local + REST
    own1 = jnp.where(
        (position >= SPLIT) & (position < GPAD), position - SPLIT, local + GPAD
    )
    came1 = jnp.where(position < SPLIT, position + GPAD, -1)
    own_from = own0 * (1 - core) + own1 * core
    came_from = came0 * (1 - core) + came1 * core
    return dot(jnp.where(own_from == column, 1.0, 0.0).astype(BF16), own) + dot(
        jnp.where(came_from == column, 1.0, 0.0).astype(BF16), came
    )


def gather_back(own, came, core):
    row = lax.broadcasted_iota(jnp.int32, (HALF, ROWS), 0)
    position = lax.broadcasted_iota(jnp.int32, (HALF, ROWS), 1)
    local = slot_row(position - WIDE)
    own0 = jnp.where(position < GPAD, position, -1)
    own1 = jnp.where(
        (position >= SPLIT) & (position < GPAD), position - SPLIT, local + GPAD
    )
    own_to = own0 * (1 - core) + own1 * core
    came_row = lax.broadcasted_iota(jnp.int32, (HALF, MOVED), 0)
    came_position = lax.broadcasted_iota(jnp.int32, (HALF, MOVED), 1)
    came0 = jnp.where(came_position < SPLIT, came_position + GPAD, -1)
    came1 = slot_row(came_position) + REST
    came_to = came0 * (1 - core) + came1 * core
    return (
        dot(jnp.where(own_to == row, 1.0, 0.0).astype(BF16), own)
        + dot(jnp.where(came_to == came_row, 1.0, 0.0).astype(BF16), came)
    ).astype(BF16)


def head_lanes():
    lane = lax.broadcasted_iota(jnp.int32, (1, 2 * HD), 1)
    left = jnp.where(lane < HD, 1.0, 0.0)
    return (left.astype(BF16), (1.0 - left).astype(BF16)), (
        (left * SCALE).astype(BF16),
        ((1.0 - left) * SCALE).astype(BF16),
    )


def both_heads(array, masks):
    return jnp.concatenate([array * masks[0], array * masks[1]], axis=0)


def own_lanes(stacked):
    rows = stacked.shape[0] // 2
    lane = lax.broadcasted_iota(jnp.int32, (rows, 2 * HD), 1)
    return jnp.where(lane < HD, stacked[:rows], stacked[rows:])


def pair(at, block):
    return slice(block * D + 2 * HD * at, block * D + 2 * HD * (at + 1))


def windows(lens_ref, core, pieces):
    column = lax.broadcasted_iota(jnp.int32, (2 * WIDE, WIDE), 1)
    plan = [(slice(0, WIDE), column < lens_ref[core])]
    count = LOCALS // pieces
    size = SLOT * count
    row = lax.broadcasted_iota(jnp.int32, (2 * size, size), 0)
    row = jnp.where(row >= size, row - size, row)
    column = lax.broadcasted_iota(jnp.int32, (2 * size, size), 1)
    for piece in range(pieces):
        allowed = None
        for at in range(count):
            begin = SLOT * at
            end = begin + lens_ref[2 + LOCALS * core + count * piece + at]
            mine = (row >= begin) & (row < begin + SLOT) & (column >= begin) & (column < end)
            allowed = mine if allowed is None else allowed | mine
        begin = WIDE + size * piece
        plan.append((slice(begin, begin + size), allowed))
    return plan


TOGETHER, PIECES = 3, 2
TOGETHER_BACK, PIECES_BACK = 3, 2


def attend(lens_ref, core, joint_ref, merged_ref, log_ref):
    _, scaled = head_lanes()
    lane = lax.broadcasted_iota(jnp.int32, (1, 128), 1)
    plan = windows(lens_ref, core, PIECES)
    logs = [jnp.zeros((rows.stop - rows.start, 128), F32) for rows, _ in plan]
    for begin in range(0, HEADS // 2, TOGETHER):
        chains = [(which, at) for at in range(begin, begin + TOGETHER) for which in range(len(plan))]
        scores = []
        for which, at in chains:
            rows, allowed = plan[which]
            queries = both_heads(joint_ref[rows, pair(at, 0)], scaled)
            scores.append(jnp.where(allowed, dot_nt(queries, joint_ref[rows, pair(at, 1)]), MASKED))
        row_max = [jnp.max(array, axis=-1, keepdims=True) for array in scores]
        exponent = [jnp.exp(array - top) for array, top in zip(scores, row_max)]
        totals = [jnp.sum(array, axis=-1, keepdims=True) for array in exponent]
        weights = [(array * (1.0 / total)).astype(BF16) for array, total in zip(exponent, totals)]
        for (which, at), array, top, total in zip(chains, weights, row_max, totals):
            rows, _ = plan[which]
            merged_ref[rows, pair(at, 0)] = own_lanes(dot(array, joint_ref[rows, pair(at, 2)])).astype(BF16)
            log_totals = top + jnp.log(total)
            count = rows.stop - rows.start
            for side in range(2):
                logs[which] = jnp.where(
                    lane == 2 * at + side, log_totals[count * side : count * (side + 1)], logs[which]
                )
    for (rows, _), array in zip(plan, logs):
        log_ref[rows, :] = array


def attend_back(lens_ref, core, joint_ref, up_ref, log_ref, grad_ref):
    plain, scaled = head_lanes()
    plan = windows(lens_ref, core, PIECES_BACK)
    for begin in range(0, HEADS // 2, TOGETHER_BACK):
        chains = [(which, at) for at in range(begin, begin + TOGETHER_BACK) for which in range(len(plan))]
        queries, upstream, weights, grad_weights = [], [], [], []
        for which, at in chains:
            rows, allowed = plan[which]
            queries.append(both_heads(joint_ref[rows, pair(at, 0)], scaled))
            upstream.append(both_heads(up_ref[rows, pair(at, 0)], plain))
            log_total = jnp.concatenate(
                [log_ref[rows, 2 * at + side : 2 * at + side + 1] for side in range(2)], axis=0
            )
            scores = jnp.where(allowed, dot_nt(queries[-1], joint_ref[rows, pair(at, 1)]), MASKED)
            weights.append(jnp.exp(scores - log_total))
            grad_weights.append(dot_nt(upstream[-1], joint_ref[rows, pair(at, 2)]))
        weighted = [one * two for one, two in zip(weights, grad_weights)]
        row_dot = [jnp.sum(array, axis=-1, keepdims=True) for array in weighted]
        grad_scores = [
            (array - one * dots).astype(BF16) for array, one, dots in zip(weighted, weights, row_dot)
        ]
        for (which, at), scores, one, query, up in zip(chains, grad_scores, weights, queries, upstream):
            rows, _ = plan[which]
            grad_ref[rows, pair(at, 2)] = dot_tn(one.astype(BF16), up).astype(BF16)
            grad_ref[rows, pair(at, 0)] = (
                own_lanes(dot(scores, joint_ref[rows, pair(at, 1)])) * SCALE
            ).astype(BF16)
            grad_ref[rows, pair(at, 1)] = dot_tn(scores, query).astype(BF16)


class Copies:
    def __init__(self, sems):
        self.sems = sems
        self.started = 0

    def start(self, source, target):
        copy = pltpu.make_async_copy(source, target, self.sems.at[self.started])
        self.started += 1
        copy.start()
        return copy


def wait_all(copies):
    for copy in copies:
        copy.wait()


def columns_of(ref, at):
    return ref.at[:, BLOCK * at : BLOCK * (at + 1)]


def core_half(ref, core):
    width = ref.shape[1] // 2
    return ref.at[:, pl.ds(pl.multiple_of(core * width, 128), width)]


def moved_rows(ref, core):
    return ref.at[pl.ds(pl.multiple_of(WIDE * (1 - core), 16), MOVED), :]


def vector(ref, layer):
    return ref[layer : layer + 1, :]


XS = FF + 3 * D
LOW2, MERGED, LOW1 = 0, D, 2 * D
GS = FF // 2 + D // 2
JS = 3 * D // 2
SUMS = 32


def ahead_kernel(
    lens, tokens, came, cot, came_cot, gain1, shift1, query_b, value_b, out_b, gain2, shift2, up_b, down_b,
    qkv_w, out_w, up_w, down_w, *refs,
):
    count = len(AHEAD)
    outs, held = refs[:count], refs[count : 2 * count]
    out_of = dict(zip((name for name, *_ in AHEAD), outs))
    ref_of = dict(zip((name for name, *_ in AHEAD), held))
    slope_ref, grad_ref, other_ref, grad_up_ref, branch_ref, *refs = refs[2 * count :]
    weights, weight_sems, out_sems = refs
    core = lax.axis_index("seq")
    loads = Copies(weight_sems)
    stores = Copies(out_sems)
    leaving = []

    def leave(name):
        leaving.append(stores.start(ref_of[name], out_of[name]))

    def load_columns(ref, layer, blocks, slot):
        return [loads.start(columns_of(ref.at[layer], at), weights.at[slot + at]) for at in range(blocks)]

    def load_rows(ref, layer, blocks, slot):
        return [
            loads.start(ref.at[layer, BLOCK * at : BLOCK * (at + 1), :], weights.at[slot + at])
            for at in range(blocks)
        ]

    qkv = load_columns(qkv_w, 0, 3, 0)
    out = load_rows(out_w, 0, 1, 3)
    ups = load_columns(up_w, 0, FFB, 4)
    downs = load_rows(down_w, 0, FFB, 8)
    next_qkv = load_columns(qkv_w, 1, 3, 12)
    next_out = load_rows(out_w, 1, 1, 15)

    hidden = spread(tokens[...], came[...], core)
    for layer in range(2):
        if layer == 0:
            low1_ref = ref_of["xs0"].at[:, FF + LOW1 : FF + LOW1 + D]
            low2_ref = ref_of["xs0"].at[:, FF + LOW2 : FF + LOW2 + D]
            merged_ref = ref_of["xs0"].at[:, FF + MERGED : FF + MERGED + D]
            active_ref = ref_of["xs0"].at[:, 0:FF]
            joint_ref, log_ref, mid_ref, gelu_slope_ref = (
                ref_of["joint0"], ref_of["log0"], ref_of["middle0"], ref_of["slope0"],
            )
            ref_of["hidden0"][...] = hidden.astype(BF16)
            leave("hidden0")
            slot = 0
        else:
            low1_ref = ref_of["xs1"].at[:, LOW1 : LOW1 + D]
            low2_ref = ref_of["xs1"].at[:, LOW2 : LOW2 + D]
            merged_ref = ref_of["xs1"].at[:, MERGED : MERGED + D]
            active_ref = ref_of["active1"]
            joint_ref, log_ref, mid_ref, gelu_slope_ref = ref_of["joint1"], ref_of["log1"], ref_of["middle1"], slope_ref
            ref_of["hidden1"][...] = hidden
            leave("hidden1")
            slot = 12
            qkv, out = next_qkv, next_out
            ups = load_columns(up_w, 1, FFB, 4)
            downs = load_rows(down_w, 1, FFB, 8)
        normed, _ = norm_parts(hidden)
        low1_ref[...] = (normed * vector(gain1, layer) + vector(shift1, layer)).astype(BF16)
        wait_all(qkv)
        for block, bias in enumerate((vector(query_b, layer), None, vector(value_b, layer))):
            joint = dot(low1_ref[...], weights[slot + block])
            if bias is not None:
                joint = joint + bias
            joint_ref[:, BLOCK * block : BLOCK * (block + 1)] = joint.astype(BF16)
        leave(f"joint{layer}")
        attend(lens, core, joint_ref, merged_ref, log_ref)
        leave(f"log{layer}")
        wait_all(out)
        middle = hidden + dot(merged_ref[...], weights[slot + 3]) + vector(out_b, layer)
        mid_ref[...] = middle
        leave(f"middle{layer}")
        if layer == 1:
            leaving.append(stores.start(moved_rows(mid_ref, core), out_of["moved_middle1"]))
        normed, _ = norm_parts(middle)
        low2_ref[...] = (normed * vector(gain2, layer) + vector(shift2, layer)).astype(BF16)
        if layer == 1:
            leave("xs1")
        wait_all(ups)
        for block in range(FFB):
            columns = slice(BLOCK * block, BLOCK * (block + 1))
            up_values = dot(low2_ref[...], weights[4 + block]) + up_b[layer : layer + 1, columns]
            mass, bell = normal_parts(up_values)
            active_ref[:, columns] = (up_values * mass).astype(BF16)
            gelu_slope_ref[:, columns] = (mass + up_values * bell).astype(BF16)
        leave("active1" if layer == 1 else "xs0")
        if layer == 0:
            leave("slope0")
        wait_all(downs)
        if layer == 0:
            hidden = mid_ref[...] + dot(active_ref[...], weights[8:12].reshape(FF, D)) + vector(down_b, layer)
    grad_ref[...] = spread(cot[...], came_cot[...], core).astype(BF16)
    other_ref[...] = spread(came_cot[...], cot[...], 1 - core).astype(BF16)
    leaving.append(stores.start(core_half(grad_ref, core), out_of["grad_own1"]))
    leaving.append(stores.start(core_half(other_ref, core), out_of["grad_other1"]))
    mlp_back_part(
        core, grad_ref[...], grad_ref[...].astype(F32), slope_ref, ref_of["middle1"], vector(gain2, 1),
        [weights[8 + at] for at in range(FFB)], [weights[4 + at] for at in range(FFB)], weights[15],
        grad_up_ref, branch_ref, ref_of["mid1"], ref_of["grad_merged1"], ref_of["sums_b1"], out_of["own1"],
        out_of["sent1"], out_of["mid1"], stores, leaving,
    )
    for name in ("grad_merged1", "sums_b1"):
        leave(name)
    wait_all(leaving)


def result_kernel(
    down_b, active, came_active, middle, came_middle, down_w, out,
    active_ref, came_active_ref, middle_ref, came_middle_ref, weights, load_sems,
):
    core = lax.axis_index("seq")
    loads = Copies(load_sems)
    coming = []
    for at in range(FFB):
        columns = slice(BLOCK * at, BLOCK * (at + 1))
        coming.append(
            (
                loads.start(down_w.at[1, columns, :], weights.at[columns, :]),
                loads.start(active.at[:, columns], active_ref.at[:, columns]),
                loads.start(moved_rows(came_active, 1 - core).at[:, columns], came_active_ref.at[:, columns]),
            )
        )
    rest = [loads.start(middle, middle_ref), loads.start(came_middle, came_middle_ref)]
    own = came = vector(down_b, 1)
    for at in range(FFB):
        columns = slice(BLOCK * at, BLOCK * (at + 1))
        wait_all(coming[at])
        own = own + dot(active_ref[:, columns], weights[columns, :])
        came = came + dot(came_active_ref[:, columns], weights[columns, :])
    wait_all(rest)
    own = (middle_ref[...] + own).astype(BF16)
    out[...] = gather_back(own, (came_middle_ref[...] + came).astype(BF16), core)


def mlp_back_part(
    core, grad, upstream, slope_ref, middle_ref, gain, downs, ups, out_weight, grad_up_ref, branch_ref, mid_ref,
    grad_merged_ref, sums_ref, own, sent, mid_out, stores, leaving,
):
    sums_ref[3:4, :] = column_sum(grad)
    back = 0.0
    for block in range(FFB):
        columns = slice(BLOCK * block, BLOCK * (block + 1))
        grad_up = (dot_nt(grad, downs[block]) * slope_ref[:, columns].astype(F32)).astype(BF16)
        grad_up_ref[:, columns] = grad_up
        sums_ref[4 + block : 5 + block, :] = column_sum(grad_up)
        back = back + dot_nt(grad_up, ups[block])
    leaving.append(stores.start(core_half(grad_up_ref, 1 - core), sent.at[:, 0 : FF // 2]))
    leaving.append(stores.start(core_half(grad_up_ref, core), own.at[:, 0 : FF // 2]))
    normed, inverse = norm_parts(middle_ref[...])
    sums_ref[1:2, :] = column_sum(back * normed)
    sums_ref[2:3, :] = column_sum(back)
    grad_mid = norm_back(back, normed, inverse, gain) + upstream
    mid_ref[...] = grad_mid
    leaving.append(stores.start(mid_ref, mid_out))
    branch = grad_mid.astype(BF16)
    branch_ref[...] = branch
    leaving.append(stores.start(core_half(branch_ref, 1 - core), sent.at[:, FF // 2 : GS]))
    leaving.append(stores.start(core_half(branch_ref, core), own.at[:, FF // 2 : GS]))
    sums_ref[0:1, :] = column_sum(branch)
    grad_merged_ref[...] = dot_nt(branch, out_weight).astype(BF16)


def attention_back_part(
    layer, lens, core, coming, qkv, held, gain1, weights, grad_joint_ref, sums_ref, sums_at, own, sent, stores, leaving
):
    joint_ref, up_ref, log_ref, hidden_ref, mid_ref = held
    wait_all(coming[:3])
    attend_back(lens, core, joint_ref, up_ref, log_ref, grad_joint_ref)
    leaving.append(stores.start(core_half(grad_joint_ref, 1 - core), sent.at[0:ROWS, 0:JS]))
    leaving.append(stores.start(core_half(grad_joint_ref, core), own.at[0:ROWS, 0:JS]))
    sums_ref[sums_at : sums_at + 1, :] = column_sum(grad_joint_ref[:, 0:D])
    sums_ref[sums_at + 1 : sums_at + 2, :] = column_sum(grad_joint_ref[:, 2 * D : 3 * D])
    wait_all(qkv)
    grad_first = 0.0
    for block in range(3):
        grad_first = grad_first + dot_nt(
            grad_joint_ref[:, BLOCK * block : BLOCK * (block + 1)], weights[block]
        )
    wait_all(coming[3:])
    normed, inverse = norm_parts(hidden_ref[...].astype(F32))
    sums_ref[sums_at + 2 : sums_at + 3, :] = column_sum(grad_first * normed)
    sums_ref[sums_at + 3 : sums_at + 4, :] = column_sum(grad_first)
    return norm_back(grad_first, normed, inverse, vector(gain1, layer)) + mid_ref[...]


def back1_kernel(
    lens, gain1, gain2, qkv_w, out_w, up_w, down_w, joint, grad_merged, log, hidden, mid, slope, middle,
    own_j, sent_j, own_g, sent_g, mid_out, grad_merged_out, sums_a_out, sums_b_out,
    joint_ref, up_ref, log_ref, hidden_ref, mid_ref, slope_ref, middle_ref, grad_joint_ref, sums_a_ref, grad_ref,
    upstream_ref, grad_up_ref, mid0_ref, branch_ref, grad_merged_ref, sums_b_ref, weights, load_sems, out_sems,
):
    core = lax.axis_index("seq")
    loads = Copies(load_sems)
    stores = Copies(out_sems)
    held = (joint_ref, up_ref, log_ref, hidden_ref, mid_ref)
    coming = [
        loads.start(source, target) for source, target in ((joint, joint_ref), (grad_merged, up_ref), (log, log_ref))
    ]
    qkv = [loads.start(columns_of(qkv_w.at[1], at), weights.at[at]) for at in range(3)]
    coming += [loads.start(hidden, hidden_ref), loads.start(mid, mid_ref)]
    later = [
        loads.start(down_w.at[0, BLOCK * at : BLOCK * (at + 1), :], weights.at[3 + at]) for at in range(FFB)
    ]
    later += [loads.start(slope, slope_ref)]
    later += [loads.start(columns_of(up_w.at[0], at), weights.at[3 + FFB + at]) for at in range(FFB)]
    later += [loads.start(middle, middle_ref), loads.start(out_w.at[0], weights.at[3 + 2 * FFB])]
    leaving = []
    sums_a_ref[...] = jnp.zeros_like(sums_a_ref)
    upstream = attention_back_part(
        1, lens, core, coming, qkv, held, gain1, weights, grad_joint_ref, sums_a_ref, 0, own_j, sent_j, stores, leaving
    )
    upstream_ref[...] = upstream
    grad = upstream.astype(BF16)
    grad_ref[...] = grad
    leaving.append(stores.start(core_half(grad_ref, 1 - core), sent_j.at[:, JS : JS + D // 2]))
    leaving.append(stores.start(core_half(grad_ref, core), own_j.at[:, JS : JS + D // 2]))
    leaving.append(stores.start(sums_a_ref, sums_a_out))
    wait_all(later)
    mlp_back_part(
        core, grad_ref[...], upstream_ref[...], slope_ref, middle_ref, vector(gain2, 0),
        [weights[3 + at] for at in range(FFB)], [weights[3 + FFB + at] for at in range(FFB)], weights[3 + 2 * FFB],
        grad_up_ref, branch_ref, mid0_ref, grad_merged_ref, sums_b_ref, own_g, sent_g, mid_out, stores, leaving,
    )
    for source, target in ((grad_merged_ref, grad_merged_out), (sums_b_ref, sums_b_out)):
        leaving.append(stores.start(source, target))
    wait_all(leaving)


def back0_kernel(
    lens, gain1, sums_b0, sums_a1, sums_b1, qkv_w, joint, grad_merged, log, hidden, mid,
    own_j, sent_j, tokens_out, moved_out,
    joint_ref, up_ref, log_ref, hidden_ref, mid_ref, grad_joint_ref, sums_ref, low_sums_ref, out_ref, weights,
    load_sems, out_sems,
):
    core = lax.axis_index("seq")
    loads = Copies(load_sems)
    stores = Copies(out_sems)
    held = (joint_ref, up_ref, log_ref, hidden_ref, mid_ref)
    sources = (joint, grad_merged, log, hidden, mid)
    coming = [loads.start(source, target) for source, target in zip(sources[:3], held[:3])]
    qkv = [loads.start(columns_of(qkv_w.at[0], at), weights.at[at]) for at in range(3)]
    coming += [loads.start(source, target) for source, target in zip(sources[3:], held[3:])]
    leaving = []
    sums_ref[...] = jnp.zeros_like(sums_ref)
    grad_in = attention_back_part(
        0, lens, core, coming, qkv, held, gain1, weights, grad_joint_ref, sums_ref, 0, own_j, sent_j, stores, leaving
    )
    sums_ref[4:8, :] = sums_b0[0:4, :]
    sums_ref[8:12, :] = sums_a1[0:4, :]
    sums_ref[12:16, :] = sums_b1[0:4, :]
    sums_ref[16:20, :] = sums_b0[4:8, :]
    sums_ref[20:24, :] = sums_b1[4:8, :]
    low_sums_ref[...] = sums_ref[...].astype(BF16)
    for target in (own_j, sent_j):
        leaving.append(stores.start(low_sums_ref, target.at[ROWS : ROWS + SUMS, 0:D]))
    out_ref[...] = grad_in.astype(BF16)
    leaving.append(stores.start(out_ref, tokens_out))
    leaving.append(stores.start(moved_rows(out_ref, core), moved_out))
    wait_all(leaving)


def hop_position(parts, core_orders, part, place, core):
    bits = parts.bit_length() - 1
    distance = part ^ place
    position = [0, 0]
    for side in range(2):
        for hop, bit in enumerate(core_orders[side]):
            position[side] |= ((distance >> bit) & 1) << (bits - 1 - hop)
    return position[0] * (1 - core) + position[1] * core


def g_blocks(count):
    return [(begin, min(G_BLOCK, count - begin)) for begin in range(0, count, G_BLOCK)]


def weight_kernel(parts, core_orders, products, with_sums, *refs):
    sources, refs = refs[: 4 * len(products)], refs[4 * len(products) :]
    kept, sent, *refs = refs
    inputs, refs = refs[: 2 * len(products)], refs[2 * len(products) :]
    if with_sums:
        own_sums, other_sums, block_ref, *refs = refs
    stage, load_sems, out_sems = refs
    core = lax.axis_index("seq")
    place = lax.axis_index("dp")
    loads = Copies(load_sems)
    first, second = slice(0, ROWS), slice(ROWS, 2 * ROWS)
    rows = stage.shape[1]
    half = parts // 2
    coming = []
    for at, (x_from, x_count, g_from, g_count) in enumerate(products):
        own_x, other_x, own_g, other_g = sources[4 * at : 4 * at + 4]
        x_ref, g_ref = inputs[2 * at : 2 * at + 2]
        x_coming, g_coming = [], []

        def load_x(block):
            columns = slice(x_from + X_BLOCK * block, x_from + X_BLOCK * (block + 1))
            place_at = slice(X_BLOCK * block, X_BLOCK * (block + 1))
            x_coming.append(
                (
                    loads.start(own_x.at[:, columns], x_ref.at[first, place_at]),
                    loads.start(other_x.at[:, columns], x_ref.at[second, place_at]),
                )
            )

        load_x(0)
        for begin, width in g_blocks(g_count):
            columns = slice(g_from + begin, g_from + begin + width)
            place_at = slice(begin, begin + width)
            g_coming.append(
                (
                    loads.start(own_g.at[0:ROWS, columns], g_ref.at[first, place_at]),
                    loads.start(other_g.at[0:ROWS, columns], g_ref.at[second, place_at]),
                )
            )
        for block in range(1, x_count // X_BLOCK):
            load_x(block)
        coming.append((x_coming, g_coming))
    if with_sums:
        below = slice(ROWS, ROWS + SUMS)
        sums_coming = (
            loads.start(sources[2].at[below, 0:D], own_sums),
            loads.start(sources[3].at[below, 0:D], other_sums),
        )
    leaving = []

    def leave(part, begin, width):
        columns = slice(begin, begin + width)
        source = stage.at[part, :, columns]
        sem = out_sems.at[len(leaving)]
        position = hop_position(parts, core_orders, part, place, core)

        @pl.when(position >= half)
        def _():
            pltpu.make_async_copy(source, sent.at[position - half, :, columns], sem).start()

        @pl.when(position < half)
        def _():
            pltpu.make_async_copy(source, kept.at[position, :, columns], sem).start()

        leaving.append(pltpu.make_async_copy(source, kept.at[0, :, columns], sem))

    done = 0
    for at, (x_from, x_count, g_from, g_count) in enumerate(products):
        x_ref, g_ref = inputs[2 * at : 2 * at + 2]
        x_coming, g_coming = coming[at]
        share = x_count // parts
        pieces = share // rows
        count = X_BLOCK // share
        for block in range(x_count // X_BLOCK):
            wait_all(x_coming[block])
            for (first_g, width), arriving in zip(g_blocks(g_count), g_coming):
                if block == 0:
                    wait_all(arriving)
                total = dot_tn(
                    x_ref[:, X_BLOCK * block : X_BLOCK * (block + 1)], g_ref[:, first_g : first_g + width]
                ).astype(BF16)
                total = total.reshape(count, pieces, rows, width)
                for piece in range(pieces):
                    begin = done + g_count * piece + first_g
                    stage[count * block : count * (block + 1), :, begin : begin + width] = total[:, piece]
            for part in range(count * block, count * (block + 1)):
                leave(part, done, g_count * pieces)
        done += g_count * pieces
    if with_sums:
        wait_all(sums_coming)
        width = D // parts
        sums = own_sums[...].astype(F32) + other_sums[...].astype(F32)
        begin = sum(g_count for _, _, _, g_count in products)
        half_wide = FF // parts // 2
        block_ref[...] = jnp.zeros_like(block_ref)
        for part in range(parts):
            block_ref[0:16, 0:width] = sums[0:16, width * part : width * (part + 1)]
            for layer in range(2):
                for side in range(2):
                    column = half_wide * (2 * part + side)
                    row = 16 + 4 * layer + column // D
                    to = 16 + 2 * layer + side
                    block_ref[to : to + 1, 0:half_wide] = sums[
                        row : row + 1, column % D : column % D + half_wide
                    ]
            stage[part, 0:SUMS, begin : begin + 128] = block_ref[...].astype(BF16)
            leave(part, begin, 128)
    wait_all(leaving)


def plain_weight_kernel(own_x, other_x, own_g, other_g, out):
    total = dot_tn(own_x[...], own_g[...]) + dot_tn(other_x[...], other_g[...])
    out[...] = total.astype(BF16)


def add_kernel(*refs):
    total = 0.0
    for ref in refs[:-1]:
        total = total + ref[...].astype(F32)
    refs[-1][...] = total.astype(refs[-1].dtype)


def finish_kernel(layers, splits, parts, terms, outs):
    for layer, columns in enumerate(layers):
        total = 0.0
        for ref, first in terms[layer]:
            total = total + ref[0, :, first : first + columns].astype(F32)
        rows = total.shape[0]
        for out, (begin, count) in zip(outs, splits):
            for piece in range(out.shape[1] // rows):
                at = begin + count * piece
                out[layer, rows * piece : rows * (piece + 1), :] = total[:, at : at + count]
        if parts is not None and layer == 0:
            sums = total[0:SUMS, columns - 128 : columns]
            width = D // parts
            for to in range(2):
                for out, row in zip(outs[len(splits) :], (0, 1, 4, 2, 3, 5, 6, 7)):
                    row += 8 * to
                    out[to : to + 1, :] = sums[row : row + 1, 0:width]
                half_wide = FF // parts // 2
                for side in range(2):
                    row = 16 + 2 * to + side
                    outs[-1][to : to + 1, half_wide * side : half_wide * (side + 1)] = sums[
                        row : row + 1, 0:half_wide
                    ]


def assemble_kernel(tokens, came_tokens, tokens_out):
    tokens_out[...] = gather_back(tokens[...], came_tokens[...], lax.axis_index("seq"))


ANY = pl.BlockSpec(memory_space=pl.ANY)
FAR = pl.BlockSpec(memory_space=pltpu.HBM)
def shaped(*dims, dtype=BF16):
    return jax.ShapeDtypeStruct(dims, dtype)


def held(*dims, dtype=BF16):
    return pltpu.VMEM(dims, dtype)


def sems(count):
    return pltpu.SemaphoreType.DMA((count,))


def whole(shape):
    return pl.BlockSpec(shape, lambda: (0,) * len(shape))


EXPECTED_US = {
    "ahead": 33.0, "down1": 6.4, "up1": 6.6, "qkv1": 0.05, "down0": 6.4, "up0": 6.6, "qkv0": 0.05, "back1": 20.0,
    "back0": 13.6, "assemble": 3.3,
}


def expected(name):
    time = 4.0 * EXPECTED_US.get(name, 2.0)
    return pl.CostEstimate(flops=int(time * 1.15e9), bytes_accessed=int(time * 3.69e6), transcendentals=0)


def call(kernel, name, operands, outs, scratch, lens=None, after=(), carry=(), out_specs=None):
    first = [] if lens is None else [lens]
    first_specs = [] if lens is None else [pl.BlockSpec(memory_space=pltpu.SMEM)]
    skip = len(first) + len(after) + len(carry)
    inputs = skip + len(operands)

    def body(*refs):
        kernel(
            *refs[: len(first)], *refs[skip:inputs], *refs[inputs : inputs + len(outs)],
            *refs[inputs + len(outs) + len(carry) :],
        )

    return pl.pallas_call(
        body,
        in_specs=first_specs
        + [ANY] * (len(after) + len(carry))
        + [whole(array.shape) if near else ANY for array, near in operands],
        out_specs=(out_specs or [ANY] * len(outs)) + [ANY] * len(carry),
        out_shape=list(outs) + [shaped(*array.shape, dtype=array.dtype) for array in carry],
        input_output_aliases={len(first) + len(after) + at: len(outs) + at for at in range(len(carry))},
        scratch_shapes=list(scratch),
        compiler_params=pltpu.CompilerParams(vmem_limit_bytes=VMEM_LIMIT),
        cost_estimate=expected(name),
        name=name,
    )(*first, *after, *carry, *(array for array, _ in operands))


def near(*arrays):
    return [(array, True) for array in arrays]


def far(*arrays):
    return [(array, False) for array in arrays]


AHEAD = (
    ("hidden0", ROWS, D, BF16), ("xs0", ROWS, XS, BF16), ("joint0", ROWS, 3 * D, BF16), ("log0", ROWS, 128, F32),
    ("middle0", ROWS, D, F32), ("slope0", ROWS, FF, BF16), ("hidden1", ROWS, D, F32), ("xs1", ROWS, 3 * D, BF16),
    ("joint1", ROWS, 3 * D, BF16), ("log1", ROWS, 128, F32), ("active1", ROWS, FF, BF16), ("middle1", ROWS, D, F32),
    ("moved_middle1", MOVED, D, F32),
    ("grad_own1", ROWS, D // 2, BF16), ("grad_other1", ROWS, D // 2, BF16), ("own1", ROWS, GS, BF16),
    ("sent1", ROWS, GS, BF16), ("mid1", ROWS, D, F32), ("grad_merged1", ROWS, D, BF16), ("sums_b1", 8, D, F32),
)


def ahead(lens, tokens, came, cot, came_cot, vectors, matrices):
    direct = ("moved_middle1", "grad_own1", "grad_other1", "own1", "sent1")
    outs = call(
        ahead_kernel, "ahead", near(tokens, came, cot, came_cot, *vectors) + far(*matrices),
        [shaped(r, c, dtype=t) for _, r, c, t in AHEAD],
        [held(8, 128) if name in direct else held(r, c, dtype=t) for name, r, c, t in AHEAD]
        + [held(ROWS, FF), held(ROWS, D), held(ROWS, D), held(ROWS, FF), held(ROWS, D),
           held(16, D, BLOCK), sems(24), sems(24)],
        lens=lens,
    )
    return {name: out for (name, *_), out in zip(AHEAD, outs)}


def last_forward(active, came_active, middle, came_middle, down_w, down_b, after=()):
    return call(
        result_kernel, "result", near(down_b) + far(active, came_active, middle, came_middle, down_w),
        [shaped(HALF, D)],
        [held(ROWS, FF), held(MOVED, FF), held(ROWS, D, dtype=F32), held(MOVED, D, dtype=F32), held(FF, D),
         sems(3 * FFB + 2)],
        after=after, out_specs=[whole((HALF, D))],
    )[0]


def back1(lens, operands, gain1, gain2, matrices, after=()):
    sums = shaped(8, D, dtype=F32)
    return call(
        back1_kernel, "back1", near(gain1, gain2) + far(*matrices, *operands),
        [shaped(ROWS, JS + D // 2), shaped(ROWS, JS + D // 2), shaped(ROWS, GS), shaped(ROWS, GS),
         shaped(ROWS, D, dtype=F32), shaped(ROWS, D), sums, sums],
        [held(ROWS, 3 * D), held(ROWS, D), held(ROWS, 128, dtype=F32), held(ROWS, D, dtype=F32),
         held(ROWS, D, dtype=F32), held(ROWS, FF), held(ROWS, D, dtype=F32), held(ROWS, 3 * D),
         held(8, D, dtype=F32), held(ROWS, D), held(ROWS, D, dtype=F32), held(ROWS, FF), held(ROWS, D, dtype=F32),
         held(ROWS, D), held(ROWS, D), held(8, D, dtype=F32),
         held(4 + 2 * FFB, D, BLOCK), sems(11 + 2 * FFB), sems(12)],
        lens=lens, after=after,
    )


def back0(lens, operands, gain1, sums, qkv_w, after=()):
    return call(
        back0_kernel, "back0", near(gain1, *sums) + far(qkv_w, *operands),
        [shaped(ROWS + SUMS, JS), shaped(ROWS + SUMS, JS), shaped(ROWS, D), shaped(MOVED, D)],
        [held(ROWS, 3 * D), held(ROWS, D), held(ROWS, 128, dtype=F32), held(ROWS, D), held(ROWS, D, dtype=F32),
         held(ROWS, 3 * D), held(SUMS, D, dtype=F32), held(SUMS, D), held(ROWS, D), held(3, D, BLOCK), sems(8),
         sems(6)],
        lens=lens, after=after,
    )


def add(sums, begin, count, name, after=(), carry=()):
    arrays = []
    for _, terms in sums:
        for array, _ in terms:
            if not any(array is seen for seen in arrays):
                arrays.append(array)
    index = {id(array): at for at, array in enumerate(arrays)}
    share = arrays[0].shape[1]
    total = sum(columns for columns, _ in sums)
    skip = len(after) + len(carry)
    pieces = min(count, 2)
    size = count // pieces

    places = [
        (at, index[id(array)], first, columns)
        for at, (columns, terms) in enumerate(sums)
        for array, first in terms
    ]

    def body(*refs):
        sources, refs = refs[skip : skip + len(arrays)], refs[skip + len(arrays) :]
        out, *refs = refs[:1] + refs[1 + len(carry) :]
        *buffers, total_ref, load_sems, out_sems = refs
        loads, stores = Copies(load_sems), Copies(out_sems)
        coming, leaving = [], []
        for piece in range(pieces):
            parts_of = slice(size * piece, size * (piece + 1))
            coming.append(
                [
                    loads.start(
                        sources[source].at[begin + size * piece : begin + size * (piece + 1), :, first : first + columns],
                        buffer.at[parts_of],
                    )
                    for (_, source, first, columns), buffer in zip(places, buffers)
                ]
            )
        for piece in range(pieces):
            parts_of = slice(size * piece, size * (piece + 1))
            wait_all(coming[piece])
            done = 0
            for at, (columns, _) in enumerate(sums):
                value = 0.0
                for (which, *_), buffer in zip(places, buffers):
                    if which == at:
                        value = value + buffer[parts_of].astype(F32)
                total_ref[parts_of, :, done : done + columns] = value.astype(BF16)
                done += columns
            leaving.append(stores.start(total_ref.at[parts_of], out.at[parts_of]))
        wait_all(leaving)

    return pl.pallas_call(
        body,
        in_specs=[ANY] * skip + [FAR] * len(arrays),
        out_specs=[FAR] + [ANY] * len(carry),
        out_shape=[shaped(count, share, total)]
        + [shaped(*array.shape, dtype=array.dtype) for array in carry],
        input_output_aliases={len(after) + at: 1 + at for at in range(len(carry))},
        scratch_shapes=[held(count, share, columns) for *_, columns in places]
        + [held(count, share, total), sems(pieces * len(places)), sems(pieces)],
        compiler_params=pltpu.CompilerParams(vmem_limit_bytes=VMEM_LIMIT),
        cost_estimate=expected(name),
        name=name,
    )(*after, *carry, *arrays)


def swap(array):
    return lax.ppermute(array, "seq", [(0, 1), (1, 0)])


EVEN = ((0, 2, 1, 3), (1, 2, 0, 3))
LATE = ((0, 1, 2, 3), (1, 0, 2, 3))


class Halving:
    def __init__(self, name, kept, orders):
        self.name, self.orders = name, orders
        self.hop = 0
        self.columns = kept.shape[2]
        self.terms = [(kept, 0)]


def send(halvings, sent):
    hop, orders = halvings[0].hop, halvings[0].orders
    pairs = []
    for place in range(lax.axis_size("dp")):
        for core in range(2):
            other = place ^ (1 << orders[core][hop])
            pairs.append((2 * place + core, 2 * other + core))
    came = lax.ppermute(sent, ("dp", "seq"), pairs)
    first = 0
    for halving in halvings:
        halving.terms.append((came, first))
        halving.hop += 1
        first += halving.columns
    return came


def weight_gradient(name, operands, products, orders, with_sums, after=(), carry=()):
    parts = lax.axis_size("dp")
    columns = sum(g_count * (x_count // D) for _, x_count, _, g_count in products) + (128 if with_sums else 0)
    share = D // parts
    scratch = []
    copies = 2
    for _, x_count, _, g_count in products:
        scratch += [held(2 * ROWS, x_count), held(2 * ROWS, g_count)]
        copies += 2 * len(g_blocks(g_count)) + 2 * (x_count // X_BLOCK)
    if with_sums:
        scratch += [held(SUMS, D), held(SUMS, D), held(SUMS, 128, dtype=F32)]
    return call(
        lambda *refs: weight_kernel(parts, orders, products, with_sums, *refs), name, far(*operands),
        [shaped(parts // 2, share, columns)] * 2,
        scratch
        + [held(parts, share, columns), sems(copies), sems(parts * (len(products) + int(with_sums)))],
        after=after, carry=carry,
    )


def finish(name, groups, after=()):
    arrays = []
    for halvings, _, _ in groups:
        for halving in halvings:
            for array, _ in halving.terms:
                if not any(array is seen for seen in arrays):
                    arrays.append(array)
    index = {id(array): at for at, array in enumerate(arrays)}
    outs, counts = [], []
    for _, splits, parts in groups:
        mine = [shaped(2, rows, count, dtype=F32) for _, count, rows in splits]
        if parts is not None:
            mine += [shaped(2, D // parts, dtype=F32)] * 8 + [shaped(2, FF // parts, dtype=F32)]
        outs += mine
        counts.append(len(mine))
    places = [
        (index[id(array)], first, halving.columns)
        for halvings, _, _ in groups
        for halving in halvings
        for array, first in halving.terms
    ]

    def body(*refs):
        sources, refs = refs[len(after) : len(after) + len(arrays)], refs[len(after) + len(arrays) :]
        results, refs = refs[: len(outs)], refs[len(outs) :]
        *buffers, load_sems = refs
        loads = Copies(load_sems)
        coming = [
            loads.start(sources[source].at[0:1, :, first : first + columns], buffer)
            for (source, first, columns), buffer in zip(places, buffers)
        ]
        used = 0
        for (halvings, splits, parts), count in zip(groups, counts):
            terms = []
            for halving in halvings:
                wait_all(coming[used : used + len(halving.terms)])
                terms.append([(buffer, 0) for buffer in buffers[used : used + len(halving.terms)]])
                used += len(halving.terms)
            finish_kernel(
                [halving.columns for halving in halvings], [split[:2] for split in splits], parts, terms,
                results[:count],
            )
            results = results[count:]

    return pl.pallas_call(
        body,
        in_specs=[ANY] * len(after) + [FAR] * len(arrays),
        out_specs=[whole(out.shape) for out in outs],
        out_shape=outs,
        scratch_shapes=[held(1, arrays[0].shape[1], columns) for *_, columns in places] + [sems(len(places))],
        compiler_params=pltpu.CompilerParams(vmem_limit_bytes=VMEM_LIMIT),
        cost_estimate=expected(name),
        name=name,
    )(*after, *arrays)


def plain_weight_gradient(name, own_x, other_x, own_g, other_g):
    rows, columns = own_x.shape[1], own_g.shape[1]
    x_spec = pl.BlockSpec((ROWS, BLOCK), lambda step: (0, step))
    g_spec = pl.BlockSpec((ROWS, columns), lambda step: (0, 0))
    return pl.pallas_call(
        plain_weight_kernel,
        grid=(rows // BLOCK,),
        in_specs=[x_spec, x_spec, g_spec, g_spec],
        out_specs=pl.BlockSpec((BLOCK, columns), lambda step: (step, 0)),
        out_shape=shaped(rows, columns),
        compiler_params=pltpu.CompilerParams(vmem_limit_bytes=VMEM_LIMIT),
        name=name,
    )(own_x, other_x, own_g, other_g)


def plain_halving(total, bit_order):
    parts = lax.axis_size("dp")
    place = lax.axis_index("dp")
    bits = parts.bit_length() - 1
    total = total.reshape((2,) * bits + (total.shape[0] // parts, total.shape[1]))
    left = list(range(bits))[::-1]
    terms = [total]
    for bit in bit_order:
        axis = left.index(bit)
        left.remove(bit)
        mine = (place >> bit) & 1
        sent = sum(lax.dynamic_index_in_dim(t, 1 - mine, axis, keepdims=False).astype(F32) for t in terms)
        terms = [lax.dynamic_index_in_dim(t, mine, axis, keepdims=False) for t in terms]
        terms.append(
            lax.ppermute(sent.astype(BF16), "dp", [(i, i ^ (1 << bit)) for i in range(parts)])
        )
    return sum(t.astype(F32) for t in terms)


def sum_everywhere(array):
    total = array + swap(array)
    parts = lax.axis_size("dp")
    for bit in range(parts.bit_length() - 1):
        total = total + lax.ppermute(total, "dp", [(i, i ^ (1 << bit)) for i in range(parts)])
    return total


def shards(
    tokens, crop_len, qkv_weight, query_bias, value_bias, out_weight, out_bias, first_gain, first_shift,
    second_gain, second_shift, up_weight, up_bias, down_weight, down_bias, cotangent,
):
    parts = lax.axis_size("dp")
    lens = crop_len.reshape(-1)
    core = lax.axis_index("seq")
    tiled = parts == 16
    matrices = (out_weight, up_weight, down_weight)
    came_tokens = swap(tokens)
    came_cot = swap(cotangent)
    kept = ahead(
        lens, tokens, came_tokens, cotangent, came_cot,
        (first_gain, first_shift, query_bias, value_bias, out_bias, second_gain, second_shift, up_bias, down_bias),
        (qkv_weight,) + matrices,
    )
    reductions = {}

    def product(name, operands, products, after=(), carry=(), with_sums=False, orders=EVEN):
        if not tiled:
            totals = []
            for at, (x_from, x_count, g_from, g_count) in enumerate(products):
                own_x, other_x, own_g, other_g = operands[4 * at : 4 * at + 4]
                x_at, g_at = slice(x_from, x_from + x_count), slice(g_from, g_from + g_count)
                total = plain_weight_gradient(
                    name, own_x[:, x_at], other_x[:, x_at], own_g[:ROWS, g_at], other_g[:ROWS, g_at]
                )
                totals.append(plain_halving(total, range(parts.bit_length() - 1)))
            reductions[name] = totals
            return (total, *carry)
        here, gone, *carried = weight_gradient(name, operands, products, orders, with_sums, after, carry)
        reductions[name] = Halving(name, here, orders)
        send([reductions[name]], gone)
        return (gone, *carried)

    def step(names, after=(), carry=()):
        if not tiled:
            return (*(after or (tokens,))[:1], *carry)
        group = [reductions[name] for name in names.split()]
        hop = group[0].hop
        count = parts >> (hop + 1)
        sums = [(halving.columns, halving.terms) for halving in group]
        sent, *carried = add(sums, count, count, "_".join(names.split()) + f"_hop{hop}", after, carry)
        send(group, sent)
        return (sent, *carried)

    def arrived(name):
        return (reductions[name].terms[-1][0],) if tiled else ()

    active1, xs1, xs0 = kept["active1"], kept["xs1"], kept["xs0"]
    own1, sent1 = kept["own1"], kept["sent1"]
    came_active1 = swap(active1)
    came_gs1 = swap(sent1)
    came_xs1 = swap(xs1)
    came_middle1 = swap(kept["moved_middle1"])
    last, xs0 = product(
        "down1", (active1, came_active1, kept["grad_own1"], kept["grad_other1"]), ((0, FF, 0, D // 2),),
        carry=(xs0,),
    )
    came_xs0 = swap(xs0)
    (last,) = product(
        "up1", (xs1, came_xs1, own1, came_gs1, xs1, came_xs1, own1, came_gs1),
        ((LOW2, D, 0, FF // 2), (MERGED, D, FF // 2, D // 2)), after=(last, came_middle1),
    )
    own_j1, sent_j1, own_g0, sent_g0, mid0, grad_merged0, sums_a1, sums_b0 = back1(
        lens,
        (kept["joint1"], kept["grad_merged1"], kept["log1"], kept["hidden1"], kept["mid1"], kept["slope0"],
         kept["middle0"]),
        first_gain, second_gain, (qkv_weight,) + matrices, after=(last,),
    )
    last, sent_j1, sent_g0 = step("down1", after=(own_j1,), carry=(sent_j1, sent_g0))
    came_j1 = swap(sent_j1)
    came_g0 = swap(sent_g0)
    (last,) = product(
        "qkv1", (xs1, came_xs1, own_j1, came_j1), ((LOW1, D, 0, JS),), after=(last,)
    )
    (last,) = step("up1", after=(last,))
    (last,) = product("down0", (xs0, came_xs0, own_j1, came_j1), ((0, FF, JS, D // 2),), after=(last,))
    (last,) = product(
        "up0", (xs0, came_xs0, own_g0, came_g0, xs0, came_xs0, own_g0, came_g0),
        ((FF + LOW2, D, 0, FF // 2), (FF + MERGED, D, FF // 2, D // 2)), after=(last,), orders=EVEN,
    )
    (last,) = step("qkv1", after=(last,))
    own_j0, sent_j0, grad_tokens, moved_tokens = back0(
        lens, (kept["joint0"], grad_merged0, kept["log0"], kept["hidden0"], mid0), first_gain,
        (sums_b0, sums_a1, kept["sums_b1"]), qkv_weight, after=(last,),
    )
    last, sent_j0 = step("down0", after=(own_j0,) + arrived("qkv1"), carry=(sent_j0,))
    came_j0 = swap(sent_j0)
    (last,) = step("down1 up1", after=(last,))
    (last,) = product(
        "qkv0", (xs0, came_xs0, own_j0, came_j0), ((FF + LOW1, D, 0, JS),), after=(last,), with_sums=True, orders=LATE,
    )
    (last,) = step("up0", after=(last,))
    last, moved_tokens = step("down1 up1", after=(last,), carry=(moved_tokens,))
    came_tokens = swap(moved_tokens)
    (last,) = step("qkv1 down0", after=(last,))
    (last,) = step("qkv0", after=(last, came_tokens))
    (last,) = step("qkv1 down0", after=(last,))
    (last,) = step("qkv0", after=(last,))
    (last,) = step("up0", after=(last,))
    (grad_tokens,) = call(
        assemble_kernel, "assemble", near(grad_tokens, came_tokens), [shaped(HALF, D)], [],
        out_specs=[whole((HALF, D))], after=(last,),
    )
    (last,) = step("up0", after=(grad_tokens,))
    (last,) = step("qkv0", after=(last,))
    result = last_forward(
        active1, came_active1, kept["middle1"], came_middle1, down_weight, down_bias, after=(last,)
    )
    if tiled:
        share = D // parts

        def layers(name):
            return reductions[name + "0"], reductions[name + "1"]

        down_g, qkv_g, *vectors, up_g, out_g = finish(
            "finish",
            (
                (layers("down"), ((0, D // 2, FF // parts),), None),
                (layers("qkv"), ((0, JS, share),), parts),
                (layers("up"), ((0, FF // 2, share), (FF // 2, D // 2, share)), None),
            ),
            after=(result,),
        )
    else:
        down_g, up_g, out_g, qkv_g = (
            jnp.stack([reductions[name + "0"][at], reductions[name + "1"][at]])
            for name, at in (("down", 0), ("up", 0), ("up", 1), ("qkv", 0))
        )
        total = sum_everywhere(own_j0[ROWS:, :D].astype(F32))
        place = lax.axis_index("dp")
        width = D // parts
        narrow = lax.dynamic_slice(total[:16], (0, place * width), (16, width)).reshape(2, 8, width)
        vectors = [narrow[:, row] for row in (0, 1, 4, 2, 3, 5, 6, 7)]
        vectors.append(
            lax.dynamic_slice(total[16:24].reshape(2, FF), (0, place * (FF // parts)), (2, FF // parts))
        )
    query_b, value_b, out_b, gain1, shift1, gain2, shift2, down_b, up_b = vectors
    return (
        result, grad_tokens, qkv_g, query_b, value_b, out_g, out_b, gain1, shift1, gain2, shift2, up_g, up_b, down_g,
        down_b,
    )


def solution(mesh):
    rows = P(("dp", "seq"), None)
    matrix = P(None, "dp", "seq")
    narrow = P(None, "dp")
    return jax.shard_map(
        shards,
        mesh=mesh,
        in_specs=(rows, P("dp", None)) + (P(),) * 13 + (rows,),
        out_specs=(
            rows, rows, matrix, narrow, narrow, matrix, narrow, narrow, narrow, narrow, narrow, matrix, narrow,
            matrix, narrow,
        ),
        check_vma=False,
    )
```
